128 devices in a mesh: row: 16 (over x_lo, z, core), col: 8 (over y, x_hi).
Axes of the slice: x: 4 (x_hi: 2, x_lo: 2; x = x_hi * 2 + x_lo), y: 4, z: 4, core: 2. Of those that a mesh axis runs over, the one named last changes fastest.
Arguments:
- pair_rep: bfloat16 [512, 512, 128], P('row', 'col'), may hold values from -12 to 12
- cotangent: bfloat16 [512, 512, 128], P('row', 'col'), may hold values from -6 to 6
- ln_gain: float32 [128], replicated, may hold values from 0.1 to 1.9
- w_query: bfloat16 [128, 128], replicated, may hold values from -9 to 9
- w_key: bfloat16 [128, 128], replicated, may hold values from -9 to 9
- w_value: bfloat16 [128, 128], replicated, may hold values from -0.5 to 0.5
- w_gate: bfloat16 [128, 128], replicated, may hold values from -0.5 to 0.5
- gate_offset: float32 [128], replicated, may hold values from -4 to 4
- w_bias: bfloat16 [128, 4], replicated, may hold values from -0.5 to 0.5
- w_out: bfloat16 [128, 128], replicated, may hold values from -0.5 to 0.5
Outputs:
- update: bfloat16 [512, 512, 128], P('row', 'col')
- grad_pair: bfloat16 [512, 512, 128], P('row', 'col')
- grad_gain: float32 [128], replicated
- grad_query: float32 [128, 128], replicated
- grad_key: float32 [128, 128], replicated
- grad_value: float32 [128, 128], replicated
- grad_gate: float32 [128, 128], replicated
- grad_offset: float32 [128], replicated
- grad_bias: float32 [128, 4], replicated
- grad_out: float32 [128, 128], replicated
The draws below stay inside these ranges and needn't reach their ends.
All inputs are finite; a program needn't handle non-finite values.
Results may differ from the reference program's by a relative error of at most 0.035.
The reference program's roundings to bfloat16 on the way count: a program that leaves them out, or rounds other values in their place, can miss the bound.
Values may be sent and summed in bfloat16 or wider, within the bound.
No kernel may reach another device: no remote copies, remote signals or barrier semaphores. Data moves between devices by JAX's collectives and lax.ppermute only.
A program may use at most 64 MiB of HBM per device.

```python
import math
import jax
import jax.numpy as jnp
from jax import lax

C = 128
H = 4
CH = 32
HC = 128
N = 512


def draw_pair_rep(key, part):
    key = jax.random.fold_in(key, 11)
    first, second = jax.random.split(key, 2)
    channel_scale = jnp.exp(jax.random.uniform(first, (C,), jnp.float32, math.log(0.3), math.log(3.0)))
    drawn = jnp.clip(jax.random.normal(second, (N, N, C), jnp.float32), -4.0, 4.0) * channel_scale
    return jnp.clip(drawn, -12.0, 12.0).astype(jnp.bfloat16)


def scaled_weight(key):
    base = jnp.clip(jax.random.normal(key, (C, HC), jnp.float32), -4.0, 4.0) * C ** (-0.5)
    return base


def draw_w_query(key, part):
    key = jax.random.fold_in(key, 21)
    return scaled_weight(key).astype(jnp.bfloat16)


def draw_w_key(key, part):
    key = jax.random.fold_in(key, 22)
    return scaled_weight(key).astype(jnp.bfloat16)


def strengthened(entries, key, source, target, parts, factor):
    def block_of(position):
        return (jnp.arange(entries.shape[position]) // (entries.shape[position] // parts)).reshape((-1,) + (1,) * (entries.ndim - 1 - position))

    first = jax.random.permutation(key, parts)[block_of(target)]
    second = (block_of(target) + parts // 2) % parts
    return jnp.where((block_of(source) == first) | (block_of(source) == second), factor * entries, entries)


def levels(rng, extent, pieces, least, largest):
    gain = 1.0
    for axis_at, parts in pieces:
        steps = jax.random.uniform(jax.random.fold_in(jax.random.fold_in(rng, 6), axis_at), (parts,), jnp.float32, least / len(pieces), largest / len(pieces))
        gain = gain * jnp.repeat(jnp.exp(steps), extent[axis_at] // parts).reshape((-1,) + (1,) * (len(extent) - 1 - axis_at))
    return gain


def scatter_about(rng, shape, deviation, limit, shards=(), dtype=jnp.bfloat16):
    entries = jax.random.normal(rng, shape, jnp.float32) * deviation
    if len(shards) > 0:
        entries = levels(rng, shape, shards, -0.22, 0.18) * entries
    return jnp.clip(entries, min=-limit, max=limit).astype(dtype)


def bell_draw_with(key, shape, scale, bound, cuts, heavy, held_as=jnp.bfloat16):
    entries = scale * jax.random.normal(key, shape, jnp.float32)
    if cuts:
        entries = entries * levels(key, shape, cuts, -0.22, 0.18)
    return jnp.clip(strengthened(entries, jax.random.fold_in(key, 3), *heavy), -bound, bound).astype(held_as)


def setup_inputs(seed: int = 0) -> dict:
    seeds = jax.random.split(jax.random.key(seed), 11)
    pair_rep = draw_pair_rep(jax.random.fold_in(seeds[10], 71), 0)
    cotangent = bell_draw_with(seeds[1], (N, N, C), 1.0, 6.0, ((0, 16), (1, 8)), (0, 1, 16, 2.0))
    ln_gain = jnp.clip(1.0 + 0.18 * jax.random.normal(seeds[2], (C,), jnp.float32), 0.1, 1.9)
    w_query = draw_w_query(jax.random.fold_in(seeds[10], 71), 0)
    w_key = draw_w_key(jax.random.fold_in(seeds[10], 71), 0)
    w_value = scatter_about(seeds[5], (C, HC), C ** -0.5, 0.5)
    w_gate = scatter_about(seeds[6], (C, HC), C ** -0.5, 0.5)
    gate_offset = scatter_about(seeds[7], (HC,), 1.0, 4.0, (), jnp.float32)
    w_bias = scatter_about(seeds[8], (C, H), C ** -0.5, 0.5)
    w_out = scatter_about(seeds[9], (HC, C), HC ** -0.5, 0.5)
    return {"pair_rep": pair_rep, "cotangent": cotangent, "ln_gain": ln_gain, "w_query": w_query, "w_key": w_key, "w_value": w_value, "w_gate": w_gate, "gate_offset": gate_offset, "w_bias": w_bias, "w_out": w_out}


EPS = 1e-05

def normalize(pair_rep, ln_gain):
    values = pair_rep.astype(jnp.float32)
    average = lax.optimization_barrier(jnp.mean(values, axis=-1, keepdims=True))
    centered = values - average
    variance = lax.optimization_barrier(jnp.mean(centered * centered, axis=-1, keepdims=True))
    inverse = lax.rsqrt(variance + EPS)
    unit_pair = centered * inverse
    normed = (unit_pair * ln_gain).astype(jnp.bfloat16)
    return (unit_pair, inverse, normed)

def row_probs(query_row, key_row, bias_full):
    scores = jnp.einsum('jhc,khc->hjk', query_row.astype(jnp.float32), key_row.astype(jnp.float32))
    return jax.nn.softmax(scores + bias_full.astype(jnp.float32), axis=-1)

def reference(pair_rep, cotangent, ln_gain, w_query, w_key, w_value, w_gate, gate_offset, w_bias, w_out):
    query_scale = CH ** (-0.5)
    unit_pair, inverse, normed = normalize(pair_rep, ln_gain)
    flat_normed = normed.reshape(N * N, C)

    def project(weight):
        return jnp.dot(flat_normed, weight, preferred_element_type=jnp.float32)
    bias_full = project(w_bias).astype(jnp.bfloat16).reshape(N, N, H).transpose(2, 0, 1)
    query = (project(w_query) * query_scale).astype(jnp.bfloat16).reshape(N, N, H, CH)
    keys = (project(w_key) * query_scale).astype(jnp.bfloat16).reshape(N, N, H, CH)
    values = project(w_value).astype(jnp.bfloat16).reshape(N, N, H, CH)
    gate_value = jax.nn.sigmoid(project(w_gate) + gate_offset)

    def forward_row(row_item):
        query_row, key_row, value_row = row_item
        probs_low = row_probs(query_row, key_row, bias_full).astype(jnp.bfloat16)
        return jnp.einsum('hjk,khc->jhc', probs_low.astype(jnp.float32), value_row.astype(jnp.float32))
    attended = lax.map(forward_row, (query, keys, values)).reshape(N * N, HC)
    gated = (gate_value * attended).astype(jnp.bfloat16)
    update = jnp.dot(gated, w_out, preferred_element_type=jnp.float32).astype(jnp.bfloat16).reshape(N, N, C)
    flat_cot = cotangent.reshape(N * N, C)
    grad_gated = jnp.dot(flat_cot, w_out.T, preferred_element_type=jnp.float32)
    grad_out = jnp.dot(gated.T, flat_cot, preferred_element_type=jnp.float32)
    grad_att = (grad_gated * gate_value).astype(jnp.bfloat16).reshape(N, N, H, CH)
    grad_gpre = (grad_gated * attended * gate_value * (1.0 - gate_value)).astype(jnp.bfloat16)

    def backward_row(bias_grad, row_item):
        query_row, key_row, value_row, att_row = row_item
        soft_probs = row_probs(query_row, key_row, bias_full)
        probs_low = soft_probs.astype(jnp.bfloat16).astype(jnp.float32)
        att_float = att_row.astype(jnp.float32)
        value_grad = jnp.einsum('hjk,jhc->khc', probs_low, att_float)
        grad_probs = jnp.einsum('jhc,khc->hjk', att_float, value_row.astype(jnp.float32))
        score_grad = soft_probs * (grad_probs - lax.optimization_barrier(jnp.sum(soft_probs * grad_probs, axis=-1, keepdims=True)))
        score_low = score_grad.astype(jnp.bfloat16).astype(jnp.float32)
        query_grad = jnp.einsum('hjk,khc->jhc', score_low, key_row.astype(jnp.float32))
        key_grad = jnp.einsum('hjk,jhc->khc', score_low, query_row.astype(jnp.float32))
        return (bias_grad + score_grad, (query_grad, key_grad, value_grad))
    bias_grad, (query_grad, key_grad, value_grad) = lax.scan(backward_row, jnp.zeros((H, N, N), jnp.float32), (query, keys, values, grad_att))
    bias_pos = bias_grad.transpose(1, 2, 0).reshape(N * N, H)
    qpre = (query_grad.reshape(N * N, HC) * query_scale).astype(jnp.bfloat16)
    kpre = (key_grad.reshape(N * N, HC) * query_scale).astype(jnp.bfloat16)
    vpre = value_grad.reshape(N * N, HC).astype(jnp.bfloat16)
    grad_normed = jnp.dot(qpre, w_query.T, preferred_element_type=jnp.float32)
    grad_normed = grad_normed + jnp.dot(kpre, w_key.T, preferred_element_type=jnp.float32)
    grad_normed = grad_normed + jnp.dot(vpre, w_value.T, preferred_element_type=jnp.float32)
    grad_normed = grad_normed + jnp.dot(grad_gpre, w_gate.T, preferred_element_type=jnp.float32)
    grad_normed = grad_normed + jnp.dot(bias_pos, w_bias.astype(jnp.float32).T, precision=lax.Precision.HIGHEST)
    grad_query = jnp.dot(flat_normed.T, qpre, preferred_element_type=jnp.float32)
    grad_key = jnp.dot(flat_normed.T, kpre, preferred_element_type=jnp.float32)
    grad_value = jnp.dot(flat_normed.T, vpre, preferred_element_type=jnp.float32)
    grad_gate = jnp.dot(flat_normed.T, grad_gpre, preferred_element_type=jnp.float32)
    grad_offset = lax.optimization_barrier(jnp.sum(grad_gpre.astype(jnp.float32), axis=0))
    grad_bias = jnp.dot(flat_normed.astype(jnp.float32).T, bias_pos, precision=lax.Precision.HIGHEST)
    flat_unit = unit_pair.reshape(N * N, C)
    grad_gain = lax.optimization_barrier(jnp.sum(grad_normed * flat_unit, axis=0))
    scaled = grad_normed * ln_gain
    first = lax.optimization_barrier(jnp.mean(scaled, axis=-1, keepdims=True))
    second = lax.optimization_barrier(jnp.mean(scaled * flat_unit, axis=-1, keepdims=True))
    grad_pair = ((scaled - first - flat_unit * second) * inverse.reshape(N * N, 1)).astype(jnp.bfloat16).reshape(N, N, C)
    return (update, grad_pair, grad_gain, grad_query, grad_key, grad_value, grad_gate, grad_offset, grad_bias, grad_out)
```

```python
import functools

import jax
import jax.numpy as jnp
from jax import lax
from jax.experimental import pallas as pl
from jax.experimental.pallas import tpu as pltpu
from jax.sharding import PartitionSpec as P

EPS = 1e-05
F32 = jnp.float32
BF16 = jnp.bfloat16
NT = (((1,), (1,)), ((), ()))
TN = (((0,), (0,)), ((), ()))
PARAMS = pltpu.CompilerParams(vmem_limit_bytes=56 * 1024 * 1024)


def dot(left, right, dims=(((1,), (0,)), ((), ()))):
    return lax.dot_general(left, right, dims, preferred_element_type=F32)


def normalize(values, gain):
    average = jnp.mean(values, axis=-1, keepdims=True)
    centered = values - average
    variance = jnp.mean(centered * centered, axis=-1, keepdims=True)
    inverse = lax.rsqrt(variance + EPS)
    unit = centered * inverse
    return unit, inverse, (unit * gain).astype(BF16)


def low_lanes(shape):
    return lax.broadcasted_iota(jnp.int32, shape, len(shape) - 1) < 64


def join_low(left, right):
    return jnp.where(low_lanes(left.shape), left, pltpu.roll(right, 64, left.ndim - 1))


def join_high(left, right):
    return jnp.where(low_lanes(left.shape), pltpu.roll(left, 64, left.ndim - 1), right)


def head_mask(heads, channels, dtype):
    lane = lax.broadcasted_iota(jnp.int32, (1, heads, 1, channels), 3)
    head = lax.broadcasted_iota(jnp.int32, (1, heads, 1, channels), 1)
    return jnp.where(lane // (channels // heads) == head, 1.0, 0.0).astype(dtype)


def tile_bias_kernel(pair_ref, gain_ref, wb_ref, msg_ref, rows_ref):
    unit, inverse, normed = normalize(pair_ref[...].astype(F32), gain_ref[...])
    bias = dot(wb_ref[...], normed, NT)
    for half in range(8):
        first = bias[0:8, half * 128 : half * 128 + 128]
        second = bias[0:8, (8 + half) * 128 : (8 + half) * 128 + 128]
        even = join_low(first, second)
        odd = join_high(first, second)
        for head in range(4):
            base = head * 16 + 2 * half
            rows_ref[base : base + 1, :] = even[head : head + 1]
            rows_ref[base + 1 : base + 2, :] = odd[head : head + 1]
    msg_ref[...] = jnp.broadcast_to(rows_ref[...].astype(BF16)[None], msg_ref.shape)


def project_kernel(scale, pair_ref, cot_ref, gain_ref, wcat_ref, off_ref, wout_ref,
                   q_ref, k_ref, v_ref, a_ref, gate_ref, gg_ref, n_ref):
    values = pair_ref[...].reshape(512, 128).astype(F32)
    unit, inverse, normed = normalize(values, gain_ref[...])
    projected = dot(normed, wcat_ref[...])
    gate = jax.nn.sigmoid(projected[:, 384:512] + off_ref[...])
    grad_gated = dot(cot_ref[...].reshape(512, 128), wout_ref[...], NT)
    q_ref[0] = (projected[:, 0:128] * scale).astype(BF16)
    k_ref[0] = (projected[:, 128:256] * scale).astype(BF16)
    v_ref[0] = projected[:, 256:384].astype(BF16)
    a_ref[0] = (grad_gated * gate).astype(BF16)
    gate_ref[0] = gate
    gg_ref[0] = grad_gated
    n_ref[0] = normed


def attend_kernel(q_ref, k_ref, v_ref, a_ref, bias_ref,
                  att_ref, dq_ref, dk_ref, dv_ref, out_ref, bias_scr, sum_scr):
    chunk = pl.program_id(0)
    for r in range(4):
        for m in range(4):
            left = bias_ref[r, 2 * m].astype(F32)
            right = bias_ref[r, 2 * m + 1].astype(F32)
            lanes = slice(m * 128, m * 128 + 128)
            bias_scr[r * 128 : r * 128 + 64, lanes] = join_low(left, right)
            bias_scr[r * 128 + 64 : r * 128 + 128, lanes] = join_high(left, right)
    mask = head_mask(4, 128, BF16)
    mask_f = head_mask(4, 128, F32)

    def spread(rows):
        return (rows.reshape(8, 1, 16, 128) * mask).reshape(512, 128)

    def collect(rows):
        return jnp.sum(rows.reshape(8, 4, 16, 128) * mask_f, axis=1).reshape(128, 128)

    def step(row, carry):
        at = pl.ds(pl.multiple_of(chunk * 128, 128), 128)
        q_big = spread(q_ref[row, at, :])
        a_big = spread(a_ref[row, at, :])
        keys = k_ref[row]
        values = v_ref[row]
        scores = dot(q_big, keys, NT) + bias_scr[...]
        top = jnp.max(scores, axis=-1, keepdims=True)
        powers = jnp.exp(scores - top)
        probs = powers * (1.0 / jnp.sum(powers, axis=-1, keepdims=True))
        probs_low = probs.astype(BF16)
        att_ref[row, at, :] = collect(dot(probs_low, values))
        grad_probs = dot(a_big, values, NT)
        inner = jnp.sum(probs * grad_probs, axis=-1, keepdims=True)
        score_grad = probs * (grad_probs - inner)
        score_low = score_grad.astype(BF16)
        dq_ref[row, at, :] = collect(dot(score_low, keys))
        dk = dot(q_big, score_low, TN)
        dv = dot(a_big, probs_low, TN)

        @pl.when(chunk == 0)
        def _():
            dk_ref[row] = dk
            dv_ref[row] = dv

        @pl.when(chunk > 0)
        def _():
            dk_ref[row] += dk
            dv_ref[row] += dv

        @pl.when(row == 0)
        def _():
            sum_scr[...] = score_grad

        @pl.when(row > 0)
        def _():
            sum_scr[...] += score_grad

        return carry

    lax.fori_loop(0, 4, step, 0)
    for r in range(4):
        for m in range(4):
            lanes = slice(m * 128, m * 128 + 128)
            low = sum_scr[r * 128 : r * 128 + 64, lanes]
            high = sum_scr[r * 128 + 64 : r * 128 + 128, lanes]
            out_ref[r, 2 * m] = join_low(low, high).astype(BF16)
            out_ref[r, 2 * m + 1] = join_high(low, high).astype(BF16)


def post_kernel(scale, att_ref, dq_ref, dk_ref, dv_ref, gate_ref, gg_ref, n_ref, cot_ref, wcat_ref,
                wout_ref, up_ref, gn_ref, par_ref, off_ref, w_scr, o_scr, s_scr):
    row = pl.program_id(0)
    attended = att_ref[0]
    gate = gate_ref[0]
    grad_gated = gg_ref[0]
    gated = (gate * attended).astype(BF16)
    cot = cot_ref[...].reshape(512, 128)
    up_ref[...] = dot(gated, wout_ref[...]).astype(BF16).reshape(8, 1, 64, 128)
    out_part = dot(gated, cot, TN)
    gpre = (grad_gated * attended * gate * (1.0 - gate)).astype(BF16)
    qpre = (dq_ref[0] * scale).astype(BF16)
    kpre = (jnp.transpose(dk_ref[0]) * scale).astype(BF16)
    vpre = jnp.transpose(dv_ref[0]).astype(BF16)
    cat = jnp.concatenate([qpre, kpre, vpre, gpre], axis=1)
    gn_ref[...] = dot(cat, wcat_ref[...], NT).astype(BF16).reshape(8, 1, 64, 128)
    w_part = dot(n_ref[0], cat, TN)
    off = jnp.sum(gpre.astype(F32), axis=0, keepdims=True)

    @pl.when(row == 0)
    def _():
        w_scr[...] = w_part
        o_scr[...] = out_part
        s_scr[...] = off

    @pl.when(row > 0)
    def _():
        w_scr[...] += w_part
        o_scr[...] += out_part
        s_scr[...] += off

    @pl.when(row == 3)
    def _():
        for t in range(4):
            par_ref[:, t, :] = w_scr[:, t * 128 : t * 128 + 128]
        par_ref[:, 4, :] = o_scr[...]
        for t in range(5, 8):
            par_ref[:, t, :] = jnp.zeros((128, 128), F32)
        off_ref[...] = jnp.broadcast_to(s_scr[...], off_ref.shape)


def tile_final_kernel(pair_ref, gn_ref, bg_ref, par_ref, off_ref, gain_ref, wb_ref,
                      gp_ref, msg_ref, rows_ref, bg_scr):
    rows_ref[...] = jnp.sum(bg_ref[...].astype(F32), axis=0)
    bg_scr[...] = jnp.zeros(bg_scr.shape, F32)
    for half in range(8):
        for head in range(4):
            base = head * 16 + 2 * half
            left = rows_ref[base : base + 1, :]
            right = rows_ref[base + 1 : base + 2, :]
            bg_scr[head : head + 1, half * 128 : half * 128 + 128] = join_low(left, right)
            bg_scr[head : head + 1, (8 + half) * 128 : (8 + half) * 128 + 128] = join_high(left, right)
    bg = bg_scr[...]
    high = bg.astype(BF16)
    low = (bg - high.astype(F32)).astype(BF16)
    both = jnp.concatenate([high.astype(F32), low.astype(F32)], axis=0).astype(BF16)
    unit, inverse, normed = normalize(pair_ref[...].astype(F32), gain_ref[...])
    total = gn_ref[...].astype(F32) + dot(both, wb_ref[...], TN)
    bias_part = dot(both, normed)
    gain_part = jnp.sum(total * unit, axis=0, keepdims=True)
    scaled = total * gain_ref[...]
    first = jnp.mean(scaled, axis=-1, keepdims=True)
    second = jnp.mean(scaled * unit, axis=-1, keepdims=True)
    gp_ref[...] = ((scaled - first - unit * second) * inverse).astype(BF16)
    params = jnp.sum(par_ref[...], axis=0)
    row = lax.broadcasted_iota(jnp.int32, (8, 128), 0)
    params = jnp.where(row == 5, off_ref[...], jnp.where(row == 6, gain_part, params))
    small = bias_part[0:8] + bias_part[8:16]
    msg_ref[...] = jnp.broadcast_to(jnp.concatenate([params, small], axis=0)[None], msg_ref.shape)


def finish_kernel(msg_ref, q_ref, k_ref, v_ref, g_ref, o_ref, small_ref):
    for t, ref in enumerate((q_ref, k_ref, v_ref, g_ref, o_ref)):
        ref[...] = msg_ref[:, t, :]
    small_ref[...] = jnp.sum(msg_ref[...], axis=0)


def sds(shape, dtype):
    return jax.ShapeDtypeStruct(shape, dtype)


def whole(shape):
    return pl.BlockSpec(shape, lambda *_: (0,) * len(shape))


def body(pair_rep, cotangent, ln_gain, w_query, w_key, w_value, w_gate, gate_offset, w_bias, w_out):
    scale = 32 ** (-0.5)
    gain = ln_gain.reshape(1, 128)
    offset = gate_offset.reshape(1, 128)
    wcat = jnp.concatenate([w_query, w_key, w_value, w_gate], axis=1)
    wb_pad = jnp.pad(w_bias.T, ((0, 4), (0, 0)))
    wb_two = jnp.concatenate([wb_pad, wb_pad], axis=0)
    everyone = ("row", "col")
    pair_tile = pair_rep.reshape(2048, 128)

    def swap(value, axes):
        return lax.all_to_all(value, axes, split_axis=0, concat_axis=0, tiled=True)

    bias_msg = pl.pallas_call(
        tile_bias_kernel,
        out_shape=sds((128, 64, 128), BF16),
        scratch_shapes=[pltpu.VMEM((64, 128), F32)],
        compiler_params=PARAMS,
        name="tile_bias",
    )(pair_tile, gain, wb_two)
    pair_rows = swap(pair_rep, "col").reshape(8, 4, 64, 128)
    cot_rows = swap(cotangent, "col").reshape(8, 4, 64, 128)
    bias_all = swap(bias_msg, everyone).reshape(16, 8, 64, 128)

    from_rows = pl.BlockSpec((8, 1, 64, 128), lambda i: (0, i, 0, 0))
    by_row = pl.BlockSpec((1, 512, 128), lambda i: (i, 0, 0))
    query, keys, values, grad_att, gate, grad_gated, normed = pl.pallas_call(
        functools.partial(project_kernel, scale),
        grid=(4,),
        in_specs=[from_rows, from_rows, whole((1, 128)), whole((128, 512)), whole((1, 128)), whole((128, 128))],
        out_specs=[by_row] * 7,
        out_shape=[sds((4, 512, 128), t) for t in (BF16, BF16, BF16, BF16, F32, F32, BF16)],
        compiler_params=PARAMS,
        name="project",
    )(pair_rows, cot_rows, gain, wcat, offset, w_out)

    full = whole((4, 512, 128))
    full_t = whole((4, 128, 512))
    blocks = pl.BlockSpec((4, 8, 64, 128), lambda c: (c, 0, 0, 0))
    attended, dq, dk, dv, bias_out = pl.pallas_call(
        attend_kernel,
        grid=(4,),
        in_specs=[full, full, full, full, blocks],
        out_specs=[full, full, full_t, full_t, blocks],
        out_shape=[sds((4, 512, 128), F32), sds((4, 512, 128), F32), sds((4, 128, 512), F32),
                   sds((4, 128, 512), F32), sds((16, 8, 64, 128), BF16)],
        scratch_shapes=[pltpu.VMEM((512, 512), F32), pltpu.VMEM((512, 512), F32)],
        compiler_params=PARAMS,
        name="attend",
    )(query, keys, values, grad_att, bias_all)
    bias_in = swap(bias_out.reshape(128, 64, 128), everyone)

    by_row_t = pl.BlockSpec((1, 128, 512), lambda i: (i, 0, 0))
    update, grad_n, params, off = pl.pallas_call(
        functools.partial(post_kernel, scale),
        grid=(4,),
        in_specs=[by_row, by_row, by_row_t, by_row_t, by_row, by_row, by_row, from_rows,
                  whole((128, 512)), whole((128, 128))],
        out_specs=[from_rows, from_rows, whole((128, 8, 128)), whole((8, 128))],
        out_shape=[sds((8, 4, 64, 128), BF16), sds((8, 4, 64, 128), BF16), sds((128, 8, 128), F32),
                   sds((8, 128), F32)],
        scratch_shapes=[pltpu.VMEM((128, 512), F32), pltpu.VMEM((128, 128), F32), pltpu.VMEM((1, 128), F32)],
        compiler_params=PARAMS,
        name="post",
    )(attended, dq, dk, dv, gate, grad_gated, normed, cot_rows, wcat, w_out)
    grad_tile = swap(grad_n.reshape(32, 64, 128), "col").reshape(2048, 128)
    params_in = swap(params, everyone)
    grad_pair, final_msg = pl.pallas_call(
        tile_final_kernel,
        out_shape=[sds((2048, 128), BF16), sds((128, 16, 128), F32)],
        scratch_shapes=[pltpu.VMEM((64, 128), F32), pltpu.VMEM((8, 2048), F32)],
        compiler_params=PARAMS,
        name="tile_final",
    )(pair_tile, grad_tile, bias_in, params_in, off, gain, wb_two)
    final_in = swap(final_msg, everyone)
    update_tile = swap(update.reshape(32, 64, 128), "col")
    g_query, g_key, g_value, g_gate, g_out, small = pl.pallas_call(
        finish_kernel,
        out_shape=[sds((128, 128), F32)] * 5 + [sds((16, 128), F32)],
        compiler_params=PARAMS,
        name="finish",
    )(final_in)
    return (
        update_tile,
        grad_pair.reshape(32, 64, 128),
        small[6],
        g_query,
        g_key,
        g_value,
        g_gate,
        small[5],
        small[8:12].T,
        g_out,
    )


def solution(mesh):
    tile = P("row", "col", None)
    return jax.shard_map(
        body,
        mesh=mesh,
        in_specs=(tile, tile) + (P(),) * 8,
        out_specs=(tile, tile) + (P(),) * 8,
        check_vma=False,
    )
```

```python
import functools

import jax
import jax.numpy as jnp
from jax import lax
from jax.experimental import pallas as pl
from jax.experimental.pallas import tpu as pltpu
from jax.sharding import PartitionSpec as P

EPS = 1e-05
F32 = jnp.float32
BF16 = jnp.bfloat16
NT = (((1,), (1,)), ((), ()))
TN = (((0,), (0,)), ((), ()))
PARAMS = pltpu.CompilerParams(vmem_limit_bytes=56 * 1024 * 1024)


def dot(left, right, dims=(((1,), (0,)), ((), ()))):
    return lax.dot_general(left, right, dims, preferred_element_type=F32)


def normalize(values, gain):
    average = jnp.mean(values, axis=-1, keepdims=True)
    centered = values - average
    variance = jnp.mean(centered * centered, axis=-1, keepdims=True)
    inverse = lax.rsqrt(variance + EPS)
    unit = centered * inverse
    return unit, inverse, (unit * gain).astype(BF16)


def low_lanes(shape):
    return lax.broadcasted_iota(jnp.int32, shape, len(shape) - 1) < 64


def join_low(left, right):
    return jnp.where(low_lanes(left.shape), left, pltpu.roll(right, 64, left.ndim - 1))


def join_high(left, right):
    return jnp.where(low_lanes(left.shape), pltpu.roll(left, 64, left.ndim - 1), right)


def head_mask(heads, channels, dtype):
    lane = lax.broadcasted_iota(jnp.int32, (1, heads, 1, channels), 3)
    head = lax.broadcasted_iota(jnp.int32, (1, heads, 1, channels), 1)
    return jnp.where(lane // (channels // heads) == head, 1.0, 0.0).astype(dtype)


def tile_bias_kernel(pair_ref, gain_ref, wb_ref, msg_ref, rows_ref):
    unit, inverse, normed = normalize(pair_ref[...].astype(F32), gain_ref[...])
    bias = dot(wb_ref[...], normed, NT)
    for half in range(8):
        first = bias[0:8, half * 128 : half * 128 + 128]
        second = bias[0:8, (8 + half) * 128 : (8 + half) * 128 + 128]
        even = join_low(first, second)
        odd = join_high(first, second)
        for head in range(4):
            base = head * 16 + 2 * half
            rows_ref[base : base + 1, :] = even[head : head + 1]
            rows_ref[base + 1 : base + 2, :] = odd[head : head + 1]
    msg_ref[...] = jnp.broadcast_to(rows_ref[...].astype(BF16)[None], msg_ref.shape)


def pack_kernel(pair_ref, cot_ref, out_ref):
    out_ref[:, 0] = pair_ref[...]
    out_ref[:, 1] = cot_ref[...]


def project_kernel(scale, rows_ref, gain_ref, wcat_ref, off_ref, wout_ref,
                   q_ref, k_ref, v_ref, a_ref, gate_ref, gg_ref, n_ref):
    values = rows_ref[:, 0, 0].reshape(512, 128).astype(F32)
    unit, inverse, normed = normalize(values, gain_ref[...])
    projected = dot(normed, wcat_ref[...])
    gate = jax.nn.sigmoid(projected[:, 384:512] + off_ref[...])
    grad_gated = dot(rows_ref[:, 1, 0].reshape(512, 128), wout_ref[...], NT)
    q_ref[0] = (projected[:, 0:128] * scale).astype(BF16)
    k_ref[0] = (projected[:, 128:256] * scale).astype(BF16)
    v_ref[0] = projected[:, 256:384].astype(BF16)
    a_ref[0] = (grad_gated * gate).astype(BF16)
    gate_ref[0] = gate
    gg_ref[0] = grad_gated
    n_ref[0] = normed


def attend_kernel(q_ref, k_ref, v_ref, a_ref, bias_ref,
                  att_ref, dq_ref, dk_ref, dv_ref, out_ref, bias_scr, sum_scr):
    chunk = pl.program_id(0)
    for r in range(4):
        for m in range(4):
            left = bias_ref[r, 2 * m].astype(F32)
            right = bias_ref[r, 2 * m + 1].astype(F32)
            lanes = slice(m * 128, m * 128 + 128)
            bias_scr[r * 128 : r * 128 + 64, lanes] = join_low(left, right)
            bias_scr[r * 128 + 64 : r * 128 + 128, lanes] = join_high(left, right)
    mask = head_mask(4, 128, BF16)
    mask_f = head_mask(4, 128, F32)

    def spread(rows):
        return (rows.reshape(8, 1, 16, 128) * mask).reshape(512, 128)

    def collect(rows):
        return jnp.sum(rows.reshape(8, 4, 16, 128) * mask_f, axis=1).reshape(128, 128)

    def step(row, carry):
        at = pl.ds(pl.multiple_of(chunk * 128, 128), 128)
        q_big = spread(q_ref[row, at, :])
        a_big = spread(a_ref[row, at, :])
        keys = k_ref[row]
        values = v_ref[row]
        scores = dot(q_big, keys, NT) + bias_scr[...]
        top = jnp.max(scores, axis=-1, keepdims=True)
        powers = jnp.exp(scores - top)
        probs = powers * (1.0 / jnp.sum(powers, axis=-1, keepdims=True))
        probs_low = probs.astype(BF16)
        att_ref[row, at, :] = collect(dot(probs_low, values))
        grad_probs = dot(a_big, values, NT)
        inner = jnp.sum(probs * grad_probs, axis=-1, keepdims=True)
        score_grad = probs * (grad_probs - inner)
        score_low = score_grad.astype(BF16)
        dq_ref[row, at, :] = collect(dot(score_low, keys))
        dk = dot(q_big, score_low, TN)
        dv = dot(a_big, probs_low, TN)

        @pl.when(chunk == 0)
        def _():
            dk_ref[row] = dk
            dv_ref[row] = dv

        @pl.when(chunk > 0)
        def _():
            dk_ref[row] += dk
            dv_ref[row] += dv

        @pl.when(row == 0)
        def _():
            sum_scr[...] = score_grad

        @pl.when(row > 0)
        def _():
            sum_scr[...] += score_grad

        return carry

    lax.fori_loop(0, 4, step, 0)
    for r in range(4):
        for m in range(4):
            lanes = slice(m * 128, m * 128 + 128)
            low = sum_scr[r * 128 : r * 128 + 64, lanes]
            high = sum_scr[r * 128 + 64 : r * 128 + 128, lanes]
            out_ref[r, 2 * m] = join_low(low, high).astype(BF16)
            out_ref[r, 2 * m + 1] = join_high(low, high).astype(BF16)


def post_kernel(scale, att_ref, dq_ref, dk_ref, dv_ref, gate_ref, gg_ref, n_ref, rows_ref, wcat_ref,
                wout_ref, held_ref, ug_ref, par_ref, off_ref, w_scr, o_scr, s_scr, p_scr):
    row = pl.program_id(0)
    attended = att_ref[0]
    gate = gate_ref[0]
    grad_gated = gg_ref[0]
    gated = (gate * attended).astype(BF16)
    cot = rows_ref[:, 0, 0].reshape(512, 128)
    ug_ref[:, 0, 0] = dot(gated, wout_ref[...]).astype(BF16).reshape(8, 64, 128)
    out_part = dot(gated, cot, TN)
    gpre = (grad_gated * attended * gate * (1.0 - gate)).astype(BF16)
    qpre = (dq_ref[0] * scale).astype(BF16)
    kpre = (jnp.transpose(dk_ref[0]) * scale).astype(BF16)
    vpre = jnp.transpose(dv_ref[0]).astype(BF16)
    cat = jnp.concatenate([qpre, kpre, vpre, gpre], axis=1)
    ug_ref[:, 1, 0] = dot(cat, wcat_ref[...], NT).astype(BF16).reshape(8, 64, 128)
    w_part = dot(n_ref[0], cat, TN)
    off = jnp.sum(gpre.astype(F32), axis=0, keepdims=True)

    @pl.when(row == 0)
    def _():
        w_scr[...] = w_part
        o_scr[...] = out_part
        s_scr[...] = off

    @pl.when(row > 0)
    def _():
        w_scr[...] += w_part
        o_scr[...] += out_part
        s_scr[...] += off

    @pl.when(row == 3)
    def _():
        for t in range(5):
            part = w_scr[:, t * 128 : t * 128 + 128] if t < 4 else o_scr[...]
            high = part.astype(BF16).astype(F32)
            p_scr[:, t, :] = high
            p_scr[:, 8 + t, :] = part - high
        for t in range(5, 8):
            p_scr[:, t, :] = jnp.zeros((128, 128), F32)
            p_scr[:, 8 + t, :] = jnp.zeros((128, 128), F32)
        par_ref[...] = p_scr[...].astype(BF16)
        off_ref[...] = jnp.broadcast_to(s_scr[...], off_ref.shape)


def tile_final_kernel(pair_ref, ug_ref, sums_ref, off_ref, gain_ref, wb_ref,
                      up_ref, gp_ref, msg_ref, rows_ref, bg_scr):
    up_ref[...] = ug_ref[:, 0].reshape(2048, 128)
    rows_ref[...] = jnp.sum(sums_ref[...].astype(F32), axis=0)
    bg_scr[...] = jnp.zeros(bg_scr.shape, F32)
    for half in range(8):
        for head in range(4):
            base = head * 16 + 2 * half
            left = rows_ref[base : base + 1, :]
            right = rows_ref[base + 1 : base + 2, :]
            bg_scr[head : head + 1, half * 128 : half * 128 + 128] = join_low(left, right)
            bg_scr[head : head + 1, (8 + half) * 128 : (8 + half) * 128 + 128] = join_high(left, right)
    bg = bg_scr[...]
    high = bg.astype(BF16)
    low = (bg - high.astype(F32)).astype(BF16)
    both = jnp.concatenate([high.astype(F32), low.astype(F32)], axis=0).astype(BF16)
    unit, inverse, normed = normalize(pair_ref[...].astype(F32), gain_ref[...])
    total = ug_ref[:, 1].reshape(2048, 128).astype(F32) + dot(both, wb_ref[...], TN)
    bias_part = dot(both, normed)
    gain_part = jnp.sum(total * unit, axis=0, keepdims=True)
    scaled = total * gain_ref[...]
    first = jnp.mean(scaled, axis=-1, keepdims=True)
    second = jnp.mean(scaled * unit, axis=-1, keepdims=True)
    gp_ref[...] = ((scaled - first - unit * second) * inverse).astype(BF16)
    params = rows_ref[64:72, :] + rows_ref[72:80, :]
    row = lax.broadcasted_iota(jnp.int32, (8, 128), 0)
    params = jnp.where(row == 5, off_ref[...], jnp.where(row == 6, gain_part, params))
    small = bias_part[0:8] + bias_part[8:16]
    msg_ref[...] = jnp.broadcast_to(jnp.concatenate([params, small], axis=0)[None], msg_ref.shape)


def finish_kernel(msg_ref, q_ref, k_ref, v_ref, g_ref, o_ref, off_ref, gain_ref, bias_ref):
    for t, ref in enumerate((q_ref, k_ref, v_ref, g_ref, o_ref)):
        ref[...] = msg_ref[:, t, :]
    small = jnp.sum(msg_ref[...], axis=0)
    off_ref[...] = small[5]
    gain_ref[...] = small[6]
    bias_ref[...] = small[8:12]


def sds(shape, dtype):
    return jax.ShapeDtypeStruct(shape, dtype)


def whole(shape):
    return pl.BlockSpec(shape, lambda *_: (0,) * len(shape))


def body(pair_rep, cotangent, ln_gain, w_query, w_key, w_value, w_gate, gate_offset, w_bias, w_out):
    scale = 32 ** (-0.5)
    gain = ln_gain.reshape(1, 128)
    offset = gate_offset.reshape(1, 128)
    wcat = jnp.concatenate([w_query, w_key, w_value, w_gate], axis=1)
    wb_pad = jnp.pad(w_bias.T, ((0, 4), (0, 0)))
    wb_two = jnp.concatenate([wb_pad, wb_pad], axis=0)
    everyone = ("row", "col")
    pair_tile = pair_rep.reshape(2048, 128)

    def swap(value, axes):
        return lax.all_to_all(value, axes, split_axis=0, concat_axis=0, tiled=True)

    bias_msg = pl.pallas_call(
        tile_bias_kernel,
        out_shape=sds((128, 64, 128), BF16),
        scratch_shapes=[pltpu.VMEM((64, 128), F32)],
        compiler_params=PARAMS,
        name="tile_bias",
    )(pair_tile, gain, wb_two)
    packed = pl.pallas_call(
        pack_kernel,
        out_shape=sds((8, 2, 4, 64, 128), BF16),
        compiler_params=PARAMS,
        name="pack",
    )(pair_rep.reshape(8, 4, 64, 128), cotangent.reshape(8, 4, 64, 128))
    both_rows = swap(packed, "col")
    bias_all = swap(bias_msg, everyone).reshape(16, 8, 64, 128)

    from_rows = pl.BlockSpec((8, 2, 1, 64, 128), lambda i: (0, 0, i, 0, 0))
    from_cot = pl.BlockSpec((8, 1, 1, 64, 128), lambda i: (0, 1, i, 0, 0))
    by_row = pl.BlockSpec((1, 512, 128), lambda i: (i, 0, 0))
    query, keys, values, grad_att, gate, grad_gated, normed = pl.pallas_call(
        functools.partial(project_kernel, scale),
        grid=(4,),
        in_specs=[from_rows, whole((1, 128)), whole((128, 512)), whole((1, 128)), whole((128, 128))],
        out_specs=[by_row] * 7,
        out_shape=[sds((4, 512, 128), t) for t in (BF16, BF16, BF16, BF16, F32, F32, BF16)],
        compiler_params=PARAMS,
        name="project",
    )(both_rows, gain, wcat, offset, w_out)

    full = whole((4, 512, 128))
    full_t = whole((4, 128, 512))
    blocks = pl.BlockSpec((4, 8, 64, 128), lambda c: (c, 0, 0, 0))
    attended, dq, dk, dv, bias_out = pl.pallas_call(
        attend_kernel,
        grid=(4,),
        in_specs=[full, full, full, full, blocks],
        out_specs=[full, full, full_t, full_t, blocks],
        out_shape=[sds((4, 512, 128), F32), sds((4, 512, 128), F32), sds((4, 128, 512), F32),
                   sds((4, 128, 512), F32), sds((16, 8, 80, 128), BF16)],
        scratch_shapes=[pltpu.VMEM((512, 512), F32), pltpu.VMEM((512, 512), F32)],
        compiler_params=PARAMS,
        name="attend",
    )(query, keys, values, grad_att, bias_all)

    by_row_t = pl.BlockSpec((1, 128, 512), lambda i: (i, 0, 0))
    ug_rows, sums_out, off = pl.pallas_call(
        functools.partial(post_kernel, scale),
        grid=(4,),
        in_specs=[by_row, by_row, by_row_t, by_row_t, by_row, by_row, by_row, from_cot,
                  whole((128, 512)), whole((128, 128)), pl.BlockSpec(memory_space=pl.ANY)],
        out_specs=[from_rows, pl.BlockSpec((128, 16, 128), lambda i: (0, 4, 0)), whole((8, 128))],
        out_shape=[sds((8, 2, 4, 64, 128), BF16), sds((128, 80, 128), BF16), sds((8, 128), F32)],
        scratch_shapes=[pltpu.VMEM((128, 512), F32), pltpu.VMEM((128, 128), F32), pltpu.VMEM((1, 128), F32),
                        pltpu.VMEM((128, 16, 128), F32)],
        input_output_aliases={10: 1},
        compiler_params=PARAMS,
        name="post",
    )(attended, dq, dk, dv, gate, grad_gated, normed, both_rows, wcat, w_out, bias_out.reshape(128, 80, 128))
    ug_tile = swap(ug_rows, "col")
    sums_in = swap(sums_out, everyone)
    update, grad_pair, final_msg = pl.pallas_call(
        tile_final_kernel,
        out_shape=[sds((2048, 128), BF16), sds((2048, 128), BF16), sds((128, 16, 128), F32)],
        scratch_shapes=[pltpu.VMEM((80, 128), F32), pltpu.VMEM((8, 2048), F32)],
        compiler_params=PARAMS,
        name="tile_final",
    )(pair_tile, ug_tile.reshape(8, 2, 256, 128), sums_in, off, gain, wb_two)
    final_in = swap(final_msg, everyone)
    g_query, g_key, g_value, g_gate, g_out, g_off, g_gain, g_bias = pl.pallas_call(
        finish_kernel,
        out_shape=[sds((128, 128), F32)] * 5 + [sds((128,), F32)] * 2 + [sds((4, 128), F32)],
        compiler_params=PARAMS,
        name="finish",
    )(final_in)
    return (
        update.reshape(32, 64, 128),
        grad_pair.reshape(32, 64, 128),
        g_gain,
        g_query,
        g_key,
        g_value,
        g_gate,
        g_off,
        g_bias.T,
        g_out,
    )


def solution(mesh):
    tile = P("row", "col", None)
    return jax.shard_map(
        body,
        mesh=mesh,
        in_specs=(tile, tile) + (P(),) * 8,
        out_specs=(tile, tile) + (P(),) * 8,
        check_vma=False,
    )
```

```python
import functools

import jax
import jax.numpy as jnp
from jax import lax
from jax.experimental import pallas as pl
from jax.experimental.pallas import tpu as pltpu
from jax.sharding import PartitionSpec as P

EPS = 1e-05
F32 = jnp.float32
BF16 = jnp.bfloat16
NT = (((1,), (1,)), ((), ()))
TN = (((0,), (0,)), ((), ()))
SHIFTS = tuple((y, x) for y in range(4) for x in range(2))
PARAMS = pltpu.CompilerParams(vmem_limit_bytes=56 * 1024 * 1024)


def dot(left, right, dims=(((1,), (0,)), ((), ()))):
    return lax.dot_general(left, right, dims, preferred_element_type=F32)


def normalize(values, gain):
    average = jnp.mean(values, axis=-1, keepdims=True)
    centered = values - average
    variance = jnp.mean(centered * centered, axis=-1, keepdims=True)
    inverse = lax.rsqrt(variance + EPS)
    unit = centered * inverse
    return unit, inverse, (unit * gain).astype(BF16)


def low_lanes(shape):
    return lax.broadcasted_iota(jnp.int32, shape, len(shape) - 1) < 64


def join_low(left, right):
    return jnp.where(low_lanes(left.shape), left, pltpu.roll(right, 64, left.ndim - 1))


def join_high(left, right):
    return jnp.where(low_lanes(left.shape), pltpu.roll(left, 64, left.ndim - 1), right)


def head_mask(heads, channels, dtype):
    lane = lax.broadcasted_iota(jnp.int32, (1, heads, 1, channels), 3)
    head = lax.broadcasted_iota(jnp.int32, (1, heads, 1, channels), 1)
    return jnp.where(lane // (channels // heads) == head, 1.0, 0.0).astype(dtype)


def col_pairs(shift):
    return [(c, ((c // 2 + shift[0]) % 4) * 2 + (c % 2 + shift[1]) % 2) for c in range(8)]


def prepare_kernel(to_ref, pair_ref, cot_ref, gain_ref, wb_ref, msg_ref, *refs):
    rows_ref = refs[8]
    unit, inverse, normed = normalize(pair_ref[...].reshape(2048, 128).astype(F32), gain_ref[...])
    bias = dot(wb_ref[...], normed, NT)
    for at in range(8):
        dest = to_ref[at]
        refs[at][0] = pair_ref[dest]
        refs[at][1] = cot_ref[dest]
    for half in range(8):
        first = bias[0:8, half * 128 : half * 128 + 128]
        second = bias[0:8, (8 + half) * 128 : (8 + half) * 128 + 128]
        even = join_low(first, second)
        odd = join_high(first, second)
        for head in range(4):
            base = head * 16 + 2 * half
            rows_ref[base : base + 1, :] = even[head : head + 1]
            rows_ref[base + 1 : base + 2, :] = odd[head : head + 1]
    msg_ref[...] = jnp.broadcast_to(rows_ref[...].astype(BF16)[None], msg_ref.shape)


def project_kernel(scale, from_ref, *refs):
    pieces = refs[:8]
    gain_ref, wcat_ref, off_ref, wout_ref = refs[8:12]
    q_ref, k_ref, v_ref, a_ref, gate_ref, gg_ref, n_ref, cot_ref, pair_scr = refs[12:]
    for at in range(8):
        rows = pl.ds(pl.multiple_of(from_ref[at] * 64, 64), 64)
        pair_scr[rows, :] = pieces[at][0, 0]
        cot_ref[0, rows, :] = pieces[at][1, 0]
    unit, inverse, normed = normalize(pair_scr[...].astype(F32), gain_ref[...])
    projected = dot(normed, wcat_ref[...])
    gate = jax.nn.sigmoid(projected[:, 384:512] + off_ref[...])
    grad_gated = dot(cot_ref[0], wout_ref[...], NT)
    q_ref[0] = (projected[:, 0:128] * scale).astype(BF16)
    k_ref[0] = (projected[:, 128:256] * scale).astype(BF16)
    v_ref[0] = projected[:, 256:384].astype(BF16)
    a_ref[0] = (grad_gated * gate).astype(BF16)
    gate_ref[0] = gate
    gg_ref[0] = grad_gated
    n_ref[0] = normed


def attend_kernel(q_ref, k_ref, v_ref, a_ref, bias_ref,
                  att_ref, dq_ref, dk_ref, dv_ref, out_ref, bias_scr, sum_scr):
    chunk = pl.program_id(0)
    for r in range(4):
        for m in range(4):
            left = bias_ref[r, 2 * m].astype(F32)
            right = bias_ref[r, 2 * m + 1].astype(F32)
            lanes = slice(m * 128, m * 128 + 128)
            bias_scr[r * 128 : r * 128 + 64, lanes] = join_low(left, right)
            bias_scr[r * 128 + 64 : r * 128 + 128, lanes] = join_high(left, right)
    mask = head_mask(4, 128, BF16)
    mask_f = head_mask(4, 128, F32)

    def spread(rows):
        return (rows.reshape(8, 1, 16, 128) * mask).reshape(512, 128)

    def collect(rows):
        return jnp.sum(rows.reshape(8, 4, 16, 128) * mask_f, axis=1).reshape(128, 128)

    def step(row, carry):
        at = pl.ds(pl.multiple_of(chunk * 128, 128), 128)
        q_big = spread(q_ref[row, at, :])
        a_big = spread(a_ref[row, at, :])
        keys = k_ref[row]
        values = v_ref[row]
        scores = dot(q_big, keys, NT) + bias_scr[...]
        top = jnp.max(scores, axis=-1, keepdims=True)
        powers = jnp.exp(scores - top)
        probs = powers * (1.0 / jnp.sum(powers, axis=-1, keepdims=True))
        probs_low = probs.astype(BF16)
        att_ref[row, at, :] = collect(dot(probs_low, values))
        grad_probs = dot(a_big, values, NT)
        inner = jnp.sum(probs * grad_probs, axis=-1, keepdims=True)
        score_grad = probs * (grad_probs - inner)
        score_low = score_grad.astype(BF16)
        dq_ref[row, at, :] = collect(dot(score_low, keys))
        dk = dot(q_big, score_low, TN)
        dv = dot(a_big, probs_low, TN)

        @pl.when(chunk == 0)
        def _():
            dk_ref[row] = dk
            dv_ref[row] = dv

        @pl.when(chunk > 0)
        def _():
            dk_ref[row] += dk
            dv_ref[row] += dv

        @pl.when(row == 0)
        def _():
            sum_scr[...] = score_grad

        @pl.when(row > 0)
        def _():
            sum_scr[...] += score_grad

        return carry

    lax.fori_loop(0, 4, step, 0)
    for r in range(4):
        for m in range(4):
            lanes = slice(m * 128, m * 128 + 128)
            low = sum_scr[r * 128 : r * 128 + 64, lanes]
            high = sum_scr[r * 128 + 64 : r * 128 + 128, lanes]
            out_ref[r, 2 * m] = join_low(low, high).astype(BF16)
            out_ref[r, 2 * m + 1] = join_high(low, high).astype(BF16)


def post_kernel(scale, to_ref, att_ref, dq_ref, dk_ref, dv_ref, gate_ref, gg_ref, n_ref, cot_ref, wcat_ref,
                wout_ref, held_ref, par_ref, off_ref, *refs):
    pieces = refs[:8]
    w_scr, o_scr, s_scr, p_scr, up_scr, gn_scr = refs[8:]
    row = pl.program_id(0)
    attended = att_ref[0]
    gate = gate_ref[0]
    grad_gated = gg_ref[0]
    gated = (gate * attended).astype(BF16)
    cot = cot_ref[0]
    up_scr[...] = dot(gated, wout_ref[...]).astype(BF16)
    out_part = dot(gated, cot, TN)
    gpre = (grad_gated * attended * gate * (1.0 - gate)).astype(BF16)
    qpre = (dq_ref[0] * scale).astype(BF16)
    kpre = (jnp.transpose(dk_ref[0]) * scale).astype(BF16)
    vpre = jnp.transpose(dv_ref[0]).astype(BF16)
    cat = jnp.concatenate([qpre, kpre, vpre, gpre], axis=1)
    gn_scr[...] = dot(cat, wcat_ref[...], NT).astype(BF16)
    for at in range(8):
        rows = pl.ds(pl.multiple_of(to_ref[at] * 64, 64), 64)
        pieces[at][0, 0] = up_scr[rows, :]
        pieces[at][1, 0] = gn_scr[rows, :]
    w_part = dot(n_ref[0], cat, TN)
    off = jnp.sum(gpre.astype(F32), axis=0, keepdims=True)

    @pl.when(row == 0)
    def _():
        w_scr[...] = w_part
        o_scr[...] = out_part
        s_scr[...] = off

    @pl.when(row > 0)
    def _():
        w_scr[...] += w_part
        o_scr[...] += out_part
        s_scr[...] += off

    @pl.when(row == 3)
    def _():
        for t in range(5):
            part = w_scr[:, t * 128 : t * 128 + 128] if t < 4 else o_scr[...]
            high = part.astype(BF16).astype(F32)
            p_scr[:, t, :] = high
            p_scr[:, 8 + t, :] = part - high
        for t in range(5, 8):
            p_scr[:, t, :] = jnp.zeros((128, 128), F32)
            p_scr[:, 8 + t, :] = jnp.zeros((128, 128), F32)
        par_ref[...] = p_scr[...].astype(BF16)
        off_ref[...] = jnp.broadcast_to(s_scr[...], off_ref.shape)


def tile_final_kernel(from_ref, pair_ref, sums_ref, off_ref, gain_ref, wb_ref, *refs):
    pieces = refs[:8]
    up_ref, gp_ref, msg_ref, rows_ref, bg_scr, gn_scr = refs[8:]
    for at in range(8):
        rows = pl.ds(pl.multiple_of(from_ref[at] * 256, 256), 256)
        up_ref[rows, :] = pieces[at][0]
        gn_scr[rows, :] = pieces[at][1]
    rows_ref[...] = jnp.sum(sums_ref[...].astype(F32), axis=0)
    bg_scr[...] = jnp.zeros(bg_scr.shape, F32)
    for half in range(8):
        for head in range(4):
            base = head * 16 + 2 * half
            left = rows_ref[base : base + 1, :]
            right = rows_ref[base + 1 : base + 2, :]
            bg_scr[head : head + 1, half * 128 : half * 128 + 128] = join_low(left, right)
            bg_scr[head : head + 1, (8 + half) * 128 : (8 + half) * 128 + 128] = join_high(left, right)
    bg = bg_scr[...]
    high = bg.astype(BF16)
    low = (bg - high.astype(F32)).astype(BF16)
    both = jnp.concatenate([high.astype(F32), low.astype(F32)], axis=0).astype(BF16)
    unit, inverse, normed = normalize(pair_ref[...].astype(F32), gain_ref[...])
    total = gn_scr[...].astype(F32) + dot(both, wb_ref[...], TN)
    bias_part = dot(both, normed)
    gain_part = jnp.sum(total * unit, axis=0, keepdims=True)
    scaled = total * gain_ref[...]
    first = jnp.mean(scaled, axis=-1, keepdims=True)
    second = jnp.mean(scaled * unit, axis=-1, keepdims=True)
    gp_ref[...] = ((scaled - first - unit * second) * inverse).astype(BF16)
    params = rows_ref[64:72, :] + rows_ref[72:80, :]
    row = lax.broadcasted_iota(jnp.int32, (8, 128), 0)
    params = jnp.where(row == 5, off_ref[...], jnp.where(row == 6, gain_part, params))
    small = bias_part[0:8] + bias_part[8:16]
    msg_ref[...] = jnp.broadcast_to(jnp.concatenate([params, small], axis=0)[None], msg_ref.shape)


def finish_kernel(msg_ref, q_ref, k_ref, v_ref, g_ref, o_ref, off_ref, gain_ref, bias_ref):
    for t, ref in enumerate((q_ref, k_ref, v_ref, g_ref, o_ref)):
        ref[...] = msg_ref[:, t, :]
    small = jnp.sum(msg_ref[...], axis=0)
    off_ref[...] = small[5]
    gain_ref[...] = small[6]
    bias_ref[...] = small[8:12]


def sds(shape, dtype):
    return jax.ShapeDtypeStruct(shape, dtype)


def whole(shape):
    return pl.BlockSpec(shape, lambda *_: (0,) * len(shape))


def body(pair_rep, cotangent, ln_gain, w_query, w_key, w_value, w_gate, gate_offset, w_bias, w_out):
    scale = 32 ** (-0.5)
    gain = ln_gain.reshape(1, 128)
    offset = gate_offset.reshape(1, 128)
    wcat = jnp.concatenate([w_query, w_key, w_value, w_gate], axis=1)
    wb_pad = jnp.pad(w_bias.T, ((0, 4), (0, 0)))
    wb_two = jnp.concatenate([wb_pad, wb_pad], axis=0)
    everyone = ("row", "col")
    pair_tile = pair_rep.reshape(2048, 128)

    def swap(value, axes):
        return lax.all_to_all(value, axes, split_axis=0, concat_axis=0, tiled=True)

    col = lax.axis_index("col")
    to_col = jnp.stack([((col // 2 + y) % 4) * 2 + (col % 2 + x) % 2 for y, x in SHIFTS])
    from_col = jnp.stack([((col // 2 + 4 - y) % 4) * 2 + (col % 2 + x) % 2 for y, x in SHIFTS])
    smem = pl.BlockSpec(memory_space=pltpu.SMEM)

    def exchange(pieces):
        return [pieces[0]] + [
            lax.ppermute(piece, "col", col_pairs(shift)) for piece, shift in zip(pieces[1:], SHIFTS[1:])
        ]

    bias_msg, *pieces = pl.pallas_call(
        prepare_kernel,
        in_specs=[smem] + [whole((8, 4, 64, 128))] * 2 + [whole((1, 128)), whole((16, 128))],
        out_shape=[sds((128, 64, 128), BF16)] + [sds((2, 4, 64, 128), BF16)] * 8,
        scratch_shapes=[pltpu.VMEM((64, 128), F32)],
        compiler_params=PARAMS,
        name="prepare",
    )(to_col, pair_rep.reshape(8, 4, 64, 128), cotangent.reshape(8, 4, 64, 128), gain, wb_two)
    bias_all = swap(bias_msg, everyone).reshape(16, 8, 64, 128)
    pieces = exchange(pieces)

    piece_row = pl.BlockSpec((2, 1, 64, 128), lambda i: (0, i, 0, 0))
    by_row = pl.BlockSpec((1, 512, 128), lambda i: (i, 0, 0))
    query, keys, values, grad_att, gate, grad_gated, normed, cot_rows = pl.pallas_call(
        functools.partial(project_kernel, scale),
        grid=(4,),
        in_specs=[smem] + [piece_row] * 8 + [whole((1, 128)), whole((128, 512)), whole((1, 128)), whole((128, 128))],
        out_specs=[by_row] * 8,
        out_shape=[sds((4, 512, 128), t) for t in (BF16, BF16, BF16, BF16, F32, F32, BF16, BF16)],
        scratch_shapes=[pltpu.VMEM((512, 128), BF16)],
        compiler_params=PARAMS,
        name="project",
    )(from_col, *pieces, gain, wcat, offset, w_out)

    full = whole((4, 512, 128))
    full_t = whole((4, 128, 512))
    blocks = pl.BlockSpec((4, 8, 64, 128), lambda c: (c, 0, 0, 0))
    attended, dq, dk, dv, bias_out = pl.pallas_call(
        attend_kernel,
        grid=(4,),
        in_specs=[full, full, full, full, blocks],
        out_specs=[full, full, full_t, full_t, blocks],
        out_shape=[sds((4, 512, 128), F32), sds((4, 512, 128), F32), sds((4, 128, 512), F32),
                   sds((4, 128, 512), F32), sds((16, 8, 80, 128), BF16)],
        scratch_shapes=[pltpu.VMEM((512, 512), F32), pltpu.VMEM((512, 512), F32)],
        compiler_params=PARAMS,
        name="attend",
    )(query, keys, values, grad_att, bias_all)

    by_row_t = pl.BlockSpec((1, 128, 512), lambda i: (i, 0, 0))
    sums_out, off, *pieces = pl.pallas_call(
        functools.partial(post_kernel, scale),
        grid=(4,),
        in_specs=[smem, by_row, by_row, by_row_t, by_row_t, by_row, by_row, by_row, by_row,
                  whole((128, 512)), whole((128, 128)), pl.BlockSpec(memory_space=pl.ANY)],
        out_specs=[pl.BlockSpec((128, 16, 128), lambda i: (0, 4, 0)), whole((8, 128))] + [piece_row] * 8,
        out_shape=[sds((128, 80, 128), BF16), sds((8, 128), F32)] + [sds((2, 4, 64, 128), BF16)] * 8,
        scratch_shapes=[pltpu.VMEM((128, 512), F32), pltpu.VMEM((128, 128), F32), pltpu.VMEM((1, 128), F32),
                        pltpu.VMEM((128, 16, 128), F32), pltpu.VMEM((512, 128), BF16), pltpu.VMEM((512, 128), BF16)],
        input_output_aliases={11: 0},
        compiler_params=PARAMS,
        name="post",
    )(to_col, attended, dq, dk, dv, gate, grad_gated, normed, cot_rows, wcat, w_out, bias_out.reshape(128, 80, 128))
    sums_in = swap(sums_out, everyone)
    pieces = [piece.reshape(2, 256, 128) for piece in exchange(pieces)]
    update, grad_pair, final_msg = pl.pallas_call(
        tile_final_kernel,
        in_specs=[smem, whole((2048, 128)), whole((128, 80, 128)), whole((8, 128)), whole((1, 128)), whole((16, 128))]
        + [whole((2, 256, 128))] * 8,
        out_shape=[sds((2048, 128), BF16), sds((2048, 128), BF16), sds((128, 16, 128), F32)],
        scratch_shapes=[pltpu.VMEM((80, 128), F32), pltpu.VMEM((8, 2048), F32), pltpu.VMEM((2048, 128), BF16)],
        compiler_params=PARAMS,
        name="tile_final",
    )(from_col, pair_tile, sums_in, off, gain, wb_two, *pieces)
    final_in = swap(final_msg, everyone)
    g_query, g_key, g_value, g_gate, g_out, g_off, g_gain, g_bias = pl.pallas_call(
        finish_kernel,
        out_shape=[sds((128, 128), F32)] * 5 + [sds((128,), F32)] * 2 + [sds((4, 128), F32)],
        compiler_params=PARAMS,
        name="finish",
    )(final_in)
    return (
        update.reshape(32, 64, 128),
        grad_pair.reshape(32, 64, 128),
        g_gain,
        g_query,
        g_key,
        g_value,
        g_gate,
        g_off,
        g_bias.T,
        g_out,
    )


def solution(mesh):
    tile = P("row", "col", None)
    return jax.shard_map(
        body,
        mesh=mesh,
        in_specs=(tile, tile) + (P(),) * 8,
        out_specs=(tile, tile) + (P(),) * 8,
        check_vma=False,
    )
```

```python
import functools

import jax
import jax.numpy as jnp
from jax import lax
from jax.experimental import pallas as pl
from jax.experimental.pallas import tpu as pltpu
from jax.sharding import PartitionSpec as P

EPS = 1e-05
F32 = jnp.float32
BF16 = jnp.bfloat16
NT = (((1,), (1,)), ((), ()))
TN = (((0,), (0,)), ((), ()))
HOPS = (0, 1, 3, 2)
PARAMS = pltpu.CompilerParams(vmem_limit_bytes=56 * 1024 * 1024)


def dot(left, right, dims=(((1,), (0,)), ((), ()))):
    return lax.dot_general(left, right, dims, preferred_element_type=F32)


def normalize(values, gain):
    average = jnp.mean(values, axis=-1, keepdims=True)
    centered = values - average
    variance = jnp.mean(centered * centered, axis=-1, keepdims=True)
    inverse = lax.rsqrt(variance + EPS)
    unit = centered * inverse
    return unit, inverse, (unit * gain).astype(BF16)


def low_lanes(shape):
    return lax.broadcasted_iota(jnp.int32, shape, len(shape) - 1) < 64


def join_low(left, right):
    return jnp.where(low_lanes(left.shape), left, pltpu.roll(right, 64, left.ndim - 1))


def join_high(left, right):
    return jnp.where(low_lanes(left.shape), pltpu.roll(left, 64, left.ndim - 1), right)


def head_mask(heads, channels, dtype):
    lane = lax.broadcasted_iota(jnp.int32, (1, heads, 1, channels), 3)
    head = lax.broadcasted_iota(jnp.int32, (1, heads, 1, channels), 1)
    return jnp.where(lane // (channels // heads) == head, 1.0, 0.0).astype(dtype)


def flat_index(x, y, z, core):
    return (((x % 2) * 4 + z) * 2 + core) * 8 + y * 2 + x // 2


def shift_pairs(x=0, y=0, z=0, core=0):
    pairs = []
    for a in range(4):
        for b in range(4):
            for c in range(4):
                for d in range(2):
                    target = flat_index((a + x) % 4, (b + y) % 4, (c + z) % 4, (d + core) % 2)
                    pairs.append((flat_index(a, b, c, d), target))
    return sorted(pairs)


def seen(place_ref, sign):
    x, y, z = ([(place_ref[at] + 4 + sign * hop) & 3 for hop in HOPS] for at in range(3))
    core = [place_ref[3], 1 - place_ref[3]]
    return (
        [(a & 1) * 64 + (a >> 1) for a in x],
        [b * 2 for b in y],
        [c * 16 for c in z],
        [d * 8 for d in core],
    )


def slot_of(delta):
    delta = (delta + 4) & 3
    return jnp.where(delta < 2, delta, 5 - delta)


def send(value, **shift):
    return lax.ppermute(value, ("row", "col"), shift_pairs(**shift))


def gather_bias(message):
    held = message
    held = jnp.stack([held] + [send(held, z=hop) for hop in HOPS[1:]])
    held = jnp.stack([held] + [send(held, y=hop) for hop in HOPS[1:]])
    held = held.reshape(16, 64, 128)
    pieces = [held] + [send(held, x=hop) for hop in HOPS[1:]]
    return pieces + [send(piece, core=1) for piece in pieces]


def add_up(parts):
    return sum(part.astype(F32) for part in parts).astype(BF16)


def scatter_sums(mine, other):
    held = add_up([mine, send(other, core=1)]).reshape(4, 16, 80, 128)
    held = add_up([held[0]] + [send(held[at], z=HOPS[at]) for at in (1, 2, 3)]).reshape(4, 4, 80, 128)
    held = add_up([held[0]] + [send(held[at], y=HOPS[at]) for at in (1, 2, 3)])
    return [held[0]] + [send(held[at], x=HOPS[at]) for at in (1, 2, 3)]


def tile_bias_kernel(pair_ref, gain_ref, wb_ref, msg_ref, rows_ref):
    unit, inverse, normed = normalize(pair_ref[...].astype(F32), gain_ref[...])
    bias = dot(wb_ref[...], normed, NT)
    for half in range(8):
        first = bias[0:8, half * 128 : half * 128 + 128]
        second = bias[0:8, (8 + half) * 128 : (8 + half) * 128 + 128]
        even = join_low(first, second)
        odd = join_high(first, second)
        for head in range(4):
            base = head * 16 + 2 * half
            rows_ref[base : base + 1, :] = even[head : head + 1]
            rows_ref[base + 1 : base + 2, :] = odd[head : head + 1]
    msg_ref[...] = rows_ref[...].astype(BF16)


def pack_kernel(pair_ref, cot_ref, out_ref):
    out_ref[:, 0] = pair_ref[...]
    out_ref[:, 1] = cot_ref[...]


def project_kernel(scale, rows_ref, gain_ref, wcat_ref, off_ref, wout_ref,
                   q_ref, k_ref, v_ref, a_ref, gate_ref, gg_ref, n_ref):
    values = rows_ref[:, 0, 0].reshape(512, 128).astype(F32)
    unit, inverse, normed = normalize(values, gain_ref[...])
    projected = dot(normed, wcat_ref[...])
    gate = jax.nn.sigmoid(projected[:, 384:512] + off_ref[...])
    grad_gated = dot(rows_ref[:, 1, 0].reshape(512, 128), wout_ref[...], NT)
    q_ref[0] = (projected[:, 0:128] * scale).astype(BF16)
    k_ref[0] = (projected[:, 128:256] * scale).astype(BF16)
    v_ref[0] = projected[:, 256:384].astype(BF16)
    a_ref[0] = (grad_gated * gate).astype(BF16)
    gate_ref[0] = gate
    gg_ref[0] = grad_gated
    n_ref[0] = normed


def attend_kernel(place_ref, q_ref, k_ref, v_ref, a_ref, *refs):
    pieces = refs[:8]
    att_ref, dq_ref, dk_ref, dv_ref, mine_ref, other_ref, block_scr, bias_scr, sum_scr = refs[8:]
    chunk = pl.program_id(0)

    @pl.when(chunk == 0)
    def _():
        x, y, z, core = seen(place_ref, -1)
        for at in range(8):
            for inner in range(16):
                owner = x[at % 4] + y[inner // 4] + z[inner % 4] + core[at // 4]
                block_scr[owner] = pieces[at][inner]

    for r in range(4):
        for m in range(4):
            left = block_scr[(chunk * 4 + r) * 8 + 2 * m].astype(F32)
            right = block_scr[(chunk * 4 + r) * 8 + 2 * m + 1].astype(F32)
            lanes = slice(m * 128, m * 128 + 128)
            bias_scr[r * 128 : r * 128 + 64, lanes] = join_low(left, right)
            bias_scr[r * 128 + 64 : r * 128 + 128, lanes] = join_high(left, right)
    mask = head_mask(4, 128, BF16)
    mask_f = head_mask(4, 128, F32)

    def spread(rows):
        return (rows.reshape(8, 1, 16, 128) * mask).reshape(512, 128)

    def collect(rows):
        return jnp.sum(rows.reshape(8, 4, 16, 128) * mask_f, axis=1).reshape(128, 128)

    def step(row, carry):
        at = pl.ds(pl.multiple_of(chunk * 128, 128), 128)
        q_big = spread(q_ref[row, at, :])
        a_big = spread(a_ref[row, at, :])
        keys = k_ref[row]
        values = v_ref[row]
        scores = dot(q_big, keys, NT) + bias_scr[...]
        top = jnp.max(scores, axis=-1, keepdims=True)
        powers = jnp.exp(scores - top)
        probs = powers * (1.0 / jnp.sum(powers, axis=-1, keepdims=True))
        probs_low = probs.astype(BF16)
        att_ref[row, at, :] = collect(dot(probs_low, values))
        grad_probs = dot(a_big, values, NT)
        inner = jnp.sum(probs * grad_probs, axis=-1, keepdims=True)
        score_grad = probs * (grad_probs - inner)
        score_low = score_grad.astype(BF16)
        dq_ref[row, at, :] = collect(dot(score_low, keys))
        dk = dot(q_big, score_low, TN)
        dv = dot(a_big, probs_low, TN)

        @pl.when(chunk == 0)
        def _():
            dk_ref[row] = dk
            dv_ref[row] = dv

        @pl.when(chunk > 0)
        def _():
            dk_ref[row] += dk
            dv_ref[row] += dv

        @pl.when(row == 0)
        def _():
            sum_scr[...] = score_grad

        @pl.when(row > 0)
        def _():
            sum_scr[...] += score_grad

        return carry

    lax.fori_loop(0, 4, step, 0)

    xs = [slot_of(chunk // 2 + 2 * high - place_ref[0]) for high in range(2)]
    ys = [slot_of(at - place_ref[1]) * 4 for at in range(4)]
    zs = [slot_of((chunk % 2) * 2 + at - place_ref[2]) * 16 for at in range(2)]

    def emit(even_ref, odd_ref):
        for r in range(4):
            out_ref = odd_ref if r % 2 else even_ref
            for m in range(4):
                lanes = slice(m * 128, m * 128 + 128)
                low = sum_scr[r * 128 : r * 128 + 64, lanes]
                high = sum_scr[r * 128 + 64 : r * 128 + 128, lanes]
                spot = zs[r // 2] + ys[m]
                out_ref[spot + xs[0], 0:64] = join_low(low, high).astype(BF16)
                out_ref[spot + xs[1], 0:64] = join_high(low, high).astype(BF16)

    @pl.when(place_ref[3] == 0)
    def _():
        emit(mine_ref, other_ref)

    @pl.when(place_ref[3] == 1)
    def _():
        emit(other_ref, mine_ref)


def post_kernel(scale, place_ref, att_ref, dq_ref, dk_ref, dv_ref, gate_ref, gg_ref, n_ref, rows_ref, wcat_ref,
                wout_ref, held_mine, held_other, ug_ref, mine_ref, other_ref, off_ref, w_scr, o_scr, s_scr, p_scr):
    row = pl.program_id(0)
    attended = att_ref[0]
    gate = gate_ref[0]
    grad_gated = gg_ref[0]
    gated = (gate * attended).astype(BF16)
    cot = rows_ref[:, 0, 0].reshape(512, 128)
    ug_ref[:, 0, 0] = dot(gated, wout_ref[...]).astype(BF16).reshape(8, 64, 128)
    out_part = dot(gated, cot, TN)
    gpre = (grad_gated * attended * gate * (1.0 - gate)).astype(BF16)
    qpre = (dq_ref[0] * scale).astype(BF16)
    kpre = (jnp.transpose(dk_ref[0]) * scale).astype(BF16)
    vpre = jnp.transpose(dv_ref[0]).astype(BF16)
    cat = jnp.concatenate([qpre, kpre, vpre, gpre], axis=1)
    ug_ref[:, 1, 0] = dot(cat, wcat_ref[...], NT).astype(BF16).reshape(8, 64, 128)
    w_part = dot(n_ref[0], cat, TN)
    off = jnp.sum(gpre.astype(F32), axis=0, keepdims=True)

    @pl.when(row == 0)
    def _():
        w_scr[...] = w_part
        o_scr[...] = out_part
        s_scr[...] = off

    @pl.when(row > 0)
    def _():
        w_scr[...] += w_part
        o_scr[...] += out_part
        s_scr[...] += off

    @pl.when(row == 3)
    def _():
        for t in range(5):
            part = w_scr[:, t * 128 : t * 128 + 128] if t < 4 else o_scr[...]
            high = part.astype(BF16).astype(F32)
            p_scr[:, t, :] = high
            p_scr[:, 8 + t, :] = part - high
        for t in range(5, 8):
            p_scr[:, t, :] = jnp.zeros((128, 128), F32)
            p_scr[:, 8 + t, :] = jnp.zeros((128, 128), F32)
        x, y, z, core = seen(place_ref, 1)
        for at in range(64):
            owner = z[at // 16] + y[at // 4 % 4] + x[at % 4]
            mine_ref[at] = p_scr[owner + core[0]].astype(BF16)
            other_ref[at] = p_scr[owner + core[1]].astype(BF16)
        off_ref[...] = jnp.broadcast_to(s_scr[...], off_ref.shape)


def tile_final_kernel(pair_ref, ug_ref, one_ref, two_ref, three_ref, four_ref, off_ref, gain_ref, wb_ref,
                      up_ref, gp_ref, msg_ref, rows_ref, bg_scr):
    up_ref[...] = ug_ref[:, 0].reshape(2048, 128)
    rows_ref[...] = (one_ref[...].astype(F32) + two_ref[...].astype(F32)) + (
        three_ref[...].astype(F32) + four_ref[...].astype(F32)
    )
    bg_scr[...] = jnp.zeros(bg_scr.shape, F32)
    for half in range(8):
        for head in range(4):
            base = head * 16 + 2 * half
            left = rows_ref[base : base + 1, :]
            right = rows_ref[base + 1 : base + 2, :]
            bg_scr[head : head + 1, half * 128 : half * 128 + 128] = join_low(left, right)
            bg_scr[head : head + 1, (8 + half) * 128 : (8 + half) * 128 + 128] = join_high(left, right)
    bg = bg_scr[...]
    high = bg.astype(BF16)
    low = (bg - high.astype(F32)).astype(BF16)
    both = jnp.concatenate([high.astype(F32), low.astype(F32)], axis=0).astype(BF16)
    unit, inverse, normed = normalize(pair_ref[...].astype(F32), gain_ref[...])
    total = ug_ref[:, 1].reshape(2048, 128).astype(F32) + dot(both, wb_ref[...], TN)
    bias_part = dot(both, normed)
    gain_part = jnp.sum(total * unit, axis=0, keepdims=True)
    scaled = total * gain_ref[...]
    first = jnp.mean(scaled, axis=-1, keepdims=True)
    second = jnp.mean(scaled * unit, axis=-1, keepdims=True)
    gp_ref[...] = ((scaled - first - unit * second) * inverse).astype(BF16)
    params = rows_ref[64:72, :] + rows_ref[72:80, :]
    row = lax.broadcasted_iota(jnp.int32, (8, 128), 0)
    params = jnp.where(row == 5, off_ref[...], jnp.where(row == 6, gain_part, params))
    small = bias_part[0:8] + bias_part[8:16]
    msg_ref[...] = jnp.broadcast_to(jnp.concatenate([params, small], axis=0)[None], msg_ref.shape)


def finish_kernel(msg_ref, q_ref, k_ref, v_ref, g_ref, o_ref, off_ref, gain_ref, bias_ref):
    for t, ref in enumerate((q_ref, k_ref, v_ref, g_ref, o_ref)):
        ref[...] = msg_ref[:, t, :]
    small = jnp.sum(msg_ref[...], axis=0)
    off_ref[...] = small[5]
    gain_ref[...] = small[6]
    bias_ref[...] = small[8:12]


def sds(shape, dtype):
    return jax.ShapeDtypeStruct(shape, dtype)


def whole(shape):
    return pl.BlockSpec(shape, lambda *_: (0,) * len(shape))


def body(pair_rep, cotangent, ln_gain, w_query, w_key, w_value, w_gate, gate_offset, w_bias, w_out):
    scale = 32 ** (-0.5)
    gain = ln_gain.reshape(1, 128)
    offset = gate_offset.reshape(1, 128)
    wcat = jnp.concatenate([w_query, w_key, w_value, w_gate], axis=1)
    wb_pad = jnp.pad(w_bias.T, ((0, 4), (0, 0)))
    wb_two = jnp.concatenate([wb_pad, wb_pad], axis=0)
    everyone = ("row", "col")
    pair_tile = pair_rep.reshape(2048, 128)

    def swap(value, axes):
        return lax.all_to_all(value, axes, split_axis=0, concat_axis=0, tiled=True)

    bias_msg = pl.pallas_call(
        tile_bias_kernel,
        out_shape=sds((64, 128), BF16),
        scratch_shapes=[pltpu.VMEM((64, 128), F32)],
        compiler_params=PARAMS,
        name="tile_bias",
    )(pair_tile, gain, wb_two)
    row, col = lax.axis_index("row"), lax.axis_index("col")
    place = ((col % 2) * 2 + row // 8, col // 2, (row // 2) % 4, row % 2)
    place = jnp.stack(place).astype(jnp.int32)
    smem = pl.BlockSpec(memory_space=pltpu.SMEM)
    packed = pl.pallas_call(
        pack_kernel,
        out_shape=sds((8, 2, 4, 64, 128), BF16),
        compiler_params=PARAMS,
        name="pack",
    )(pair_rep.reshape(8, 4, 64, 128), cotangent.reshape(8, 4, 64, 128))
    both_rows = swap(packed, "col")
    bias_pieces = gather_bias(bias_msg)

    from_rows = pl.BlockSpec((8, 2, 1, 64, 128), lambda i: (0, 0, i, 0, 0))
    from_cot = pl.BlockSpec((8, 1, 1, 64, 128), lambda i: (0, 1, i, 0, 0))
    by_row = pl.BlockSpec((1, 512, 128), lambda i: (i, 0, 0))
    query, keys, values, grad_att, gate, grad_gated, normed = pl.pallas_call(
        functools.partial(project_kernel, scale),
        grid=(4,),
        in_specs=[from_rows, whole((1, 128)), whole((128, 512)), whole((1, 128)), whole((128, 128))],
        out_specs=[by_row] * 7,
        out_shape=[sds((4, 512, 128), t) for t in (BF16, BF16, BF16, BF16, F32, F32, BF16)],
        compiler_params=PARAMS,
        name="project",
    )(both_rows, gain, wcat, offset, w_out)

    full = whole((4, 512, 128))
    full_t = whole((4, 128, 512))
    attended, dq, dk, dv, mine, other = pl.pallas_call(
        attend_kernel,
        grid=(4,),
        in_specs=[smem, full, full, full, full] + [whole((16, 64, 128))] * 8,
        out_specs=[full, full, full_t, full_t, whole((64, 80, 128)), whole((64, 80, 128))],
        out_shape=[sds((4, 512, 128), F32), sds((4, 512, 128), F32), sds((4, 128, 512), F32),
                   sds((4, 128, 512), F32), sds((64, 80, 128), BF16), sds((64, 80, 128), BF16)],
        scratch_shapes=[pltpu.VMEM((128, 64, 128), BF16), pltpu.VMEM((512, 512), F32), pltpu.VMEM((512, 512), F32)],
        compiler_params=PARAMS,
        name="attend",
    )(place, query, keys, values, grad_att, *bias_pieces)

    by_row_t = pl.BlockSpec((1, 128, 512), lambda i: (i, 0, 0))
    tail = pl.BlockSpec((64, 16, 128), lambda i: (0, 4, 0))
    ug_rows, mine, other, off = pl.pallas_call(
        functools.partial(post_kernel, scale),
        grid=(4,),
        in_specs=[smem, by_row, by_row, by_row_t, by_row_t, by_row, by_row, by_row, from_cot,
                  whole((128, 512)), whole((128, 128))] + [pl.BlockSpec(memory_space=pl.ANY)] * 2,
        out_specs=[from_rows, tail, tail, whole((8, 128))],
        out_shape=[sds((8, 2, 4, 64, 128), BF16), sds((64, 80, 128), BF16), sds((64, 80, 128), BF16),
                   sds((8, 128), F32)],
        scratch_shapes=[pltpu.VMEM((128, 512), F32), pltpu.VMEM((128, 128), F32), pltpu.VMEM((1, 128), F32),
                        pltpu.VMEM((128, 16, 128), F32)],
        input_output_aliases={11: 1, 12: 2},
        compiler_params=PARAMS,
        name="post",
    )(place, attended, dq, dk, dv, gate, grad_gated, normed, both_rows, wcat, w_out, mine, other)
    ug_tile = swap(ug_rows, "col")
    sums = scatter_sums(mine, other)
    update, grad_pair, final_msg = pl.pallas_call(
        tile_final_kernel,
        out_shape=[sds((2048, 128), BF16), sds((2048, 128), BF16), sds((128, 16, 128), F32)],
        scratch_shapes=[pltpu.VMEM((80, 128), F32), pltpu.VMEM((8, 2048), F32)],
        compiler_params=PARAMS,
        name="tile_final",
    )(pair_tile, ug_tile.reshape(8, 2, 256, 128), *sums, off, gain, wb_two)
    final_in = swap(final_msg, everyone)
    g_query, g_key, g_value, g_gate, g_out, g_off, g_gain, g_bias = pl.pallas_call(
        finish_kernel,
        out_shape=[sds((128, 128), F32)] * 5 + [sds((128,), F32)] * 2 + [sds((4, 128), F32)],
        compiler_params=PARAMS,
        name="finish",
    )(final_in)
    return (
        update.reshape(32, 64, 128),
        grad_pair.reshape(32, 64, 128),
        g_gain,
        g_query,
        g_key,
        g_value,
        g_gate,
        g_off,
        g_bias.T,
        g_out,
    )


def solution(mesh):
    tile = P("row", "col", None)
    return jax.shard_map(
        body,
        mesh=mesh,
        in_specs=(tile, tile) + (P(),) * 8,
        out_specs=(tile, tile) + (P(),) * 8,
        check_vma=False,
    )
```

```python
import functools

import jax
import jax.numpy as jnp
from jax import lax
from jax.experimental import pallas as pl
from jax.experimental.pallas import tpu as pltpu
from jax.sharding import PartitionSpec as P

EPS = 1e-05
F32 = jnp.float32
BF16 = jnp.bfloat16
NT = (((1,), (1,)), ((), ()))
TN = (((0,), (0,)), ((), ()))
HOPS = (0, 1, 3, 2)
PARAMS = pltpu.CompilerParams(vmem_limit_bytes=56 * 1024 * 1024)


def dot(left, right, dims=(((1,), (0,)), ((), ()))):
    return lax.dot_general(left, right, dims, preferred_element_type=F32)


def normalize(values, gain):
    average = jnp.mean(values, axis=-1, keepdims=True)
    centered = values - average
    variance = jnp.mean(centered * centered, axis=-1, keepdims=True)
    inverse = lax.rsqrt(variance + EPS)
    unit = centered * inverse
    return unit, inverse, (unit * gain).astype(BF16)


def low_lanes(shape):
    return lax.broadcasted_iota(jnp.int32, shape, len(shape) - 1) < 64


def join_low(left, right):
    return jnp.where(low_lanes(left.shape), left, pltpu.roll(right, 64, left.ndim - 1))


def join_high(left, right):
    return jnp.where(low_lanes(left.shape), pltpu.roll(left, 64, left.ndim - 1), right)


def head_mask(heads, channels, dtype):
    lane = lax.broadcasted_iota(jnp.int32, (1, heads, 1, channels), 3)
    head = lax.broadcasted_iota(jnp.int32, (1, heads, 1, channels), 1)
    return jnp.where(lane // (channels // heads) == head, 1.0, 0.0).astype(dtype)


def flat_index(x, y, z, core):
    return (((x % 2) * 4 + z) * 2 + core) * 8 + y * 2 + x // 2


def shift_pairs(x=0, y=0, z=0, core=0):
    pairs = []
    for a in range(4):
        for b in range(4):
            for c in range(4):
                for d in range(2):
                    target = flat_index((a + x) % 4, (b + y) % 4, (c + z) % 4, (d + core) % 2)
                    pairs.append((flat_index(a, b, c, d), target))
    return sorted(pairs)


def seen(place_ref, sign):
    x, y, z = ([(place_ref[at] + 4 + sign * hop) & 3 for hop in HOPS] for at in range(3))
    core = [place_ref[3], 1 - place_ref[3]]
    return (
        [(a & 1) * 64 + (a >> 1) for a in x],
        [b * 2 for b in y],
        [c * 16 for c in z],
        [d * 8 for d in core],
    )


def slot_of(delta):
    delta = (delta + 4) & 3
    return jnp.where(delta < 2, delta, 5 - delta)


def send(value, **shift):
    return lax.ppermute(value, ("row", "col"), shift_pairs(**shift))


def gather_bias(message):
    held = message
    held = jnp.stack([held] + [send(held, z=hop) for hop in HOPS[1:]])
    held = jnp.stack([held] + [send(held, y=hop) for hop in HOPS[1:]])
    held = held.reshape(16, 64, 128)
    pieces = [held] + [send(held, x=hop) for hop in HOPS[1:]]
    return pieces + [send(piece, core=1) for piece in pieces]


def add_up(parts):
    return sum(part.astype(F32) for part in parts).astype(BF16)


def scatter_sums(mine, other):
    held = add_up([mine, send(other, core=1)]).reshape(4, 16, 80, 128)
    held = add_up([held[0]] + [send(held[at], z=HOPS[at]) for at in (1, 2, 3)]).reshape(4, 4, 80, 128)
    held = add_up([held[0]] + [send(held[at], y=HOPS[at]) for at in (1, 2, 3)])
    return [held[0]] + [send(held[at], x=HOPS[at]) for at in (1, 2, 3)]


def tile_bias_kernel(pair_ref, gain_ref, wb_ref, msg_ref, n_ref, u_ref, rows_ref):
    unit, inverse, normed = normalize(pair_ref[...].astype(F32), gain_ref[...])
    n_ref[...] = normed
    u_ref[...] = unit.astype(BF16)
    bias = dot(wb_ref[...], normed, NT)
    for half in range(8):
        first = bias[0:8, half * 128 : half * 128 + 128]
        second = bias[0:8, (8 + half) * 128 : (8 + half) * 128 + 128]
        even = join_low(first, second)
        odd = join_high(first, second)
        for head in range(4):
            base = head * 16 + 2 * half
            rows_ref[base : base + 1, :] = even[head : head + 1]
            rows_ref[base + 1 : base + 2, :] = odd[head : head + 1]
    msg_ref[...] = rows_ref[...].astype(BF16)


def pack_kernel(pair_ref, cot_ref, after_ref, out_ref):
    out_ref[:, 0] = pair_ref[...]
    out_ref[:, 1] = cot_ref[...]


def project_kernel(scale, rows_ref, gain_ref, wcat_ref, off_ref, wout_ref,
                   q_ref, k_ref, v_ref, a_ref, gate_ref, gg_ref, n_ref, u_ref):
    values = rows_ref[:, 0, 0].reshape(512, 128).astype(F32)
    unit, inverse, normed = normalize(values, gain_ref[...])
    projected = dot(normed, wcat_ref[...])
    gate = jax.nn.sigmoid(projected[:, 384:512] + off_ref[...])
    grad_gated = dot(rows_ref[:, 1, 0].reshape(512, 128), wout_ref[...], NT)
    q_ref[0] = (projected[:, 0:128] * scale).astype(BF16)
    k_ref[0] = (projected[:, 128:256] * scale).astype(BF16)
    v_ref[0] = projected[:, 256:384].astype(BF16)
    a_ref[0] = (grad_gated * gate).astype(BF16)
    gate_ref[0] = gate
    gg_ref[0] = grad_gated
    n_ref[0] = normed
    u_ref[0] = unit.astype(BF16)


def attend_kernel(place_ref, q_ref, k_ref, v_ref, a_ref, *refs):
    pieces = refs[:8]
    att_ref, dq_ref, dk_ref, dv_ref, mine_ref, other_ref, block_scr, bias_scr, sum_scr = refs[8:]
    chunk = pl.program_id(0)

    @pl.when(chunk == 0)
    def _():
        x, y, z, core = seen(place_ref, -1)
        for at in range(8):
            for inner in range(16):
                owner = x[at % 4] + y[inner // 4] + z[inner % 4] + core[at // 4]
                block_scr[owner] = pieces[at][inner]
        dk_ref[...] = jnp.zeros(dk_ref.shape, F32)
        dv_ref[...] = jnp.zeros(dv_ref.shape, F32)

    for r in range(8):
        for m in range(4):
            left = block_scr[(chunk * 8 + r) * 8 + 2 * m].astype(F32)
            right = block_scr[(chunk * 8 + r) * 8 + 2 * m + 1].astype(F32)
            lanes = slice(m * 128, m * 128 + 128)
            bias_scr[r * 128 : r * 128 + 64, lanes] = join_low(left, right)
            bias_scr[r * 128 + 64 : r * 128 + 128, lanes] = join_high(left, right)
    mask = head_mask(4, 128, BF16)
    mask_f = head_mask(4, 128, F32)

    def spread(rows):
        return (rows.reshape(16, 1, 16, 128) * mask).reshape(1024, 128)

    def collect(rows):
        return jnp.sum(rows.reshape(16, 4, 16, 128) * mask_f, axis=1).reshape(256, 128)

    at = pl.ds(pl.multiple_of(chunk * 256, 256), 256)
    for row in range(4):
        q_big = spread(q_ref[row, at, :])
        a_big = spread(a_ref[row, at, :])
        keys = k_ref[row]
        values = v_ref[row]
        scores = dot(q_big, keys, NT) + bias_scr[...]
        top = jnp.max(scores, axis=-1, keepdims=True)
        powers = jnp.exp(scores - top)
        inverse = 1.0 / jnp.sum(powers, axis=-1, keepdims=True)
        powers_low = powers.astype(BF16)
        attended = dot(powers_low, values) * inverse
        att_ref[row, at, :] = collect(attended)
        a_float = a_big.astype(F32)
        inner = jnp.sum(a_float * attended, axis=-1, keepdims=True)
        grad_probs = dot(a_big, values, NT)
        score_grad = powers * ((grad_probs - inner) * inverse)
        score_low = score_grad.astype(BF16)
        dq_ref[row, at, :] = collect(dot(score_low, keys))
        dk_ref[row] += dot(q_big, score_low, TN)
        dv_ref[row] += dot((a_float * inverse).astype(BF16), powers_low, TN)
        if row == 0:
            sum_scr[...] = score_grad
        else:
            sum_scr[...] += score_grad

    xs = [slot_of(chunk + 2 * high - place_ref[0]) for high in range(2)]
    ys = [slot_of(b - place_ref[1]) * 4 for b in range(4)]
    zs = [slot_of(c - place_ref[2]) * 16 for c in range(4)]

    def emit(even_ref, odd_ref):
        for r in range(8):
            out_ref = odd_ref if r % 2 else even_ref
            for m in range(4):
                lanes = slice(m * 128, m * 128 + 128)
                low = sum_scr[r * 128 : r * 128 + 64, lanes]
                high = sum_scr[r * 128 + 64 : r * 128 + 128, lanes]
                spot = zs[r // 2] + ys[m]
                out_ref[spot + xs[0], 0:64] = join_low(low, high).astype(BF16)
                out_ref[spot + xs[1], 0:64] = join_high(low, high).astype(BF16)

    @pl.when(place_ref[3] == 0)
    def _():
        emit(mine_ref, other_ref)

    @pl.when(place_ref[3] == 1)
    def _():
        emit(other_ref, mine_ref)


def post_kernel(scale, place_ref, att_ref, dq_ref, dk_ref, dv_ref, gate_ref, gg_ref, n_ref, u_ref, rows_ref, wcat_ref,
                wout_ref, held_mine, held_other, ug_ref, mine_ref, other_ref, off_ref, w_scr, o_scr, s_scr, p_scr):
    row = pl.program_id(0)
    attended = att_ref[0]
    gate = gate_ref[0]
    grad_gated = gg_ref[0]
    gated = (gate * attended).astype(BF16)
    cot = rows_ref[:, 0, 0].reshape(512, 128)
    ug_ref[:, 0, 0] = dot(gated, wout_ref[...]).astype(BF16).reshape(8, 64, 128)
    out_part = dot(gated, cot, TN)
    gpre = (grad_gated * attended * gate * (1.0 - gate)).astype(BF16)
    qpre = (dq_ref[0] * scale).astype(BF16)
    kpre = (jnp.transpose(dk_ref[0]) * scale).astype(BF16)
    vpre = jnp.transpose(dv_ref[0]).astype(BF16)
    cat = jnp.concatenate([qpre, kpre, vpre, gpre], axis=1)
    grad_normed = dot(cat, wcat_ref[...], NT)
    ug_ref[:, 1, 0] = grad_normed.astype(BF16).reshape(8, 64, 128)
    w_part = dot(n_ref[0], cat, TN)
    off = jnp.sum(gpre.astype(F32), axis=0, keepdims=True)
    gain = jnp.sum(grad_normed * u_ref[0].astype(F32), axis=0, keepdims=True)
    off = jnp.concatenate([off, gain], axis=0)

    @pl.when(row == 0)
    def _():
        w_scr[...] = w_part
        o_scr[...] = out_part
        s_scr[...] = off

    @pl.when(row > 0)
    def _():
        w_scr[...] += w_part
        o_scr[...] += out_part
        s_scr[...] += off

    @pl.when(row == 3)
    def _():
        for t in range(5):
            part = w_scr[:, t * 128 : t * 128 + 128] if t < 4 else o_scr[...]
            high = part.astype(BF16).astype(F32)
            p_scr[:, t, :] = high
            p_scr[:, 8 + t, :] = part - high
        for t in range(5, 8):
            p_scr[:, t, :] = jnp.zeros((128, 128), F32)
            p_scr[:, 8 + t, :] = jnp.zeros((128, 128), F32)
        x, y, z, core = seen(place_ref, 1)
        for at in range(64):
            owner = z[at // 16] + y[at // 4 % 4] + x[at % 4]
            mine_ref[at] = p_scr[owner + core[0]].astype(BF16)
            other_ref[at] = p_scr[owner + core[1]].astype(BF16)
        off_ref[...] = s_scr[...]


def tile_sums_kernel(n_ref, u_ref, one_ref, two_ref, three_ref, four_ref, off_ref, wb_ref,
                     both_ref, msg_ref, rows_ref, bg_scr):
    rows_ref[...] = (one_ref[...].astype(F32) + two_ref[...].astype(F32)) + (
        three_ref[...].astype(F32) + four_ref[...].astype(F32)
    )
    bg_scr[...] = jnp.zeros(bg_scr.shape, F32)
    for half in range(8):
        for head in range(4):
            base = head * 16 + 2 * half
            left = rows_ref[base : base + 1, :]
            right = rows_ref[base + 1 : base + 2, :]
            bg_scr[head : head + 1, half * 128 : half * 128 + 128] = join_low(left, right)
            bg_scr[head : head + 1, (8 + half) * 128 : (8 + half) * 128 + 128] = join_high(left, right)
    bg = bg_scr[...]
    high = bg.astype(BF16).astype(F32)
    both = jnp.concatenate([high, bg - high], axis=0).astype(BF16)
    both_ref[...] = both
    bias_part = dot(both, n_ref[...])
    unit_part = dot(both, u_ref[...])
    gain_part = jnp.sum(unit_part * wb_ref[...].astype(F32), axis=0, keepdims=True) + off_ref[1:2]
    params = rows_ref[64:72, :] + rows_ref[72:80, :]
    row = lax.broadcasted_iota(jnp.int32, (8, 128), 0)
    params = jnp.where(row == 5, off_ref[0:1], jnp.where(row == 6, gain_part, params))
    small = bias_part[0:8] + bias_part[8:16]
    message = jnp.concatenate([params, small], axis=0).astype(BF16)
    msg_ref[...] = jnp.broadcast_to(message[None], msg_ref.shape)


def tile_final_kernel(pair_ref, ug_ref, both_ref, gain_ref, wb_ref, up_ref, gp_ref):
    up_ref[...] = ug_ref[:, 0].reshape(2048, 128)
    unit, inverse, normed = normalize(pair_ref[...].astype(F32), gain_ref[...])
    total = ug_ref[:, 1].reshape(2048, 128).astype(F32) + dot(both_ref[...], wb_ref[...], TN)
    scaled = total * gain_ref[...]
    first = jnp.mean(scaled, axis=-1, keepdims=True)
    second = jnp.mean(scaled * unit, axis=-1, keepdims=True)
    gp_ref[...] = ((scaled - first - unit * second) * inverse).astype(BF16)


def finish_kernel(msg_ref, q_ref, k_ref, v_ref, g_ref, o_ref, off_ref, gain_ref, bias_ref, msg_scr):
    messages = msg_ref[...].astype(F32)
    msg_scr[...] = messages
    for t, ref in enumerate((q_ref, k_ref, v_ref, g_ref, o_ref)):
        ref[...] = msg_scr[:, t, :]
    small = jnp.sum(messages, axis=0)
    off_ref[...] = small[5]
    gain_ref[...] = small[6]
    bias_ref[...] = small[8:12]


def estimate(microseconds):
    return pl.CostEstimate(
        flops=microseconds * 1_000_000_000, bytes_accessed=microseconds * 3_600_000, transcendentals=0
    )


def sds(shape, dtype):
    return jax.ShapeDtypeStruct(shape, dtype)


def whole(shape):
    return pl.BlockSpec(shape, lambda *_: (0,) * len(shape))


def body(pair_rep, cotangent, ln_gain, w_query, w_key, w_value, w_gate, gate_offset, w_bias, w_out):
    scale = 32 ** (-0.5)
    gain = ln_gain.reshape(1, 128)
    offset = gate_offset.reshape(1, 128)
    wcat = jnp.concatenate([w_query, w_key, w_value, w_gate], axis=1)
    wb_pad = jnp.pad(w_bias.T, ((0, 4), (0, 0)))
    wb_two = jnp.concatenate([wb_pad, wb_pad], axis=0)
    everyone = ("row", "col")
    pair_tile = pair_rep.reshape(2048, 128)

    def swap(value, axes):
        return lax.all_to_all(value, axes, split_axis=0, concat_axis=0, tiled=True)

    bias_msg, normed_tile, unit_tile = pl.pallas_call(
        tile_bias_kernel,
        out_shape=[sds((64, 128), BF16), sds((2048, 128), BF16), sds((2048, 128), BF16)],
        scratch_shapes=[pltpu.VMEM((64, 128), F32)],
        compiler_params=PARAMS,
        name="tile_bias",
    )(pair_tile, gain, wb_two)
    row, col = lax.axis_index("row"), lax.axis_index("col")
    place = ((col % 2) * 2 + row // 8, col // 2, (row // 2) % 4, row % 2)
    place = jnp.stack(place).astype(jnp.int32)
    smem = pl.BlockSpec(memory_space=pltpu.SMEM)
    packed = pl.pallas_call(
        pack_kernel,
        in_specs=[whole((8, 4, 64, 128))] * 2 + [pl.BlockSpec(memory_space=pl.ANY)],
        cost_estimate=estimate(2),
        out_shape=sds((8, 2, 4, 64, 128), BF16),
        compiler_params=PARAMS,
        name="pack",
    )(pair_rep.reshape(8, 4, 64, 128), cotangent.reshape(8, 4, 64, 128), bias_msg)
    both_rows = swap(packed, "col")
    bias_pieces = gather_bias(bias_msg)

    from_rows = pl.BlockSpec((8, 2, 1, 64, 128), lambda i: (0, 0, i, 0, 0))
    from_cot = pl.BlockSpec((8, 1, 1, 64, 128), lambda i: (0, 1, i, 0, 0))
    by_row = pl.BlockSpec((1, 512, 128), lambda i: (i, 0, 0))
    query, keys, values, grad_att, gate, grad_gated, normed, unit = pl.pallas_call(
        functools.partial(project_kernel, scale),
        grid=(4,),
        in_specs=[from_rows, whole((1, 128)), whole((128, 512)), whole((1, 128)), whole((128, 128))],
        out_specs=[by_row] * 8,
        out_shape=[sds((4, 512, 128), t) for t in (BF16, BF16, BF16, BF16, F32, F32, BF16, BF16)],
        compiler_params=PARAMS,
        cost_estimate=estimate(5),
        name="project",
    )(both_rows, gain, wcat, offset, w_out)

    full = whole((4, 512, 128))
    full_t = whole((4, 128, 512))
    attended, dq, dk, dv, mine, other = pl.pallas_call(
        attend_kernel,
        grid=(2,),
        in_specs=[smem, full, full, full, full] + [whole((16, 64, 128))] * 8,
        out_specs=[full, full, full_t, full_t, whole((64, 80, 128)), whole((64, 80, 128))],
        out_shape=[sds((4, 512, 128), F32), sds((4, 512, 128), F32), sds((4, 128, 512), F32),
                   sds((4, 128, 512), F32), sds((64, 80, 128), BF16), sds((64, 80, 128), BF16)],
        scratch_shapes=[pltpu.VMEM((128, 64, 128), BF16), pltpu.VMEM((1024, 512), F32), pltpu.VMEM((1024, 512), F32)],
        compiler_params=PARAMS,
        name="attend",
    )(place, query, keys, values, grad_att, *bias_pieces)

    by_row_t = pl.BlockSpec((1, 128, 512), lambda i: (i, 0, 0))
    tail = pl.BlockSpec((64, 16, 128), lambda i: (0, 4, 0))
    ug_rows, mine, other, off = pl.pallas_call(
        functools.partial(post_kernel, scale),
        grid=(4,),
        in_specs=[smem, by_row, by_row, by_row_t, by_row_t, by_row, by_row, by_row, by_row, from_cot,
                  whole((128, 512)), whole((128, 128))] + [pl.BlockSpec(memory_space=pl.ANY)] * 2,
        out_specs=[from_rows, tail, tail, whole((2, 128))],
        out_shape=[sds((8, 2, 4, 64, 128), BF16), sds((64, 80, 128), BF16), sds((64, 80, 128), BF16),
                   sds((2, 128), F32)],
        scratch_shapes=[pltpu.VMEM((128, 512), F32), pltpu.VMEM((128, 128), F32), pltpu.VMEM((2, 128), F32),
                        pltpu.VMEM((128, 16, 128), F32)],
        input_output_aliases={12: 1, 13: 2},
        compiler_params=PARAMS,
        name="post",
    )(place, attended, dq, dk, dv, gate, grad_gated, normed, unit, both_rows, wcat, w_out, mine, other)
    ug_tile = swap(ug_rows, "col")
    sums = scatter_sums(mine, other)
    both, final_msg = pl.pallas_call(
        tile_sums_kernel,
        out_shape=[sds((16, 2048), BF16), sds((128, 16, 128), BF16)],
        scratch_shapes=[pltpu.VMEM((80, 128), F32), pltpu.VMEM((8, 2048), F32)],
        compiler_params=PARAMS,
        name="tile_sums",
    )(normed_tile, unit_tile, *sums, off, wb_two)
    final_in = swap(final_msg, everyone)
    update, grad_pair = pl.pallas_call(
        tile_final_kernel,
        out_shape=[sds((2048, 128), BF16), sds((2048, 128), BF16)],
        compiler_params=PARAMS,
        cost_estimate=estimate(5),
        name="tile_final",
    )(pair_tile, ug_tile.reshape(8, 2, 256, 128), both, gain, wb_two)
    g_query, g_key, g_value, g_gate, g_out, g_off, g_gain, g_bias = pl.pallas_call(
        finish_kernel,
        out_shape=[sds((128, 128), F32)] * 5 + [sds((128,), F32)] * 2 + [sds((4, 128), F32)],
        scratch_shapes=[pltpu.VMEM((128, 16, 128), F32)],
        compiler_params=PARAMS,
        name="finish",
    )(final_in)
    return (
        update.reshape(32, 64, 128),
        grad_pair.reshape(32, 64, 128),
        g_gain,
        g_query,
        g_key,
        g_value,
        g_gate,
        g_off,
        g_bias.T,
        g_out,
    )


def solution(mesh):
    tile = P("row", "col", None)
    return jax.shard_map(
        body,
        mesh=mesh,
        in_specs=(tile, tile) + (P(),) * 8,
        out_specs=(tile, tile) + (P(),) * 8,
        check_vma=False,
    )
```

```python
import functools

import jax
import jax.numpy as jnp
from jax import lax
from jax.experimental import pallas as pl
from jax.experimental.pallas import tpu as pltpu
from jax.sharding import PartitionSpec as P

EPS = 1e-05
F32 = jnp.float32
BF16 = jnp.bfloat16
NT = (((1,), (1,)), ((), ()))
TN = (((0,), (0,)), ((), ()))
HOPS = (0, 1, 3, 2)
PARAMS = pltpu.CompilerParams(vmem_limit_bytes=56 * 1024 * 1024)


def dot(left, right, dims=(((1,), (0,)), ((), ()))):
    return lax.dot_general(left, right, dims, preferred_element_type=F32)


def normalize(values, gain):
    average = jnp.mean(values, axis=-1, keepdims=True)
    centered = values - average
    variance = jnp.mean(centered * centered, axis=-1, keepdims=True)
    inverse = lax.rsqrt(variance + EPS)
    unit = centered * inverse
    return unit, inverse, (unit * gain).astype(BF16)


def low_lanes(shape):
    return lax.broadcasted_iota(jnp.int32, shape, len(shape) - 1) < 64


def join_low(left, right):
    return jnp.where(low_lanes(left.shape), left, pltpu.roll(right, 64, left.ndim - 1))


def join_high(left, right):
    return jnp.where(low_lanes(left.shape), pltpu.roll(left, 64, left.ndim - 1), right)


def head_mask(heads, channels, dtype):
    lane = lax.broadcasted_iota(jnp.int32, (1, heads, 1, channels), 3)
    head = lax.broadcasted_iota(jnp.int32, (1, heads, 1, channels), 1)
    return jnp.where(lane // (channels // heads) == head, 1.0, 0.0).astype(dtype)


def flat_index(x, y, z, core):
    return (((x % 2) * 4 + z) * 2 + core) * 8 + y * 2 + x // 2


def shift_pairs(x=0, y=0, z=0, core=0):
    pairs = []
    for a in range(4):
        for b in range(4):
            for c in range(4):
                for d in range(2):
                    target = flat_index((a + x) % 4, (b + y) % 4, (c + z) % 4, (d + core) % 2)
                    pairs.append((flat_index(a, b, c, d), target))
    return sorted(pairs)


def seen(place_ref, sign):
    x, y, z = ([(place_ref[at] + 4 + sign * hop) & 3 for hop in HOPS] for at in range(3))
    core = [place_ref[3], 1 - place_ref[3]]
    return (
        [(a & 1) * 64 + (a >> 1) for a in x],
        [b * 2 for b in y],
        [c * 16 for c in z],
        [d * 8 for d in core],
    )


def slot_of(delta):
    delta = (delta + 4) & 3
    return jnp.where(delta < 2, delta, 5 - delta)


def send(value, **shift):
    return lax.ppermute(value, ("row", "col"), shift_pairs(**shift))


def gate_kernel(*refs):
    pass


def after(values, other):
    anywhere = pl.BlockSpec(memory_space=pl.ANY)
    return pl.pallas_call(
        gate_kernel,
        in_specs=[anywhere] * (len(values) + 1),
        out_specs=[anywhere] * len(values),
        out_shape=[jax.ShapeDtypeStruct(value.shape, value.dtype) for value in values],
        input_output_aliases={at: at for at in range(len(values))},
        name="after",
    )(*values, other)


def gather_in_plane(first):
    held = jnp.stack(first)
    held = jnp.stack([held] + [send(held, y=hop) for hop in HOPS[1:]])
    held = held.reshape(16, 64, 128)
    return [held] + [send(held, x=hop) for hop in HOPS[1:]]


def add_up(parts):
    return sum(part.astype(F32) for part in parts).astype(BF16)


def scatter_sums(mine, other):
    got = send(other, core=1)
    held = [add_up([mine[at * 16 : at * 16 + 16], got[at * 16 : at * 16 + 16]]) for at in range(4)]
    got = [held[0]] + [send(held[at], z=HOPS[at]) for at in (1, 2, 3)]
    held = [add_up([part[at * 4 : at * 4 + 4] for part in got]) for at in range(4)]
    got = [held[0]] + [send(held[at], y=HOPS[at]) for at in (1, 2, 3)]
    held = [add_up([part[at] for part in got]) for at in range(4)]
    return [held[0]] + [send(held[at], x=HOPS[at]) for at in (1, 2, 3)]


def tile_bias_kernel(pair_ref, gain_ref, w_ref, msg_ref, n_ref, u_ref, wb_ref, rows_ref, w_scr):
    w_scr[...] = jnp.zeros(w_scr.shape, F32)
    w_scr[0:4, :] = w_ref[...].astype(F32)
    w_scr[8:12, :] = w_ref[...].astype(F32)
    wb_ref[...] = w_scr[...].astype(BF16)
    unit, inverse, normed = normalize(pair_ref[...].astype(F32), gain_ref[...])
    n_ref[...] = normed
    u_ref[...] = unit.astype(BF16)
    bias = dot(w_scr[...].astype(BF16), normed, NT)
    for half in range(8):
        first = bias[0:8, half * 128 : half * 128 + 128]
        second = bias[0:8, (8 + half) * 128 : (8 + half) * 128 + 128]
        even = join_low(first, second)
        odd = join_high(first, second)
        for head in range(4):
            base = head * 16 + 2 * half
            rows_ref[base : base + 1, :] = even[head : head + 1]
            rows_ref[base + 1 : base + 2, :] = odd[head : head + 1]
    msg_ref[...] = rows_ref[...].astype(BF16)


def pack_kernel(pair_ref, cot_ref, out_ref):
    out_ref[:, 0] = pair_ref[...]
    out_ref[:, 1] = cot_ref[...]


def project_kernel(scale, rows_ref, gain_ref, wcat_ref, off_ref, wout_ref,
                   q_ref, k_ref, v_ref, a_ref, gate_ref, gg_ref, n_ref, u_ref):
    values = rows_ref[:, 0, 0].reshape(512, 128).astype(F32)
    unit, inverse, normed = normalize(values, gain_ref[...])
    projected = dot(normed, wcat_ref[...])
    gate = jax.nn.sigmoid(projected[:, 384:512] + off_ref[...])
    grad_gated = dot(rows_ref[:, 1, 0].reshape(512, 128), wout_ref[...], NT)
    q_ref[0] = (projected[:, 0:128] * scale).astype(BF16)
    k_ref[0] = (projected[:, 128:256] * scale).astype(BF16)
    v_ref[0] = projected[:, 256:384].astype(BF16)
    a_ref[0] = (grad_gated * gate).astype(BF16)
    gate_ref[0] = gate
    gg_ref[0] = grad_gated
    n_ref[0] = normed
    u_ref[0] = unit.astype(BF16)


def attend_kernel(scale, place_ref, q_ref, k_ref, v_ref, a_ref, *refs):
    pieces = refs[:8]
    att_ref, dq_ref, dk_out, dv_out, mine_ref, other_ref, block_scr, bias_scr, sum_scr, dk_ref, dv_ref = refs[8:]
    chunk = pl.program_id(0)

    @pl.when(chunk == 0)
    def _():
        x, y, z, core = seen(place_ref, -1)
        for at in range(8):
            for inner in range(16):
                owner = x[at % 4] + y[inner // 4] + z[inner % 4] + core[at // 4]
                block_scr[owner] = pieces[at][inner]
        dk_ref[...] = jnp.zeros(dk_ref.shape, F32)
        dv_ref[...] = jnp.zeros(dv_ref.shape, F32)

    for r in range(8):
        for m in range(4):
            left = block_scr[(chunk * 8 + r) * 8 + 2 * m].astype(F32)
            right = block_scr[(chunk * 8 + r) * 8 + 2 * m + 1].astype(F32)
            lanes = slice(m * 128, m * 128 + 128)
            bias_scr[r * 128 : r * 128 + 64, lanes] = join_low(left, right)
            bias_scr[r * 128 + 64 : r * 128 + 128, lanes] = join_high(left, right)
    mask = head_mask(4, 128, BF16)
    mask_f = head_mask(4, 128, F32)

    def spread(rows):
        return (rows.reshape(16, 1, 16, 128) * mask).reshape(1024, 128)

    def collect(rows):
        return jnp.sum(rows.reshape(16, 4, 16, 128) * mask_f, axis=1).reshape(256, 128)

    at = pl.ds(pl.multiple_of(chunk * 256, 256), 256)
    for row in range(4):
        q_big = spread(q_ref[row, at, :])
        a_big = spread(a_ref[row, at, :])
        keys = k_ref[row]
        values = v_ref[row]
        scores = dot(q_big, keys, NT) + bias_scr[...]
        top = jnp.max(scores, axis=-1, keepdims=True)
        powers = jnp.exp(scores - top)
        inverse = 1.0 / jnp.sum(powers, axis=-1, keepdims=True)
        powers_low = powers.astype(BF16)
        attended = dot(powers_low, values) * inverse
        att_ref[row] = collect(attended).astype(BF16)
        a_float = a_big.astype(F32)
        inner = jnp.sum(a_float * attended, axis=-1, keepdims=True)
        grad_probs = dot(a_big, values, NT)
        score_grad = powers * ((grad_probs - inner) * inverse)
        score_low = score_grad.astype(BF16)
        dq_ref[row] = (collect(dot(score_low, keys)) * scale).astype(BF16)
        dk_ref[row] += dot(q_big, score_low, TN)
        dv_ref[row] += dot((a_float * inverse).astype(BF16), powers_low, TN)
        if row == 0:
            sum_scr[...] = score_grad
        else:
            sum_scr[...] += score_grad

    @pl.when(chunk == 1)
    def _():
        dk_out[...] = (dk_ref[...] * scale).astype(BF16)
        dv_out[...] = dv_ref[...].astype(BF16)

    xs = [slot_of(chunk + 2 * high - place_ref[0]) for high in range(2)]
    ys = [slot_of(b - place_ref[1]) * 4 for b in range(4)]
    zs = [slot_of(c - place_ref[2]) * 16 for c in range(4)]

    def emit(even_ref, odd_ref):
        for r in range(8):
            out_ref = odd_ref if r % 2 else even_ref
            for m in range(4):
                lanes = slice(m * 128, m * 128 + 128)
                low = sum_scr[r * 128 : r * 128 + 64, lanes]
                high = sum_scr[r * 128 + 64 : r * 128 + 128, lanes]
                spot = zs[r // 2] + ys[m]
                out_ref[spot + xs[0], 0:64] = join_low(low, high).astype(BF16)
                out_ref[spot + xs[1], 0:64] = join_high(low, high).astype(BF16)

    @pl.when(place_ref[3] == 0)
    def _():
        emit(mine_ref, other_ref)

    @pl.when(place_ref[3] == 1)
    def _():
        emit(other_ref, mine_ref)


def post_kernel(place_ref, att_ref, dq_ref, dk_ref, dv_ref, gate_ref, gg_ref, n_ref, u_ref, rows_ref, wcat_ref,
                wout_ref, held_mine, held_other, ug_ref, mine_ref, other_ref, off_ref, w_scr, o_scr, s_scr, p_scr):
    row = pl.program_id(0)
    attended = att_ref[...].reshape(1024, 128).astype(F32)
    gate = gate_ref[...].reshape(1024, 128)
    grad_gated = gg_ref[...].reshape(1024, 128)
    gated = (gate * attended).astype(BF16)
    cot = jnp.concatenate([rows_ref[:, 0, at].reshape(512, 128) for at in range(2)], axis=0)
    update = dot(gated, wout_ref[...]).astype(BF16).reshape(2, 8, 64, 128)
    out_part = dot(gated, cot, TN)
    gpre = (grad_gated * attended * gate * (1.0 - gate)).astype(BF16)
    qpre = dq_ref[...].reshape(1024, 128)
    kpre, vpre = (
        jnp.concatenate([jnp.transpose(ref[at].astype(F32)) for at in range(2)], axis=0).astype(BF16)
        for ref in (dk_ref, dv_ref)
    )
    cat = jnp.concatenate([qpre, kpre, vpre, gpre], axis=1)
    grad_normed = dot(cat, wcat_ref[...], NT)
    grad_low = grad_normed.astype(BF16).reshape(2, 8, 64, 128)
    for at in range(2):
        ug_ref[:, 0, at] = update[at]
        ug_ref[:, 1, at] = grad_low[at]
    w_part = dot(n_ref[...].reshape(1024, 128), cat, TN)
    off = jnp.sum(gpre.astype(F32), axis=0, keepdims=True)
    gain = jnp.sum(grad_normed * u_ref[...].reshape(1024, 128).astype(F32), axis=0, keepdims=True)
    off = jnp.concatenate([off, gain], axis=0)

    @pl.when(row == 0)
    def _():
        w_scr[...] = w_part
        o_scr[...] = out_part
        s_scr[...] = off

    @pl.when(row > 0)
    def _():
        w_scr[...] += w_part
        o_scr[...] += out_part
        s_scr[...] += off

    @pl.when(row == 1)
    def _():
        for t in range(5):
            part = w_scr[:, t * 128 : t * 128 + 128] if t < 4 else o_scr[...]
            high = part.astype(BF16).astype(F32)
            p_scr[:, t, :] = high
            p_scr[:, 8 + t, :] = part - high
        for t in range(5, 8):
            p_scr[:, t, :] = jnp.zeros((128, 128), F32)
            p_scr[:, 8 + t, :] = jnp.zeros((128, 128), F32)
        x, y, z, core = seen(place_ref, 1)
        for at in range(64):
            owner = z[at // 16] + y[at // 4 % 4] + x[at % 4]
            mine_ref[at] = p_scr[owner + core[0]].astype(BF16)
            other_ref[at] = p_scr[owner + core[1]].astype(BF16)
        off_ref[...] = s_scr[...]


def tile_sums_kernel(n_ref, u_ref, one_ref, two_ref, three_ref, four_ref, off_ref, wb_ref,
                     both_ref, msg_ref, rows_ref, bg_scr):
    rows_ref[...] = (one_ref[...].astype(F32) + two_ref[...].astype(F32)) + (
        three_ref[...].astype(F32) + four_ref[...].astype(F32)
    )
    bg_scr[...] = jnp.zeros(bg_scr.shape, F32)
    for half in range(8):
        for head in range(4):
            base = head * 16 + 2 * half
            left = rows_ref[base : base + 1, :]
            right = rows_ref[base + 1 : base + 2, :]
            bg_scr[head : head + 1, half * 128 : half * 128 + 128] = join_low(left, right)
            bg_scr[head : head + 1, (8 + half) * 128 : (8 + half) * 128 + 128] = join_high(left, right)
    bg = bg_scr[...]
    high = bg.astype(BF16).astype(F32)
    both = jnp.concatenate([high, bg - high], axis=0).astype(BF16)
    both_ref[...] = both
    bias_part = dot(both, n_ref[...])
    unit_part = dot(both, u_ref[...])
    gain_part = jnp.sum(unit_part * wb_ref[...].astype(F32), axis=0, keepdims=True) + off_ref[1:2]
    params = rows_ref[64:72, :] + rows_ref[72:80, :]
    row = lax.broadcasted_iota(jnp.int32, (8, 128), 0)
    params = jnp.where(row == 5, off_ref[0:1], jnp.where(row == 6, gain_part, params))
    small = bias_part[0:8] + bias_part[8:16]
    message = jnp.concatenate([params, small], axis=0).astype(BF16)
    msg_ref[...] = jnp.broadcast_to(message[None], msg_ref.shape)


def tile_final_kernel(pair_ref, ug_ref, both_ref, gain_ref, wb_ref, up_ref, gp_ref):
    up_ref[...] = ug_ref[:, 0].reshape(2048, 128)
    unit, inverse, normed = normalize(pair_ref[...].astype(F32), gain_ref[...])
    total = ug_ref[:, 1].reshape(2048, 128).astype(F32) + dot(both_ref[...], wb_ref[...], TN)
    scaled = total * gain_ref[...]
    first = jnp.mean(scaled, axis=-1, keepdims=True)
    second = jnp.mean(scaled * unit, axis=-1, keepdims=True)
    gp_ref[...] = ((scaled - first - unit * second) * inverse).astype(BF16)


def finish_kernel(msg_ref, q_ref, k_ref, v_ref, g_ref, o_ref, off_ref, gain_ref, bias_ref, msg_scr):
    messages = msg_ref[...].astype(F32)
    msg_scr[...] = messages
    for t, ref in enumerate((q_ref, k_ref, v_ref, g_ref, o_ref)):
        ref[...] = msg_scr[:, t, :]
    small = jnp.sum(messages, axis=0)
    off_ref[...] = small[5]
    gain_ref[...] = small[6]
    bias_ref[...] = small[8:12]


def estimate(microseconds):
    return pl.CostEstimate(
        flops=microseconds * 1_000_000_000, bytes_accessed=microseconds * 3_600_000, transcendentals=0
    )


def sds(shape, dtype):
    return jax.ShapeDtypeStruct(shape, dtype)


def whole(shape):
    return pl.BlockSpec(shape, lambda *_: (0,) * len(shape))


def body(pair_rep, cotangent, ln_gain, w_query, w_key, w_value, w_gate, gate_offset, w_bias, w_out):
    scale = 32 ** (-0.5)
    gain = ln_gain.reshape(1, 128)
    offset = gate_offset.reshape(1, 128)
    wcat = jnp.concatenate([w_query, w_key, w_value, w_gate], axis=1)
    everyone = ("row", "col")
    pair_tile = pair_rep.reshape(2048, 128)

    def swap(value, axes):
        return lax.all_to_all(value, axes, split_axis=0, concat_axis=0, tiled=True)

    bias_msg, normed_tile, unit_tile, wb_two = pl.pallas_call(
        tile_bias_kernel,
        out_shape=[sds((64, 128), BF16), sds((2048, 128), BF16), sds((2048, 128), BF16), sds((16, 128), BF16)],
        scratch_shapes=[pltpu.VMEM((64, 128), F32), pltpu.VMEM((16, 128), F32)],
        compiler_params=PARAMS,
        name="tile_bias",
    )(pair_tile, gain, w_bias.T)
    row, col = lax.axis_index("row"), lax.axis_index("col")
    place = ((col % 2) * 2 + row // 8, col // 2, (row // 2) % 4, row % 2)
    place = jnp.stack(place).astype(jnp.int32)
    smem = pl.BlockSpec(memory_space=pltpu.SMEM)
    packed = pl.pallas_call(
        pack_kernel,
        cost_estimate=estimate(2),
        out_shape=sds((8, 2, 4, 64, 128), BF16),
        compiler_params=PARAMS,
        name="pack",
    )(pair_rep.reshape(8, 4, 64, 128), cotangent.reshape(8, 4, 64, 128))
    first = [bias_msg] + [send(bias_msg, z=hop) for hop in HOPS[1:]]
    both_rows = swap(packed, "col")
    bias_pieces = gather_in_plane(first)

    from_rows = pl.BlockSpec((8, 2, 1, 64, 128), lambda i: (0, 0, i, 0, 0))
    by_row = pl.BlockSpec((1, 512, 128), lambda i: (i, 0, 0))
    query, keys, values, grad_att, gate, grad_gated, normed, unit = pl.pallas_call(
        functools.partial(project_kernel, scale),
        grid=(4,),
        in_specs=[from_rows, whole((1, 128)), whole((128, 512)), whole((1, 128)), whole((128, 128))],
        out_specs=[by_row] * 8,
        out_shape=[sds((4, 512, 128), t) for t in (BF16, BF16, BF16, BF16, F32, F32, BF16, BF16)],
        compiler_params=PARAMS,
        cost_estimate=estimate(5),
        name="project",
    )(both_rows, gain, wcat, offset, w_out)

    bias_pieces = bias_pieces[:1] + list(after(bias_pieces[1:], query))
    bias_pieces = bias_pieces + [send(piece, core=1) for piece in bias_pieces]

    full = whole((4, 512, 128))
    half = pl.BlockSpec((4, 256, 128), lambda c: (0, c, 0))
    full_t = whole((4, 128, 512))
    attended, dq, dk, dv, mine, other = pl.pallas_call(
        functools.partial(attend_kernel, scale),
        grid=(2,),
        in_specs=[smem, full, full, full, full] + [whole((16, 64, 128))] * 8,
        out_specs=[half, half, full_t, full_t, whole((64, 80, 128)), whole((64, 80, 128))],
        out_shape=[sds((4, 512, 128), BF16), sds((4, 512, 128), BF16), sds((4, 128, 512), BF16),
                   sds((4, 128, 512), BF16), sds((64, 80, 128), BF16), sds((64, 80, 128), BF16)],
        scratch_shapes=[pltpu.VMEM((128, 64, 128), BF16), pltpu.VMEM((1024, 512), F32), pltpu.VMEM((1024, 512), F32),
                        pltpu.VMEM((4, 128, 512), F32), pltpu.VMEM((4, 128, 512), F32)],
        compiler_params=PARAMS,
        name="attend",
    )(place, query, keys, values, grad_att, *bias_pieces)

    two_t = pl.BlockSpec((2, 128, 512), lambda i: (i, 0, 0))
    two = pl.BlockSpec((2, 512, 128), lambda i: (i, 0, 0))
    two_rows = pl.BlockSpec((8, 2, 2, 64, 128), lambda i: (0, 0, i, 0, 0))
    two_cot = pl.BlockSpec((8, 1, 2, 64, 128), lambda i: (0, 1, i, 0, 0))
    tail = pl.BlockSpec((64, 16, 128), lambda i: (0, 4, 0))
    ug_rows, mine, other, off = pl.pallas_call(
        post_kernel,
        grid=(2,),
        in_specs=[smem, two, two, two_t, two_t, two, two, two, two, two_cot,
                  whole((128, 512)), whole((128, 128))] + [pl.BlockSpec(memory_space=pl.ANY)] * 2,
        out_specs=[two_rows, tail, tail, whole((2, 128))],
        out_shape=[sds((8, 2, 4, 64, 128), BF16), sds((64, 80, 128), BF16), sds((64, 80, 128), BF16),
                   sds((2, 128), F32)],
        scratch_shapes=[pltpu.VMEM((128, 512), F32), pltpu.VMEM((128, 128), F32), pltpu.VMEM((2, 128), F32),
                        pltpu.VMEM((128, 16, 128), F32)],
        input_output_aliases={12: 1, 13: 2},
        compiler_params=PARAMS,
        name="post",
    )(place, attended, dq, dk, dv, gate, grad_gated, normed, unit, both_rows, wcat, w_out, mine, other)
    ug_tile = swap(ug_rows, "col")
    sums = scatter_sums(mine, other)
    both, final_msg = pl.pallas_call(
        tile_sums_kernel,
        out_shape=[sds((16, 2048), BF16), sds((128, 16, 128), BF16)],
        scratch_shapes=[pltpu.VMEM((80, 128), F32), pltpu.VMEM((8, 2048), F32)],
        compiler_params=PARAMS,
        name="tile_sums",
    )(normed_tile, unit_tile, *sums, off, wb_two)
    final_in = swap(final_msg, everyone)
    update, grad_pair = pl.pallas_call(
        tile_final_kernel,
        out_shape=[sds((2048, 128), BF16), sds((2048, 128), BF16)],
        compiler_params=PARAMS,
        cost_estimate=estimate(5),
        name="tile_final",
    )(pair_tile, ug_tile.reshape(8, 2, 256, 128), both, gain, wb_two)
    g_query, g_key, g_value, g_gate, g_out, g_off, g_gain, g_bias = pl.pallas_call(
        finish_kernel,
        out_shape=[sds((128, 128), F32)] * 5 + [sds((128,), F32)] * 2 + [sds((4, 128), F32)],
        scratch_shapes=[pltpu.VMEM((128, 16, 128), F32)],
        compiler_params=PARAMS,
        name="finish",
    )(final_in)
    return (
        update.reshape(32, 64, 128),
        grad_pair.reshape(32, 64, 128),
        g_gain,
        g_query,
        g_key,
        g_value,
        g_gate,
        g_off,
        g_bias.T,
        g_out,
    )


def solution(mesh):
    tile = P("row", "col", None)
    return jax.shard_map(
        body,
        mesh=mesh,
        in_specs=(tile, tile) + (P(),) * 8,
        out_specs=(tile, tile) + (P(),) * 8,
        check_vma=False,
    )
```

```python
import functools

import jax
import jax.numpy as jnp
from jax import lax
from jax.experimental import pallas as pl
from jax.experimental.pallas import tpu as pltpu
from jax.sharding import PartitionSpec as P

EPS = 1e-05
F32 = jnp.float32
BF16 = jnp.bfloat16
NT = (((1,), (1,)), ((), ()))
TN = (((0,), (0,)), ((), ()))
HOPS = (0, 1, 3, 2)


def grant(mebibytes):
    return pltpu.CompilerParams(vmem_limit_bytes=mebibytes * 1024 * 1024)


def dot(left, right, dims=(((1,), (0,)), ((), ()))):
    return lax.dot_general(left, right, dims, preferred_element_type=F32)


def normalize(values, gain):
    average = jnp.mean(values, axis=-1, keepdims=True)
    centered = values - average
    variance = jnp.mean(centered * centered, axis=-1, keepdims=True)
    inverse = lax.rsqrt(variance + EPS)
    unit = centered * inverse
    return unit, inverse, (unit * gain).astype(BF16)


def low_lanes(shape):
    return lax.broadcasted_iota(jnp.int32, shape, len(shape) - 1) < 64


def join_low(left, right):
    return jnp.where(low_lanes(left.shape), left, pltpu.roll(right, 64, left.ndim - 1))


def join_high(left, right):
    return jnp.where(low_lanes(left.shape), pltpu.roll(left, 64, left.ndim - 1), right)


def head_mask(heads, channels, dtype):
    lane = lax.broadcasted_iota(jnp.int32, (1, heads, 1, channels), 3)
    head = lax.broadcasted_iota(jnp.int32, (1, heads, 1, channels), 1)
    return jnp.where(lane // (channels // heads) == head, 1.0, 0.0).astype(dtype)


def flat_index(x, y, z, core):
    return (((x % 2) * 4 + z) * 2 + core) * 8 + y * 2 + x // 2


def shift_pairs(x=0, y=0, z=0, core=0):
    pairs = []
    for a in range(4):
        for b in range(4):
            for c in range(4):
                for d in range(2):
                    target = flat_index((a + x) % 4, (b + y) % 4, (c + z) % 4, (d + core) % 2)
                    pairs.append((flat_index(a, b, c, d), target))
    return sorted(pairs)


def seen(place_ref, sign):
    x, y, z = ([(place_ref[at] + 4 + sign * hop) & 3 for hop in HOPS] for at in range(3))
    core = [place_ref[3], 1 - place_ref[3]]
    return (
        [(a & 1) * 64 + (a >> 1) for a in x],
        [b * 2 for b in y],
        [c * 16 for c in z],
        [d * 8 for d in core],
    )


def slot_of(delta):
    delta = (delta + 4) & 3
    return jnp.where(delta < 2, delta, 5 - delta)


def send(value, **shift):
    return lax.ppermute(value, ("row", "col"), shift_pairs(**shift))


def gate_kernel(*refs):
    pass


def after(values, other):
    anywhere = pl.BlockSpec(memory_space=pl.ANY)
    return pl.pallas_call(
        gate_kernel,
        in_specs=[anywhere] * (len(values) + 1),
        out_specs=[anywhere] * len(values),
        out_shape=[jax.ShapeDtypeStruct(value.shape, value.dtype) for value in values],
        input_output_aliases={at: at for at in range(len(values))},
        compiler_params=grant(1),
        name="after",
    )(*values, other)


def gather_in_plane(first):
    held = jnp.stack(first)
    held = jnp.stack([held] + [send(held, y=hop) for hop in HOPS[1:]])
    held = held.reshape(16, 64, 128)
    return [held] + [send(held, x=hop) for hop in HOPS[1:]]


def add_up(parts):
    return sum(part.astype(F32) for part in parts).astype(BF16)


def scatter_sums(mine, other):
    got = send(other, core=1)
    held = [add_up([mine[at * 16 : at * 16 + 16], got[at * 16 : at * 16 + 16]]) for at in range(4)]
    got = [held[0]] + [send(held[at], z=HOPS[at]) for at in (1, 2, 3)]
    held = [add_up([part[at * 4 : at * 4 + 4] for part in got]) for at in range(4)]
    got = [held[0]] + [send(held[at], y=HOPS[at]) for at in (1, 2, 3)]
    held = [add_up([part[at] for part in got]) for at in range(4)]
    return [held[0]] + [send(held[at], x=HOPS[at]) for at in (1, 2, 3)]


def tile_bias_kernel(pair_ref, gain_ref, w_ref, msg_ref, n_ref, u_ref, wb_ref, rows_ref, w_scr):
    w_scr[...] = jnp.zeros(w_scr.shape, F32)
    w_scr[0:4, :] = w_ref[...].astype(F32)
    w_scr[8:12, :] = w_ref[...].astype(F32)
    wb_ref[...] = w_scr[...].astype(BF16)
    unit, inverse, normed = normalize(pair_ref[...].astype(F32), gain_ref[...])
    n_ref[...] = normed
    u_ref[...] = unit.astype(BF16)
    bias = dot(w_scr[...].astype(BF16), normed, NT)
    for half in range(8):
        first = bias[0:8, half * 128 : half * 128 + 128]
        second = bias[0:8, (8 + half) * 128 : (8 + half) * 128 + 128]
        even = join_low(first, second)
        odd = join_high(first, second)
        for head in range(4):
            base = head * 16 + 2 * half
            rows_ref[base : base + 1, :] = even[head : head + 1]
            rows_ref[base + 1 : base + 2, :] = odd[head : head + 1]
    msg_ref[...] = rows_ref[...].astype(BF16)


def pack_kernel(pair_ref, cot_ref, out_ref):
    out_ref[:, 0] = pair_ref[...]
    out_ref[:, 1] = cot_ref[...]


def project_kernel(scale, place_ref, rows_ref, gain_ref, wcat_ref, off_ref, wout_ref,
                   q_ref, k_ref, v_ref, a_ref, gate_ref, gg_ref, n_ref, u_ref):
    values = rows_ref[:, 0, 0].reshape(512, 128).astype(F32)
    unit, inverse, normed = normalize(values, gain_ref[...])
    projected = dot(normed, wcat_ref[...])
    gate = jax.nn.sigmoid(projected[:, 384:512] + off_ref[...])
    grad_gated = dot(rows_ref[:, 1, 0].reshape(512, 128), wout_ref[...], NT)
    q_ref[0] = (projected[:, 0:128] * scale).astype(BF16)
    k_ref[0] = (projected[:, 128:256] * scale).astype(BF16)
    v_ref[0] = projected[:, 256:384].astype(BF16)
    a_ref[0] = (grad_gated * gate).astype(BF16)
    gate_ref[0] = gate
    gg_ref[0] = grad_gated
    n_ref[0] = normed
    u_ref[0] = unit.astype(BF16)


def attend_kernel(scale, place_ref, q_ref, k_ref, v_ref, a_ref, *refs):
    pieces = refs[:8]
    att_ref, dq_ref, dk_out, dv_out, mine_ref, other_ref, block_scr, bias_scr, sum_scr, dk_ref, dv_ref = refs[8:]
    chunk = pl.program_id(0)

    @pl.when(chunk == 0)
    def _():
        x, y, z, core = seen(place_ref, -1)
        for at in range(8):
            for inner in range(16):
                owner = x[at % 4] + y[inner // 4] + z[inner % 4] + core[at // 4]
                block_scr[owner] = pieces[at][inner]
        dk_ref[...] = jnp.zeros(dk_ref.shape, F32)
        dv_ref[...] = jnp.zeros(dv_ref.shape, F32)

    for r in range(8):
        for m in range(4):
            left = block_scr[(chunk * 8 + r) * 8 + 2 * m].astype(F32)
            right = block_scr[(chunk * 8 + r) * 8 + 2 * m + 1].astype(F32)
            lanes = slice(m * 128, m * 128 + 128)
            bias_scr[r * 128 : r * 128 + 64, lanes] = join_low(left, right)
            bias_scr[r * 128 + 64 : r * 128 + 128, lanes] = join_high(left, right)
    mask = head_mask(4, 128, BF16)
    mask_f = head_mask(4, 128, F32)

    def spread(rows):
        return (rows.reshape(16, 1, 16, 128) * mask).reshape(1024, 128)

    def collect(rows):
        return jnp.sum(rows.reshape(16, 4, 16, 128) * mask_f, axis=1).reshape(256, 128)

    at = pl.ds(pl.multiple_of(chunk * 256, 256), 256)
    for row in range(4):
        q_big = spread(q_ref[row, at, :])
        a_big = spread(a_ref[row, at, :])
        keys = k_ref[row]
        values = v_ref[row]
        scores = dot(q_big, keys, NT) + bias_scr[...]
        top = jnp.max(scores, axis=-1, keepdims=True)
        powers = jnp.exp(scores - top)
        inverse = 1.0 / jnp.sum(powers, axis=-1, keepdims=True)
        powers_low = powers.astype(BF16)
        attended = dot(powers_low, values) * inverse
        att_ref[row] = collect(attended).astype(BF16)
        a_float = a_big.astype(F32)
        inner = jnp.sum(a_float * attended, axis=-1, keepdims=True)
        grad_probs = dot(a_big, values, NT)
        score_grad = powers * ((grad_probs - inner) * inverse)
        score_low = score_grad.astype(BF16)
        dq_ref[row] = (collect(dot(score_low, keys)) * scale).astype(BF16)
        dk_ref[row] += dot(q_big, score_low, TN)
        dv_ref[row] += dot((a_float * inverse).astype(BF16), powers_low, TN)
        if row == 0:
            sum_scr[...] = score_grad
        else:
            sum_scr[...] += score_grad

    @pl.when(chunk == 1)
    def _():
        dk_out[...] = (dk_ref[...] * scale).astype(BF16)
        dv_out[...] = dv_ref[...].astype(BF16)

    xs = [slot_of(chunk + 2 * high - place_ref[0]) for high in range(2)]
    ys = [slot_of(b - place_ref[1]) * 4 for b in range(4)]
    zs = [slot_of(c - place_ref[2]) * 16 for c in range(4)]

    def emit(even_ref, odd_ref):
        for r in range(8):
            out_ref = odd_ref if r % 2 else even_ref
            for m in range(4):
                lanes = slice(m * 128, m * 128 + 128)
                low = sum_scr[r * 128 : r * 128 + 64, lanes]
                high = sum_scr[r * 128 + 64 : r * 128 + 128, lanes]
                spot = zs[r // 2] + ys[m]
                out_ref[spot + xs[0], 0:64] = join_low(low, high).astype(BF16)
                out_ref[spot + xs[1], 0:64] = join_high(low, high).astype(BF16)

    @pl.when(place_ref[3] == 0)
    def _():
        emit(mine_ref, other_ref)

    @pl.when(place_ref[3] == 1)
    def _():
        emit(other_ref, mine_ref)


def post_kernel(place_ref, att_ref, dq_ref, dk_ref, dv_ref, gate_ref, gg_ref, n_ref, u_ref, rows_ref, wcat_ref,
                wout_ref, held_mine, held_other, ug_ref, mine_ref, other_ref, off_ref, w_scr, o_scr, s_scr, p_scr):
    row = pl.program_id(0)
    attended = att_ref[...].reshape(1024, 128).astype(F32)
    gate = gate_ref[...].reshape(1024, 128)
    grad_gated = gg_ref[...].reshape(1024, 128)
    gated = (gate * attended).astype(BF16)
    cot = jnp.concatenate([rows_ref[:, 0, at].reshape(512, 128) for at in range(2)], axis=0)
    update = dot(gated, wout_ref[...]).astype(BF16).reshape(2, 8, 64, 128)
    out_part = dot(gated, cot, TN)
    gpre = (grad_gated * attended * gate * (1.0 - gate)).astype(BF16)
    qpre = dq_ref[...].reshape(1024, 128)
    kpre, vpre = (
        jnp.concatenate([jnp.transpose(ref[at].astype(F32)) for at in range(2)], axis=0).astype(BF16)
        for ref in (dk_ref, dv_ref)
    )
    cat = jnp.concatenate([qpre, kpre, vpre, gpre], axis=1)
    grad_normed = dot(cat, wcat_ref[...], NT)
    grad_low = grad_normed.astype(BF16).reshape(2, 8, 64, 128)
    for at in range(2):
        ug_ref[:, 0, at] = update[at]
        ug_ref[:, 1, at] = grad_low[at]
    w_part = dot(n_ref[...].reshape(1024, 128), cat, TN)
    off = jnp.sum(gpre.astype(F32), axis=0, keepdims=True)
    gain = jnp.sum(grad_normed * u_ref[...].reshape(1024, 128).astype(F32), axis=0, keepdims=True)
    off = jnp.concatenate([off, gain], axis=0)

    @pl.when(row == 0)
    def _():
        w_scr[...] = w_part
        o_scr[...] = out_part
        s_scr[...] = off

    @pl.when(row > 0)
    def _():
        w_scr[...] += w_part
        o_scr[...] += out_part
        s_scr[...] += off

    @pl.when(row == 1)
    def _():
        for t in range(5):
            part = w_scr[:, t * 128 : t * 128 + 128] if t < 4 else o_scr[...]
            high = part.astype(BF16).astype(F32)
            p_scr[:, t, :] = high
            p_scr[:, 8 + t, :] = part - high
        for t in range(5, 8):
            p_scr[:, t, :] = jnp.zeros((128, 128), F32)
            p_scr[:, 8 + t, :] = jnp.zeros((128, 128), F32)
        x, y, z, core = seen(place_ref, 1)
        for at in range(64):
            owner = z[at // 16] + y[at // 4 % 4] + x[at % 4]
            mine_ref[at] = p_scr[owner + core[0]].astype(BF16)
            other_ref[at] = p_scr[owner + core[1]].astype(BF16)
        off_ref[...] = s_scr[...]


def tile_sums_kernel(n_ref, u_ref, one_ref, two_ref, three_ref, four_ref, off_ref, wb_ref,
                     both_ref, msg_ref, rows_ref, bg_scr):
    rows_ref[...] = (one_ref[...].astype(F32) + two_ref[...].astype(F32)) + (
        three_ref[...].astype(F32) + four_ref[...].astype(F32)
    )
    bg_scr[...] = jnp.zeros(bg_scr.shape, F32)
    for half in range(8):
        for head in range(4):
            base = head * 16 + 2 * half
            left = rows_ref[base : base + 1, :]
            right = rows_ref[base + 1 : base + 2, :]
            bg_scr[head : head + 1, half * 128 : half * 128 + 128] = join_low(left, right)
            bg_scr[head : head + 1, (8 + half) * 128 : (8 + half) * 128 + 128] = join_high(left, right)
    bg = bg_scr[...]
    high = bg.astype(BF16).astype(F32)
    both = jnp.concatenate([high, bg - high], axis=0).astype(BF16)
    both_ref[...] = both
    bias_part = dot(both, n_ref[...])
    unit_part = dot(both, u_ref[...])
    gain_part = jnp.sum(unit_part * wb_ref[...].astype(F32), axis=0, keepdims=True) + off_ref[1:2]
    params = rows_ref[64:72, :] + rows_ref[72:80, :]
    row = lax.broadcasted_iota(jnp.int32, (8, 128), 0)
    params = jnp.where(row == 5, off_ref[0:1], jnp.where(row == 6, gain_part, params))
    small = bias_part[0:8] + bias_part[8:16]
    message = jnp.concatenate([params, small], axis=0).astype(BF16)
    msg_ref[...] = jnp.broadcast_to(message[None], msg_ref.shape)


def tile_final_kernel(pair_ref, ug_ref, both_ref, gain_ref, wb_ref, up_ref, gp_ref):
    up_ref[...] = ug_ref[:, 0].reshape(2048, 128)
    unit, inverse, normed = normalize(pair_ref[...].astype(F32), gain_ref[...])
    total = ug_ref[:, 1].reshape(2048, 128).astype(F32) + dot(both_ref[...], wb_ref[...], TN)
    scaled = total * gain_ref[...]
    first = jnp.mean(scaled, axis=-1, keepdims=True)
    second = jnp.mean(scaled * unit, axis=-1, keepdims=True)
    gp_ref[...] = ((scaled - first - unit * second) * inverse).astype(BF16)


def finish_kernel(msg_ref, q_ref, k_ref, v_ref, g_ref, o_ref, off_ref, gain_ref, bias_ref, msg_scr):
    messages = msg_ref[...].astype(F32)
    msg_scr[...] = messages
    for t, ref in enumerate((q_ref, k_ref, v_ref, g_ref, o_ref)):
        ref[...] = msg_scr[:, t, :]
    small = jnp.sum(messages, axis=0)
    off_ref[...] = small[5]
    gain_ref[...] = small[6]
    bias_ref[...] = small[8:12]


def estimate(microseconds):
    return pl.CostEstimate(
        flops=microseconds * 1_000_000_000, bytes_accessed=microseconds * 3_600_000, transcendentals=0
    )


def sds(shape, dtype):
    return jax.ShapeDtypeStruct(shape, dtype)


def whole(shape):
    return pl.BlockSpec(shape, lambda *_: (0,) * len(shape))


def body(pair_rep, cotangent, ln_gain, w_query, w_key, w_value, w_gate, gate_offset, w_bias, w_out):
    scale = 32 ** (-0.5)
    gain = ln_gain.reshape(1, 128)
    offset = gate_offset.reshape(1, 128)
    wcat = jnp.concatenate([w_query, w_key, w_value, w_gate], axis=1)
    everyone = ("row", "col")
    pair_tile = pair_rep.reshape(2048, 128)

    def swap(value, axes):
        return lax.all_to_all(value, axes, split_axis=0, concat_axis=0, tiled=True)

    bias_msg, normed_tile, unit_tile, wb_two = pl.pallas_call(
        tile_bias_kernel,
        out_shape=[sds((64, 128), BF16), sds((2048, 128), BF16), sds((2048, 128), BF16), sds((16, 128), BF16)],
        scratch_shapes=[pltpu.VMEM((64, 128), F32), pltpu.VMEM((16, 128), F32)],
        compiler_params=grant(16),
        name="tile_bias",
    )(pair_tile, gain, w_bias.T)
    row, col = lax.axis_index("row"), lax.axis_index("col")
    place = ((col % 2) * 2 + row // 8, col // 2, (row // 2) % 4, row % 2)
    place = jnp.stack(place).astype(jnp.int32)
    smem = pl.BlockSpec(memory_space=pltpu.SMEM)
    packed = pl.pallas_call(
        pack_kernel,
        cost_estimate=estimate(2),
        out_shape=sds((8, 2, 4, 64, 128), BF16),
        compiler_params=grant(60),
        name="pack",
    )(pair_rep.reshape(8, 4, 64, 128), cotangent.reshape(8, 4, 64, 128))
    first = [bias_msg] + [send(bias_msg, z=hop) for hop in HOPS[1:]]
    both_rows = swap(packed, "col")
    bias_pieces = gather_in_plane(first)

    from_rows = pl.BlockSpec((8, 2, 1, 64, 128), lambda i: (0, 0, i, 0, 0))
    by_row = pl.BlockSpec((1, 512, 128), lambda i: (i, 0, 0))
    query, keys, values, grad_att, gate, grad_gated, normed, unit = pl.pallas_call(
        functools.partial(project_kernel, scale),
        grid=(4,),
        in_specs=[smem, from_rows, whole((1, 128)), whole((128, 512)), whole((1, 128)), whole((128, 128))],
        out_specs=[by_row] * 8,
        out_shape=[sds((4, 512, 128), t) for t in (BF16, BF16, BF16, BF16, F32, F32, BF16, BF16)],
        compiler_params=grant(16),
        cost_estimate=estimate(5),
        name="project",
    )(place, both_rows, gain, wcat, offset, w_out)

    bias_pieces = bias_pieces[:1] + list(after(bias_pieces[1:], query))
    bias_pieces = bias_pieces + [send(piece, core=1) for piece in bias_pieces]

    full = whole((4, 512, 128))
    half = pl.BlockSpec((4, 256, 128), lambda c: (0, c, 0))
    full_t = whole((4, 128, 512))
    attended, dq, dk, dv, mine, other = pl.pallas_call(
        functools.partial(attend_kernel, scale),
        grid=(2,),
        in_specs=[smem, full, full, full, full] + [whole((16, 64, 128))] * 8,
        out_specs=[half, half, full_t, full_t, whole((64, 80, 128)), whole((64, 80, 128))],
        out_shape=[sds((4, 512, 128), BF16), sds((4, 512, 128), BF16), sds((4, 128, 512), BF16),
                   sds((4, 128, 512), BF16), sds((64, 80, 128), BF16), sds((64, 80, 128), BF16)],
        scratch_shapes=[pltpu.VMEM((128, 64, 128), BF16), pltpu.VMEM((1024, 512), F32), pltpu.VMEM((1024, 512), F32),
                        pltpu.VMEM((4, 128, 512), F32), pltpu.VMEM((4, 128, 512), F32)],
        compiler_params=grant(26),
        name="attend",
    )(place, query, keys, values, grad_att, *bias_pieces)

    two_t = pl.BlockSpec((2, 128, 512), lambda i: (i, 0, 0))
    two = pl.BlockSpec((2, 512, 128), lambda i: (i, 0, 0))
    two_rows = pl.BlockSpec((8, 2, 2, 64, 128), lambda i: (0, 0, i, 0, 0))
    two_cot = pl.BlockSpec((8, 1, 2, 64, 128), lambda i: (0, 1, i, 0, 0))
    tail = pl.BlockSpec((64, 16, 128), lambda i: (0, 4, 0))
    ug_rows, mine, other, off = pl.pallas_call(
        post_kernel,
        grid=(2,),
        in_specs=[smem, two, two, two_t, two_t, two, two, two, two, two_cot,
                  whole((128, 512)), whole((128, 128))] + [pl.BlockSpec(memory_space=pl.ANY)] * 2,
        out_specs=[two_rows, tail, tail, whole((2, 128))],
        out_shape=[sds((8, 2, 4, 64, 128), BF16), sds((64, 80, 128), BF16), sds((64, 80, 128), BF16),
                   sds((2, 128), F32)],
        scratch_shapes=[pltpu.VMEM((128, 512), F32), pltpu.VMEM((128, 128), F32), pltpu.VMEM((2, 128), F32),
                        pltpu.VMEM((128, 16, 128), F32)],
        input_output_aliases={12: 1, 13: 2},
        compiler_params=grant(24),
        name="post",
    )(place, attended, dq, dk, dv, gate, grad_gated, normed, unit, both_rows, wcat, w_out, mine, other)
    ug_tile = swap(ug_rows, "col")
    sums = scatter_sums(mine, other)
    both, final_msg = pl.pallas_call(
        tile_sums_kernel,
        out_shape=[sds((16, 2048), BF16), sds((128, 16, 128), BF16)],
        scratch_shapes=[pltpu.VMEM((80, 128), F32), pltpu.VMEM((8, 2048), F32)],
        compiler_params=grant(10),
        name="tile_sums",
    )(normed_tile, unit_tile, *sums, off, wb_two)
    final_in = swap(final_msg, everyone)
    update, grad_pair = pl.pallas_call(
        tile_final_kernel,
        out_shape=[sds((2048, 128), BF16), sds((2048, 128), BF16)],
        compiler_params=grant(20),
        cost_estimate=estimate(5),
        name="tile_final",
    )(pair_tile, ug_tile.reshape(8, 2, 256, 128), both, gain, wb_two)
    g_query, g_key, g_value, g_gate, g_out, g_off, g_gain, g_bias = pl.pallas_call(
        finish_kernel,
        out_shape=[sds((128, 128), F32)] * 5 + [sds((128,), F32)] * 2 + [sds((4, 128), F32)],
        scratch_shapes=[pltpu.VMEM((128, 16, 128), F32)],
        compiler_params=grant(8),
        name="finish",
    )(final_in)
    return (
        update.reshape(32, 64, 128),
        grad_pair.reshape(32, 64, 128),
        g_gain,
        g_query,
        g_key,
        g_value,
        g_gate,
        g_off,
        g_bias.T,
        g_out,
    )


def solution(mesh):
    tile = P("row", "col", None)
    return jax.shard_map(
        body,
        mesh=mesh,
        in_specs=(tile, tile) + (P(),) * 8,
        out_specs=(tile, tile) + (P(),) * 8,
        check_vma=False,
    )
```

```python
import functools

import jax
import jax.numpy as jnp
from jax import lax
from jax.experimental import pallas as pl
from jax.experimental.pallas import tpu as pltpu
from jax.sharding import PartitionSpec as P

EPS = 1e-05
F32 = jnp.float32
BF16 = jnp.bfloat16
NT = (((1,), (1,)), ((), ()))
TN = (((0,), (0,)), ((), ()))
HOPS = (0, 1, 3, 2)


def grant(mebibytes):
    return pltpu.CompilerParams(vmem_limit_bytes=mebibytes * 1024 * 1024)


def dot(left, right, dims=(((1,), (0,)), ((), ()))):
    return lax.dot_general(left, right, dims, preferred_element_type=F32)


def normalize(values, gain):
    average = jnp.mean(values, axis=-1, keepdims=True)
    centered = values - average
    variance = jnp.mean(centered * centered, axis=-1, keepdims=True)
    inverse = lax.rsqrt(variance + EPS)
    unit = centered * inverse
    return unit, inverse, (unit * gain).astype(BF16)


def low_lanes(shape):
    return lax.broadcasted_iota(jnp.int32, shape, len(shape) - 1) < 64


def join_low(left, right):
    return jnp.where(low_lanes(left.shape), left, pltpu.roll(right, 64, left.ndim - 1))


def join_high(left, right):
    return jnp.where(low_lanes(left.shape), pltpu.roll(left, 64, left.ndim - 1), right)


def head_mask(heads, channels, dtype):
    lane = lax.broadcasted_iota(jnp.int32, (1, heads, 1, channels), 3)
    head = lax.broadcasted_iota(jnp.int32, (1, heads, 1, channels), 1)
    return jnp.where(lane // (channels // heads) == head, 1.0, 0.0).astype(dtype)


def flat_index(x, y, z, core):
    return (((x % 2) * 4 + z) * 2 + core) * 8 + y * 2 + x // 2


def shift_pairs(x=0, y=0, z=0, core=0):
    pairs = []
    for a in range(4):
        for b in range(4):
            for c in range(4):
                for d in range(2):
                    target = flat_index((a + x) % 4, (b + y) % 4, (c + z) % 4, (d + core) % 2)
                    pairs.append((flat_index(a, b, c, d), target))
    return sorted(pairs)


def seen(place_ref, sign):
    x, y, z = ([(place_ref[at] + 4 + sign * hop) & 3 for hop in HOPS] for at in range(3))
    core = [place_ref[3], 1 - place_ref[3]]
    return (
        [(a & 1) * 64 + (a >> 1) for a in x],
        [b * 2 for b in y],
        [c * 16 for c in z],
        [d * 8 for d in core],
    )


def slot_of(delta):
    delta = (delta + 4) & 3
    return jnp.where(delta < 2, delta, 5 - delta)


def send(value, **shift):
    return lax.ppermute(value, ("row", "col"), shift_pairs(**shift))


def gate_kernel(*refs):
    pass


def after(values, other):
    anywhere = pl.BlockSpec(memory_space=pl.ANY)
    return pl.pallas_call(
        gate_kernel,
        in_specs=[anywhere] * (len(values) + 1),
        out_specs=[anywhere] * len(values),
        out_shape=[jax.ShapeDtypeStruct(value.shape, value.dtype) for value in values],
        input_output_aliases={at: at for at in range(len(values))},
        compiler_params=grant(1),
        name="after",
    )(*values, other)


def gather_in_plane(first):
    held = jnp.stack(first)
    held = jnp.stack([held] + [send(held, y=hop) for hop in HOPS[1:]])
    held = held.reshape(16, 64, 128)
    return [held] + [send(held, x=hop) for hop in HOPS[1:]]


def add_up(parts):
    return sum(part.astype(F32) for part in parts).astype(BF16)


def scatter_sums(mine, other):
    got = send(other, core=1)
    held = [add_up([mine[at * 16 : at * 16 + 16], got[at * 16 : at * 16 + 16]]) for at in range(4)]
    got = [held[0]] + [send(held[at], z=HOPS[at]) for at in (1, 2, 3)]
    held = [add_up([part[at * 4 : at * 4 + 4] for part in got]) for at in range(4)]
    got = [held[0]] + [send(held[at], y=HOPS[at]) for at in (1, 2, 3)]
    held = [add_up([part[at] for part in got]) for at in range(4)]
    return [held[0]] + [send(held[at], x=HOPS[at]) for at in (1, 2, 3)]


def tile_bias_kernel(pair_ref, gain_ref, w_ref, msg_ref, n_ref, u_ref, wb_ref, rows_ref, w_scr):
    w_scr[...] = jnp.zeros(w_scr.shape, F32)
    w_scr[0:4, :] = w_ref[...].astype(F32)
    w_scr[8:12, :] = w_ref[...].astype(F32)
    wb_ref[...] = w_scr[...].astype(BF16)
    unit, inverse, normed = normalize(pair_ref[...].astype(F32), gain_ref[...])
    n_ref[...] = normed
    u_ref[...] = unit.astype(BF16)
    bias = dot(w_scr[...].astype(BF16), normed, NT)
    for half in range(8):
        first = bias[0:8, half * 128 : half * 128 + 128]
        second = bias[0:8, (8 + half) * 128 : (8 + half) * 128 + 128]
        even = join_low(first, second)
        odd = join_high(first, second)
        for head in range(4):
            base = head * 16 + 2 * half
            rows_ref[base : base + 1, :] = even[head : head + 1]
            rows_ref[base + 1 : base + 2, :] = odd[head : head + 1]
    msg_ref[...] = rows_ref[...].astype(BF16)


def pack_kernel(pair_ref, cot_ref, out_ref):
    out_ref[:, 0] = pair_ref[...]
    out_ref[:, 1] = cot_ref[...]


def project_kernel(scale, place_ref, rows_ref, gain_ref, wcat_ref, off_ref, wout_ref,
                   q_ref, k_ref, v_ref, a_ref, gate_ref, gg_ref, n_ref, u_ref):
    values = rows_ref[:, 0, 0].reshape(512, 128).astype(F32)
    unit, inverse, normed = normalize(values, gain_ref[...])
    projected = dot(normed, wcat_ref[...])
    gate = jax.nn.sigmoid(projected[:, 384:512] + off_ref[...])
    grad_gated = dot(rows_ref[:, 1, 0].reshape(512, 128), wout_ref[...], NT)
    q_ref[0] = (projected[:, 0:128] * scale).astype(BF16)
    k_ref[0] = (projected[:, 128:256] * scale).astype(BF16)
    v_ref[0] = projected[:, 256:384].astype(BF16)
    a_ref[0] = (grad_gated * gate).astype(BF16)
    gate_ref[0] = gate
    gg_ref[0] = grad_gated
    n_ref[0] = normed
    u_ref[0] = unit.astype(BF16)


def attend_kernel(scale, place_ref, q_ref, k_ref, v_ref, a_ref, *refs):
    pieces = refs[:8]
    att_ref, dq_ref, dk_out, dv_out, mine_ref, other_ref, block_scr, bias_scr, sum_scr, dk_ref, dv_ref = refs[8:]
    chunk = pl.program_id(0)

    @pl.when(chunk == 0)
    def _():
        x, y, z, core = seen(place_ref, -1)
        for at in range(8):
            for inner in range(16):
                owner = x[at % 4] + y[inner // 4] + z[inner % 4] + core[at // 4]
                block_scr[owner] = pieces[at][inner]
        dk_ref[...] = jnp.zeros(dk_ref.shape, F32)
        dv_ref[...] = jnp.zeros(dv_ref.shape, F32)

    for r in range(8):
        for m in range(4):
            left = block_scr[(chunk * 8 + r) * 8 + 2 * m].astype(F32)
            right = block_scr[(chunk * 8 + r) * 8 + 2 * m + 1].astype(F32)
            lanes = slice(m * 128, m * 128 + 128)
            bias_scr[r * 128 : r * 128 + 64, lanes] = join_low(left, right)
            bias_scr[r * 128 + 64 : r * 128 + 128, lanes] = join_high(left, right)
    mask = head_mask(4, 128, BF16)
    mask_f = head_mask(4, 128, F32)

    def spread(rows):
        return (rows.reshape(16, 1, 16, 128) * mask).reshape(1024, 128)

    def collect(rows):
        return jnp.sum(rows.reshape(16, 4, 16, 128) * mask_f, axis=1).reshape(256, 128)

    at = pl.ds(pl.multiple_of(chunk * 256, 256), 256)
    for row in range(4):
        q_big = spread(q_ref[row, at, :])
        a_big = spread(a_ref[row, at, :])
        keys = k_ref[row]
        values = v_ref[row]
        scores = dot(q_big, keys, NT) + bias_scr[...]
        top = jnp.max(scores, axis=-1, keepdims=True)
        powers = jnp.exp(scores - top)
        inverse = 1.0 / jnp.sum(powers, axis=-1, keepdims=True)
        powers_low = powers.astype(BF16)
        attended = dot(powers_low, values) * inverse
        att_ref[row] = collect(attended).astype(BF16)
        a_float = a_big.astype(F32)
        inner = jnp.sum(a_float * attended, axis=-1, keepdims=True)
        grad_probs = dot(a_big, values, NT)
        score_grad = powers * ((grad_probs - inner) * inverse)
        score_low = score_grad.astype(BF16)
        dq_ref[row] = (collect(dot(score_low, keys)) * scale).astype(BF16)
        dk_ref[row] += dot(q_big, score_low, TN)
        dv_ref[row] += dot((a_float * inverse).astype(BF16), powers_low, TN)
        if row == 0:
            sum_scr[...] = score_grad
        else:
            sum_scr[...] += score_grad

    @pl.when(chunk == 1)
    def _():
        dk_out[...] = (dk_ref[...] * scale).astype(BF16)
        dv_out[...] = dv_ref[...].astype(BF16)

    xs = [slot_of(chunk + 2 * high - place_ref[0]) for high in range(2)]
    ys = [slot_of(b - place_ref[1]) * 4 for b in range(4)]
    zs = [slot_of(c - place_ref[2]) * 16 for c in range(4)]

    def emit(even_ref, odd_ref):
        for r in range(8):
            out_ref = odd_ref if r % 2 else even_ref
            for m in range(4):
                lanes = slice(m * 128, m * 128 + 128)
                low = sum_scr[r * 128 : r * 128 + 64, lanes]
                high = sum_scr[r * 128 + 64 : r * 128 + 128, lanes]
                spot = zs[r // 2] + ys[m]
                out_ref[spot + xs[0], 0:64] = join_low(low, high).astype(BF16)
                out_ref[spot + xs[1], 0:64] = join_high(low, high).astype(BF16)

    @pl.when(place_ref[3] == 0)
    def _():
        emit(mine_ref, other_ref)

    @pl.when(place_ref[3] == 1)
    def _():
        emit(other_ref, mine_ref)


def post_kernel(place_ref, att_ref, dq_ref, dk_ref, dv_ref, gate_ref, gg_ref, n_ref, u_ref, rows_ref, wcat_ref,
                wout_ref, held_mine, held_other, ug_ref, mine_ref, other_ref, off_ref, w_scr, o_scr, s_scr, p_scr):
    row = pl.program_id(0)
    attended = att_ref[...].reshape(1024, 128).astype(F32)
    gate = gate_ref[...].reshape(1024, 128)
    grad_gated = gg_ref[...].reshape(1024, 128)
    gated = (gate * attended).astype(BF16)
    cot = jnp.concatenate([rows_ref[:, 0, at].reshape(512, 128) for at in range(2)], axis=0)
    update = dot(gated, wout_ref[...]).astype(BF16).reshape(2, 8, 64, 128)
    out_part = dot(gated, cot, TN)
    gpre = (grad_gated * attended * gate * (1.0 - gate)).astype(BF16)
    qpre = dq_ref[...].reshape(1024, 128)
    kpre, vpre = (
        jnp.concatenate([jnp.transpose(ref[at].astype(F32)) for at in range(2)], axis=0).astype(BF16)
        for ref in (dk_ref, dv_ref)
    )
    cat = jnp.concatenate([qpre, kpre, vpre, gpre], axis=1)
    grad_normed = dot(cat, wcat_ref[...], NT)
    grad_low = grad_normed.astype(BF16).reshape(2, 8, 64, 128)
    for at in range(2):
        ug_ref[:, 0, at] = update[at]
        ug_ref[:, 1, at] = grad_low[at]
    w_part = dot(n_ref[...].reshape(1024, 128), cat, TN)
    off = jnp.sum(gpre.astype(F32), axis=0, keepdims=True)
    gain = jnp.sum(grad_normed * u_ref[...].reshape(1024, 128).astype(F32), axis=0, keepdims=True)
    off = jnp.concatenate([off, gain], axis=0)

    @pl.when(row == 0)
    def _():
        w_scr[...] = w_part
        o_scr[...] = out_part
        s_scr[...] = off

    @pl.when(row > 0)
    def _():
        w_scr[...] += w_part
        o_scr[...] += out_part
        s_scr[...] += off

    @pl.when(row == 1)
    def _():
        for t in range(5):
            part = w_scr[:, t * 128 : t * 128 + 128] if t < 4 else o_scr[...]
            high = part.astype(BF16).astype(F32)
            p_scr[:, t, :] = high
            p_scr[:, 8 + t, :] = part - high
        for t in range(5, 8):
            p_scr[:, t, :] = jnp.zeros((128, 128), F32)
            p_scr[:, 8 + t, :] = jnp.zeros((128, 128), F32)
        x, y, z, core = seen(place_ref, 1)
        for at in range(64):
            owner = z[at // 16] + y[at // 4 % 4] + x[at % 4]
            mine_ref[at] = p_scr[owner + core[0]].astype(BF16)
            other_ref[at] = p_scr[owner + core[1]].astype(BF16)
        off_ref[...] = s_scr[...]


def tile_sums_kernel(n_ref, u_ref, one_ref, two_ref, three_ref, four_ref, off_ref, wb_ref,
                     both_ref, msg_ref, rows_ref, bg_scr):
    rows_ref[...] = (one_ref[...].astype(F32) + two_ref[...].astype(F32)) + (
        three_ref[...].astype(F32) + four_ref[...].astype(F32)
    )
    bg_scr[...] = jnp.zeros(bg_scr.shape, F32)
    for half in range(8):
        for head in range(4):
            base = head * 16 + 2 * half
            left = rows_ref[base : base + 1, :]
            right = rows_ref[base + 1 : base + 2, :]
            bg_scr[head : head + 1, half * 128 : half * 128 + 128] = join_low(left, right)
            bg_scr[head : head + 1, (8 + half) * 128 : (8 + half) * 128 + 128] = join_high(left, right)
    bg = bg_scr[...]
    high = bg.astype(BF16).astype(F32)
    both = jnp.concatenate([high, bg - high], axis=0).astype(BF16)
    both_ref[...] = both
    bias_part = dot(both, n_ref[...])
    unit_part = dot(both, u_ref[...])
    gain_part = jnp.sum(unit_part * wb_ref[...].astype(F32), axis=0, keepdims=True) + off_ref[1:2]
    params = rows_ref[64:72, :] + rows_ref[72:80, :]
    row = lax.broadcasted_iota(jnp.int32, (8, 128), 0)
    params = jnp.where(row == 5, off_ref[0:1], jnp.where(row == 6, gain_part, params))
    small = bias_part[0:8] + bias_part[8:16]
    message = jnp.concatenate([params, small], axis=0).astype(BF16)
    msg_ref[...] = jnp.broadcast_to(message[None], msg_ref.shape)


def tile_final_kernel(pair_ref, ug_ref, both_ref, gain_ref, wb_ref, up_ref, gp_ref):
    up_ref[...] = ug_ref[:, 0].reshape(2048, 128)
    unit, inverse, normed = normalize(pair_ref[...].astype(F32), gain_ref[...])
    total = ug_ref[:, 1].reshape(2048, 128).astype(F32) + dot(both_ref[...], wb_ref[...], TN)
    scaled = total * gain_ref[...]
    first = jnp.mean(scaled, axis=-1, keepdims=True)
    second = jnp.mean(scaled * unit, axis=-1, keepdims=True)
    gp_ref[...] = ((scaled - first - unit * second) * inverse).astype(BF16)


def finish_kernel(msg_ref, q_ref, k_ref, v_ref, g_ref, o_ref, off_ref, gain_ref, bias_ref, msg_scr):
    messages = msg_ref[...].astype(F32)
    msg_scr[...] = messages
    for t, ref in enumerate((q_ref, k_ref, v_ref, g_ref, o_ref)):
        ref[...] = msg_scr[:, t, :]
    small = jnp.sum(messages, axis=0)
    off_ref[...] = small[5]
    gain_ref[...] = small[6]
    bias_ref[...] = small[8:12]


def estimate(microseconds):
    return pl.CostEstimate(
        flops=microseconds * 1_000_000_000, bytes_accessed=microseconds * 3_600_000, transcendentals=0
    )


def sds(shape, dtype):
    return jax.ShapeDtypeStruct(shape, dtype)


def whole(shape):
    return pl.BlockSpec(shape, lambda *_: (0,) * len(shape))


def body(pair_rep, cotangent, ln_gain, w_query, w_key, w_value, w_gate, gate_offset, w_bias, w_out):
    scale = 32 ** (-0.5)
    gain = ln_gain.reshape(1, 128)
    offset = gate_offset.reshape(1, 128)
    wcat = jnp.concatenate([w_query, w_key, w_value, w_gate], axis=1)
    everyone = ("row", "col")
    pair_tile = pair_rep.reshape(2048, 128)

    def swap(value, axes):
        return lax.all_to_all(value, axes, split_axis=0, concat_axis=0, tiled=True)

    bias_msg, normed_tile, unit_tile, wb_two = pl.pallas_call(
        tile_bias_kernel,
        out_shape=[sds((64, 128), BF16), sds((2048, 128), BF16), sds((2048, 128), BF16), sds((16, 128), BF16)],
        scratch_shapes=[pltpu.VMEM((64, 128), F32), pltpu.VMEM((16, 128), F32)],
        compiler_params=grant(16),
        name="tile_bias",
    )(pair_tile, gain, w_bias.T)
    row, col = lax.axis_index("row"), lax.axis_index("col")
    place = ((col % 2) * 2 + row // 8, col // 2, (row // 2) % 4, row % 2)
    place = jnp.stack(place).astype(jnp.int32)
    smem = pl.BlockSpec(memory_space=pltpu.SMEM)
    packed = pl.pallas_call(
        pack_kernel,
        cost_estimate=estimate(2),
        out_shape=sds((8, 2, 4, 64, 128), BF16),
        compiler_params=grant(60),
        name="pack",
    )(pair_rep.reshape(8, 4, 64, 128), cotangent.reshape(8, 4, 64, 128))
    first = [bias_msg] + [send(bias_msg, z=hop) for hop in HOPS[1:]]
    both_rows = swap(packed, "col")
    bias_pieces = gather_in_plane(first)

    from_rows = pl.BlockSpec((8, 2, 1, 64, 128), lambda i: (0, 0, i, 0, 0))
    by_row = pl.BlockSpec((1, 512, 128), lambda i: (i, 0, 0))
    query, keys, values, grad_att, gate, grad_gated, normed, unit = pl.pallas_call(
        functools.partial(project_kernel, scale),
        grid=(4,),
        in_specs=[smem, from_rows, whole((1, 128)), whole((128, 512)), whole((1, 128)), whole((128, 128))],
        out_specs=[by_row] * 8,
        out_shape=[sds((4, 512, 128), t) for t in (BF16, BF16, BF16, BF16, F32, F32, BF16, BF16)],
        compiler_params=grant(16),
        cost_estimate=estimate(5),
        name="project",
    )(place, both_rows, gain, wcat, offset, w_out)

    bias_pieces = list(after(bias_pieces, query))
    bias_pieces = bias_pieces + [send(piece, core=1) for piece in bias_pieces]

    full = whole((4, 512, 128))
    half = pl.BlockSpec((4, 256, 128), lambda c: (0, c, 0))
    full_t = whole((4, 128, 512))
    attended, dq, dk, dv, mine, other = pl.pallas_call(
        functools.partial(attend_kernel, scale),
        grid=(2,),
        in_specs=[smem, full, full, full, full] + [whole((16, 64, 128))] * 8,
        out_specs=[half, half, full_t, full_t, whole((64, 80, 128)), whole((64, 80, 128))],
        out_shape=[sds((4, 512, 128), BF16), sds((4, 512, 128), BF16), sds((4, 128, 512), BF16),
                   sds((4, 128, 512), BF16), sds((64, 80, 128), BF16), sds((64, 80, 128), BF16)],
        scratch_shapes=[pltpu.VMEM((128, 64, 128), BF16), pltpu.VMEM((1024, 512), F32), pltpu.VMEM((1024, 512), F32),
                        pltpu.VMEM((4, 128, 512), F32), pltpu.VMEM((4, 128, 512), F32)],
        compiler_params=grant(26),
        name="attend",
    )(place, query, keys, values, grad_att, *bias_pieces)

    two_t = pl.BlockSpec((2, 128, 512), lambda i: (i, 0, 0))
    two = pl.BlockSpec((2, 512, 128), lambda i: (i, 0, 0))
    two_rows = pl.BlockSpec((8, 2, 2, 64, 128), lambda i: (0, 0, i, 0, 0))
    two_cot = pl.BlockSpec((8, 1, 2, 64, 128), lambda i: (0, 1, i, 0, 0))
    tail = pl.BlockSpec((64, 16, 128), lambda i: (0, 4, 0))
    ug_rows, mine, other, off = pl.pallas_call(
        post_kernel,
        grid=(2,),
        in_specs=[smem, two, two, two_t, two_t, two, two, two, two, two_cot,
                  whole((128, 512)), whole((128, 128))] + [pl.BlockSpec(memory_space=pl.ANY)] * 2,
        out_specs=[two_rows, tail, tail, whole((2, 128))],
        out_shape=[sds((8, 2, 4, 64, 128), BF16), sds((64, 80, 128), BF16), sds((64, 80, 128), BF16),
                   sds((2, 128), F32)],
        scratch_shapes=[pltpu.VMEM((128, 512), F32), pltpu.VMEM((128, 128), F32), pltpu.VMEM((2, 128), F32),
                        pltpu.VMEM((128, 16, 128), F32)],
        input_output_aliases={12: 1, 13: 2},
        compiler_params=grant(24),
        name="post",
    )(place, attended, dq, dk, dv, gate, grad_gated, normed, unit, both_rows, wcat, w_out, mine, other)
    ug_tile = swap(ug_rows, "col")
    sums = scatter_sums(mine, other)
    both, final_msg = pl.pallas_call(
        tile_sums_kernel,
        out_shape=[sds((16, 2048), BF16), sds((128, 16, 128), BF16)],
        scratch_shapes=[pltpu.VMEM((80, 128), F32), pltpu.VMEM((8, 2048), F32)],
        compiler_params=grant(10),
        name="tile_sums",
    )(normed_tile, unit_tile, *sums, off, wb_two)
    final_in = swap(final_msg, everyone)
    update, grad_pair = pl.pallas_call(
        tile_final_kernel,
        out_shape=[sds((2048, 128), BF16), sds((2048, 128), BF16)],
        compiler_params=grant(20),
        cost_estimate=estimate(5),
        name="tile_final",
    )(pair_tile, ug_tile.reshape(8, 2, 256, 128), both, gain, wb_two)
    g_query, g_key, g_value, g_gate, g_out, g_off, g_gain, g_bias = pl.pallas_call(
        finish_kernel,
        out_shape=[sds((128, 128), F32)] * 5 + [sds((128,), F32)] * 2 + [sds((4, 128), F32)],
        scratch_shapes=[pltpu.VMEM((128, 16, 128), F32)],
        compiler_params=grant(8),
        name="finish",
    )(final_in)
    return (
        update.reshape(32, 64, 128),
        grad_pair.reshape(32, 64, 128),
        g_gain,
        g_query,
        g_key,
        g_value,
        g_gate,
        g_off,
        g_bias.T,
        g_out,
    )


def solution(mesh):
    tile = P("row", "col", None)
    return jax.shard_map(
        body,
        mesh=mesh,
        in_specs=(tile, tile) + (P(),) * 8,
        out_specs=(tile, tile) + (P(),) * 8,
        check_vma=False,
    )
```

```python
import functools

import jax
import jax.numpy as jnp
from jax import lax
from jax.experimental import pallas as pl
from jax.experimental.pallas import tpu as pltpu
from jax.sharding import PartitionSpec as P

EPS = 1e-05
F32 = jnp.float32
BF16 = jnp.bfloat16
NT = (((1,), (1,)), ((), ()))
TN = (((0,), (0,)), ((), ()))
HOPS = (0, 1, 3, 2)


def grant(mebibytes):
    return pltpu.CompilerParams(vmem_limit_bytes=mebibytes * 1024 * 1024)


def dot(left, right, dims=(((1,), (0,)), ((), ()))):
    return lax.dot_general(left, right, dims, preferred_element_type=F32)


def normalize(values, gain):
    average = jnp.mean(values, axis=-1, keepdims=True)
    centered = values - average
    variance = jnp.mean(centered * centered, axis=-1, keepdims=True)
    inverse = lax.rsqrt(variance + EPS)
    unit = centered * inverse
    return unit, inverse, (unit * gain).astype(BF16)


def low_lanes(shape):
    return lax.broadcasted_iota(jnp.int32, shape, len(shape) - 1) < 64


def join_low(left, right):
    return jnp.where(low_lanes(left.shape), left, pltpu.roll(right, 64, left.ndim - 1))


def join_high(left, right):
    return jnp.where(low_lanes(left.shape), pltpu.roll(left, 64, left.ndim - 1), right)


def head_mask(heads, channels, dtype):
    lane = lax.broadcasted_iota(jnp.int32, (1, heads, 1, channels), 3)
    head = lax.broadcasted_iota(jnp.int32, (1, heads, 1, channels), 1)
    return jnp.where(lane // (channels // heads) == head, 1.0, 0.0).astype(dtype)


def flat_index(x, y, z, core):
    return (((x % 2) * 4 + z) * 2 + core) * 8 + y * 2 + x // 2


def shift_pairs(x=0, y=0, z=0, core=0):
    pairs = []
    for a in range(4):
        for b in range(4):
            for c in range(4):
                for d in range(2):
                    target = flat_index((a + x) % 4, (b + y) % 4, (c + z) % 4, (d + core) % 2)
                    pairs.append((flat_index(a, b, c, d), target))
    return sorted(pairs)


def seen(place_ref, sign):
    x, y, z = ([(place_ref[at] + 4 + sign * hop) & 3 for hop in HOPS] for at in range(3))
    core = [place_ref[3], 1 - place_ref[3]]
    return (
        [(a & 1) * 64 + (a >> 1) for a in x],
        [b * 2 for b in y],
        [c * 16 for c in z],
        [d * 8 for d in core],
    )


def slot_of(delta):
    delta = (delta + 4) & 3
    return jnp.where(delta < 2, delta, 5 - delta)


def send(value, **shift):
    return lax.ppermute(value, ("row", "col"), shift_pairs(**shift))


def gate_kernel(*refs):
    pass


def after(values, other):
    anywhere = pl.BlockSpec(memory_space=pl.ANY)
    return pl.pallas_call(
        gate_kernel,
        in_specs=[anywhere] * (len(values) + 1),
        out_specs=[anywhere] * len(values),
        out_shape=[jax.ShapeDtypeStruct(value.shape, value.dtype) for value in values],
        input_output_aliases={at: at for at in range(len(values))},
        compiler_params=grant(1),
        name="after",
    )(*values, other)


def gather_in_plane(first):
    held = jnp.stack(first)
    held = jnp.stack([held] + [send(held, y=hop) for hop in HOPS[1:]])
    held = held.reshape(16, 64, 128)
    return [held] + [send(held, x=hop) for hop in HOPS[1:]]


def add_up(parts):
    return sum(part.astype(F32) for part in parts).astype(BF16)


def scatter_sums(mine, other):
    got = send(other, core=1)
    held = [add_up([mine[at * 16 : at * 16 + 16], got[at * 16 : at * 16 + 16]]) for at in range(4)]
    got = [held[0]] + [send(held[at], z=HOPS[at]) for at in (1, 2, 3)]
    held = [add_up([part[at * 4 : at * 4 + 4] for part in got]) for at in range(4)]
    got = [held[0]] + [send(held[at], y=HOPS[at]) for at in (1, 2, 3)]
    held = [add_up([part[at] for part in got]) for at in range(4)]
    return [held[0]] + [send(held[at], x=HOPS[at]) for at in (1, 2, 3)]


def tile_bias_kernel(pair_ref, gain_ref, w_ref, msg_ref, wb_ref, rows_ref, w_scr):
    w_scr[...] = jnp.zeros(w_scr.shape, F32)
    w_scr[0:4, :] = w_ref[...].astype(F32)
    w_scr[8:12, :] = w_ref[...].astype(F32)
    wb_ref[...] = w_scr[...].astype(BF16)
    unit, inverse, normed = normalize(pair_ref[...].astype(F32), gain_ref[...])
    bias = dot(w_scr[...].astype(BF16), normed, NT)
    for half in range(8):
        first = bias[0:8, half * 128 : half * 128 + 128]
        second = bias[0:8, (8 + half) * 128 : (8 + half) * 128 + 128]
        even = join_low(first, second)
        odd = join_high(first, second)
        for head in range(4):
            base = head * 16 + 2 * half
            rows_ref[base : base + 1, :] = even[head : head + 1]
            rows_ref[base + 1 : base + 2, :] = odd[head : head + 1]
    msg_ref[...] = rows_ref[...].astype(BF16)


def tile_units_kernel(pair_ref, gain_ref, sums_ref, n_ref, u_ref):
    unit, inverse, normed = normalize(pair_ref[...].astype(F32), gain_ref[...])
    n_ref[...] = normed
    u_ref[...] = unit.astype(BF16)


def pack_kernel(pair_ref, cot_ref, out_ref):
    out_ref[:, 0] = pair_ref[...]
    out_ref[:, 1] = cot_ref[...]


def project_kernel(scale, place_ref, rows_ref, gain_ref, wcat_ref, off_ref, wout_ref,
                   q_ref, k_ref, v_ref, a_ref, gate_ref, gg_ref, n_ref, u_ref):
    values = rows_ref[:, 0, 0].reshape(512, 128).astype(F32)
    unit, inverse, normed = normalize(values, gain_ref[...])
    projected = dot(normed, wcat_ref[...])
    gate = jax.nn.sigmoid(projected[:, 384:512] + off_ref[...])
    grad_gated = dot(rows_ref[:, 1, 0].reshape(512, 128), wout_ref[...], NT)
    q_ref[0] = (projected[:, 0:128] * scale).astype(BF16)
    k_ref[0] = (projected[:, 128:256] * scale).astype(BF16)
    v_ref[0] = projected[:, 256:384].astype(BF16)
    a_ref[0] = (grad_gated * gate).astype(BF16)
    gate_ref[0] = gate
    gg_ref[0] = grad_gated
    n_ref[0] = normed
    u_ref[0] = unit.astype(BF16)


def attend_kernel(scale, place_ref, q_ref, k_ref, v_ref, a_ref, *refs):
    pieces = refs[:8]
    att_ref, dq_ref, dk_out, dv_out, mine_ref, other_ref, block_scr, bias_scr, sum_scr, dk_ref, dv_ref = refs[8:]
    chunk = pl.program_id(0)

    @pl.when(chunk == 0)
    def _():
        x, y, z, core = seen(place_ref, -1)
        for at in range(8):
            for inner in range(16):
                owner = x[at % 4] + y[inner // 4] + z[inner % 4] + core[at // 4]
                block_scr[owner] = pieces[at][inner]
        dk_ref[...] = jnp.zeros(dk_ref.shape, F32)
        dv_ref[...] = jnp.zeros(dv_ref.shape, F32)

    for r in range(8):
        for m in range(4):
            left = block_scr[(chunk * 8 + r) * 8 + 2 * m].astype(F32)
            right = block_scr[(chunk * 8 + r) * 8 + 2 * m + 1].astype(F32)
            lanes = slice(m * 128, m * 128 + 128)
            bias_scr[r * 128 : r * 128 + 64, lanes] = join_low(left, right)
            bias_scr[r * 128 + 64 : r * 128 + 128, lanes] = join_high(left, right)
    mask = head_mask(4, 128, BF16)
    mask_f = head_mask(4, 128, F32)

    def spread(rows):
        return (rows.reshape(16, 1, 16, 128) * mask).reshape(1024, 128)

    def collect(rows):
        return jnp.sum(rows.reshape(16, 4, 16, 128) * mask_f, axis=1).reshape(256, 128)

    at = pl.ds(pl.multiple_of(chunk * 256, 256), 256)
    for row in range(4):
        q_big = spread(q_ref[row, at, :])
        a_big = spread(a_ref[row, at, :])
        keys = k_ref[row]
        values = v_ref[row]
        scores = dot(q_big, keys, NT) + bias_scr[...]
        top = jnp.max(scores, axis=-1, keepdims=True)
        powers = jnp.exp(scores - top)
        inverse = 1.0 / jnp.sum(powers, axis=-1, keepdims=True)
        powers_low = powers.astype(BF16)
        attended = dot(powers_low, values) * inverse
        att_ref[row] = collect(attended).astype(BF16)
        a_float = a_big.astype(F32)
        inner = jnp.sum(a_float * attended, axis=-1, keepdims=True)
        grad_probs = dot(a_big, values, NT)
        score_grad = powers * ((grad_probs - inner) * inverse)
        score_low = score_grad.astype(BF16)
        dq_ref[row] = (collect(dot(score_low, keys)) * scale).astype(BF16)
        dk_ref[row] += dot(q_big, score_low, TN)
        dv_ref[row] += dot((a_float * inverse).astype(BF16), powers_low, TN)
        if row == 0:
            sum_scr[...] = score_grad
        else:
            sum_scr[...] += score_grad

    @pl.when(chunk == 1)
    def _():
        dk_out[...] = (dk_ref[...] * scale).astype(BF16)
        dv_out[...] = dv_ref[...].astype(BF16)

    xs = [slot_of(chunk + 2 * high - place_ref[0]) for high in range(2)]
    ys = [slot_of(b - place_ref[1]) * 4 for b in range(4)]
    zs = [slot_of(c - place_ref[2]) * 16 for c in range(4)]

    def emit(even_ref, odd_ref):
        for r in range(8):
            out_ref = odd_ref if r % 2 else even_ref
            for m in range(4):
                lanes = slice(m * 128, m * 128 + 128)
                low = sum_scr[r * 128 : r * 128 + 64, lanes]
                high = sum_scr[r * 128 + 64 : r * 128 + 128, lanes]
                spot = zs[r // 2] + ys[m]
                out_ref[spot + xs[0], 0:64] = join_low(low, high).astype(BF16)
                out_ref[spot + xs[1], 0:64] = join_high(low, high).astype(BF16)

    @pl.when(place_ref[3] == 0)
    def _():
        emit(mine_ref, other_ref)

    @pl.when(place_ref[3] == 1)
    def _():
        emit(other_ref, mine_ref)


def post_kernel(place_ref, att_ref, dq_ref, dk_ref, dv_ref, gate_ref, gg_ref, n_ref, u_ref, rows_ref, wcat_ref,
                wout_ref, held_mine, held_other, ug_ref, mine_ref, other_ref, off_ref, w_scr, o_scr, s_scr, p_scr):
    row = pl.program_id(0)
    attended = att_ref[...].reshape(1024, 128).astype(F32)
    gate = gate_ref[...].reshape(1024, 128)
    grad_gated = gg_ref[...].reshape(1024, 128)
    gated = (gate * attended).astype(BF16)
    cot = jnp.concatenate([rows_ref[:, 0, at].reshape(512, 128) for at in range(2)], axis=0)
    update = dot(gated, wout_ref[...]).astype(BF16).reshape(2, 8, 64, 128)
    out_part = dot(gated, cot, TN)
    gpre = (grad_gated * attended * gate * (1.0 - gate)).astype(BF16)
    qpre = dq_ref[...].reshape(1024, 128)
    kpre, vpre = (
        jnp.concatenate([jnp.transpose(ref[at].astype(F32)) for at in range(2)], axis=0).astype(BF16)
        for ref in (dk_ref, dv_ref)
    )
    cat = jnp.concatenate([qpre, kpre, vpre, gpre], axis=1)
    grad_normed = dot(cat, wcat_ref[...], NT)
    grad_low = grad_normed.astype(BF16).reshape(2, 8, 64, 128)
    for at in range(2):
        ug_ref[:, 0, at] = update[at]
        ug_ref[:, 1, at] = grad_low[at]
    w_part = dot(n_ref[...].reshape(1024, 128), cat, TN)
    off = jnp.sum(gpre.astype(F32), axis=0, keepdims=True)
    gain = jnp.sum(grad_normed * u_ref[...].reshape(1024, 128).astype(F32), axis=0, keepdims=True)
    off = jnp.concatenate([off, gain], axis=0)

    @pl.when(row == 0)
    def _():
        w_scr[...] = w_part
        o_scr[...] = out_part
        s_scr[...] = off

    @pl.when(row > 0)
    def _():
        w_scr[...] += w_part
        o_scr[...] += out_part
        s_scr[...] += off

    @pl.when(row == 1)
    def _():
        for t in range(5):
            part = w_scr[:, t * 128 : t * 128 + 128] if t < 4 else o_scr[...]
            high = part.astype(BF16).astype(F32)
            p_scr[:, t, :] = high
            p_scr[:, 8 + t, :] = part - high
        for t in range(5, 8):
            p_scr[:, t, :] = jnp.zeros((128, 128), F32)
            p_scr[:, 8 + t, :] = jnp.zeros((128, 128), F32)
        x, y, z, core = seen(place_ref, 1)
        for at in range(64):
            owner = z[at // 16] + y[at // 4 % 4] + x[at % 4]
            mine_ref[at] = p_scr[owner + core[0]].astype(BF16)
            other_ref[at] = p_scr[owner + core[1]].astype(BF16)
        off_ref[...] = s_scr[...]


def tile_sums_kernel(n_ref, u_ref, one_ref, two_ref, three_ref, four_ref, off_ref, wb_ref,
                     both_ref, msg_ref, rows_ref, bg_scr):
    rows_ref[...] = (one_ref[...].astype(F32) + two_ref[...].astype(F32)) + (
        three_ref[...].astype(F32) + four_ref[...].astype(F32)
    )
    bg_scr[...] = jnp.zeros(bg_scr.shape, F32)
    for half in range(8):
        for head in range(4):
            base = head * 16 + 2 * half
            left = rows_ref[base : base + 1, :]
            right = rows_ref[base + 1 : base + 2, :]
            bg_scr[head : head + 1, half * 128 : half * 128 + 128] = join_low(left, right)
            bg_scr[head : head + 1, (8 + half) * 128 : (8 + half) * 128 + 128] = join_high(left, right)
    bg = bg_scr[...]
    high = bg.astype(BF16).astype(F32)
    both = jnp.concatenate([high, bg - high], axis=0).astype(BF16)
    both_ref[...] = both
    bias_part = dot(both, n_ref[...])
    unit_part = dot(both, u_ref[...])
    gain_part = jnp.sum(unit_part * wb_ref[...].astype(F32), axis=0, keepdims=True) + off_ref[1:2]
    params = rows_ref[64:72, :] + rows_ref[72:80, :]
    row = lax.broadcasted_iota(jnp.int32, (8, 128), 0)
    params = jnp.where(row == 5, off_ref[0:1], jnp.where(row == 6, gain_part, params))
    small = bias_part[0:8] + bias_part[8:16]
    message = jnp.concatenate([params, small], axis=0).astype(BF16)
    msg_ref[...] = jnp.broadcast_to(message[None], msg_ref.shape)


def tile_final_kernel(pair_ref, ug_ref, both_ref, gain_ref, wb_ref, up_ref, gp_ref):
    up_ref[...] = ug_ref[:, 0].reshape(2048, 128)
    unit, inverse, normed = normalize(pair_ref[...].astype(F32), gain_ref[...])
    total = ug_ref[:, 1].reshape(2048, 128).astype(F32) + dot(both_ref[...], wb_ref[...], TN)
    scaled = total * gain_ref[...]
    first = jnp.mean(scaled, axis=-1, keepdims=True)
    second = jnp.mean(scaled * unit, axis=-1, keepdims=True)
    gp_ref[...] = ((scaled - first - unit * second) * inverse).astype(BF16)


def finish_kernel(msg_ref, q_ref, k_ref, v_ref, g_ref, o_ref, off_ref, gain_ref, bias_ref, msg_scr):
    messages = msg_ref[...].astype(F32)
    msg_scr[...] = messages
    for t, ref in enumerate((q_ref, k_ref, v_ref, g_ref, o_ref)):
        ref[...] = msg_scr[:, t, :]
    small = jnp.sum(messages, axis=0)
    off_ref[...] = small[5]
    gain_ref[...] = small[6]
    bias_ref[...] = small[8:12]


def estimate(microseconds):
    return pl.CostEstimate(
        flops=microseconds * 1_000_000_000, bytes_accessed=microseconds * 3_600_000, transcendentals=0
    )


def sds(shape, dtype):
    return jax.ShapeDtypeStruct(shape, dtype)


def whole(shape):
    return pl.BlockSpec(shape, lambda *_: (0,) * len(shape))


def body(pair_rep, cotangent, ln_gain, w_query, w_key, w_value, w_gate, gate_offset, w_bias, w_out):
    scale = 32 ** (-0.5)
    gain = ln_gain.reshape(1, 128)
    offset = gate_offset.reshape(1, 128)
    wcat = jnp.concatenate([w_query, w_key, w_value, w_gate], axis=1)
    everyone = ("row", "col")
    pair_tile = pair_rep.reshape(2048, 128)

    def swap(value, axes):
        return lax.all_to_all(value, axes, split_axis=0, concat_axis=0, tiled=True)

    bias_msg, wb_two = pl.pallas_call(
        tile_bias_kernel,
        out_shape=[sds((64, 128), BF16), sds((16, 128), BF16)],
        scratch_shapes=[pltpu.VMEM((64, 128), F32), pltpu.VMEM((16, 128), F32)],
        compiler_params=grant(16),
        name="tile_bias",
    )(pair_tile, gain, w_bias.T)
    row, col = lax.axis_index("row"), lax.axis_index("col")
    place = ((col % 2) * 2 + row // 8, col // 2, (row // 2) % 4, row % 2)
    place = jnp.stack(place).astype(jnp.int32)
    smem = pl.BlockSpec(memory_space=pltpu.SMEM)
    packed = pl.pallas_call(
        pack_kernel,
        cost_estimate=estimate(2),
        out_shape=sds((8, 2, 4, 64, 128), BF16),
        compiler_params=grant(60),
        name="pack",
    )(pair_rep.reshape(8, 4, 64, 128), cotangent.reshape(8, 4, 64, 128))
    first = [bias_msg] + [send(bias_msg, z=hop) for hop in HOPS[1:]]
    both_rows = swap(packed, "col")
    bias_pieces = gather_in_plane(first)

    from_rows = pl.BlockSpec((8, 2, 1, 64, 128), lambda i: (0, 0, i, 0, 0))
    by_row = pl.BlockSpec((1, 512, 128), lambda i: (i, 0, 0))
    query, keys, values, grad_att, gate, grad_gated, normed, unit = pl.pallas_call(
        functools.partial(project_kernel, scale),
        grid=(4,),
        in_specs=[smem, from_rows, whole((1, 128)), whole((128, 512)), whole((1, 128)), whole((128, 128))],
        out_specs=[by_row] * 8,
        out_shape=[sds((4, 512, 128), t) for t in (BF16, BF16, BF16, BF16, F32, F32, BF16, BF16)],
        compiler_params=grant(16),
        cost_estimate=estimate(5),
        name="project",
    )(place, both_rows, gain, wcat, offset, w_out)

    bias_pieces = list(after(bias_pieces, query))
    bias_pieces = bias_pieces + [send(piece, core=1) for piece in bias_pieces]

    full = whole((4, 512, 128))
    half = pl.BlockSpec((4, 256, 128), lambda c: (0, c, 0))
    full_t = whole((4, 128, 512))
    attended, dq, dk, dv, mine, other = pl.pallas_call(
        functools.partial(attend_kernel, scale),
        grid=(2,),
        in_specs=[smem, full, full, full, full] + [whole((16, 64, 128))] * 8,
        out_specs=[half, half, full_t, full_t, whole((64, 80, 128)), whole((64, 80, 128))],
        out_shape=[sds((4, 512, 128), BF16), sds((4, 512, 128), BF16), sds((4, 128, 512), BF16),
                   sds((4, 128, 512), BF16), sds((64, 80, 128), BF16), sds((64, 80, 128), BF16)],
        scratch_shapes=[pltpu.VMEM((128, 64, 128), BF16), pltpu.VMEM((1024, 512), F32), pltpu.VMEM((1024, 512), F32),
                        pltpu.VMEM((4, 128, 512), F32), pltpu.VMEM((4, 128, 512), F32)],
        compiler_params=grant(26),
        name="attend",
    )(place, query, keys, values, grad_att, *bias_pieces)

    two_t = pl.BlockSpec((2, 128, 512), lambda i: (i, 0, 0))
    two = pl.BlockSpec((2, 512, 128), lambda i: (i, 0, 0))
    two_rows = pl.BlockSpec((8, 2, 2, 64, 128), lambda i: (0, 0, i, 0, 0))
    two_cot = pl.BlockSpec((8, 1, 2, 64, 128), lambda i: (0, 1, i, 0, 0))
    tail = pl.BlockSpec((64, 16, 128), lambda i: (0, 4, 0))
    ug_rows, mine, other, off = pl.pallas_call(
        post_kernel,
        grid=(2,),
        in_specs=[smem, two, two, two_t, two_t, two, two, two, two, two_cot,
                  whole((128, 512)), whole((128, 128))] + [pl.BlockSpec(memory_space=pl.ANY)] * 2,
        out_specs=[two_rows, tail, tail, whole((2, 128))],
        out_shape=[sds((8, 2, 4, 64, 128), BF16), sds((64, 80, 128), BF16), sds((64, 80, 128), BF16),
                   sds((2, 128), F32)],
        scratch_shapes=[pltpu.VMEM((128, 512), F32), pltpu.VMEM((128, 128), F32), pltpu.VMEM((2, 128), F32),
                        pltpu.VMEM((128, 16, 128), F32)],
        input_output_aliases={12: 1, 13: 2},
        compiler_params=grant(24),
        name="post",
    )(place, attended, dq, dk, dv, gate, grad_gated, normed, unit, both_rows, wcat, w_out, mine, other)
    ug_tile = swap(ug_rows, "col")
    sums = scatter_sums(mine, other)
    normed_tile, unit_tile = pl.pallas_call(
        tile_units_kernel,
        in_specs=[whole((2048, 128)), whole((1, 128)), pl.BlockSpec(memory_space=pl.ANY)],
        out_shape=[sds((2048, 128), BF16), sds((2048, 128), BF16)],
        compiler_params=grant(12),
        cost_estimate=estimate(2),
        name="tile_units",
    )(pair_tile, gain, off)
    both, final_msg = pl.pallas_call(
        tile_sums_kernel,
        out_shape=[sds((16, 2048), BF16), sds((128, 16, 128), BF16)],
        scratch_shapes=[pltpu.VMEM((80, 128), F32), pltpu.VMEM((8, 2048), F32)],
        compiler_params=grant(10),
        name="tile_sums",
    )(normed_tile, unit_tile, *sums, off, wb_two)
    final_in = swap(final_msg, everyone)
    update, grad_pair = pl.pallas_call(
        tile_final_kernel,
        out_shape=[sds((2048, 128), BF16), sds((2048, 128), BF16)],
        compiler_params=grant(20),
        cost_estimate=estimate(5),
        name="tile_final",
    )(pair_tile, ug_tile.reshape(8, 2, 256, 128), both, gain, wb_two)
    g_query, g_key, g_value, g_gate, g_out, g_off, g_gain, g_bias = pl.pallas_call(
        finish_kernel,
        out_shape=[sds((128, 128), F32)] * 5 + [sds((128,), F32)] * 2 + [sds((4, 128), F32)],
        scratch_shapes=[pltpu.VMEM((128, 16, 128), F32)],
        compiler_params=grant(8),
        name="finish",
    )(final_in)
    return (
        update.reshape(32, 64, 128),
        grad_pair.reshape(32, 64, 128),
        g_gain,
        g_query,
        g_key,
        g_value,
        g_gate,
        g_off,
        g_bias.T,
        g_out,
    )


def solution(mesh):
    tile = P("row", "col", None)
    return jax.shard_map(
        body,
        mesh=mesh,
        in_specs=(tile, tile) + (P(),) * 8,
        out_specs=(tile, tile) + (P(),) * 8,
        check_vma=False,
    )
```
